32 devices in a mesh: dp: 4 (over y, core), rows: 2 (over x), chan: 4 (over z).
Axes of the slice: x: 2, y: 2, z: 4, core: 2. Of those that a mesh axis runs over, the one named last changes fastest.
Arguments:
- pair: bfloat16 [16, 128, 128, 128], P('dp', 'rows', 'chan'), may hold values from -6 to 6
- node: bfloat16 [16, 128, 256], P('dp', 'rows', 'chan'), may hold values from -6 to 6
- pair_cot: bfloat16 [16, 128, 128, 128], P('dp', 'rows', 'chan'), may hold values from -6 to 6
- node_cot: bfloat16 [16, 128, 256], P('dp', 'rows', 'chan'), may hold values from -6 to 6
- lengths: int32 [16], P('dp'), may hold values from 32 to 128, as said below
- present: int32 [16, 128], P('dp'), may hold values 0 or 1
- gain_pair: float32 [128], replicated, may hold values from 0.5 to 1.5
- w_tri_in: bfloat16 [2, 4, 128, 128], P(None, None, None, 'chan'), may hold values from -0.5 to 0.5
- w_out_gate: bfloat16 [2, 128, 128], P(None, None, 'chan'), may hold values from -0.5 to 0.5
- gain_tri: float32 [2, 128], replicated, may hold values from 0.5 to 1.5
- w_tri_out: bfloat16 [2, 128, 128], P(None, None, 'chan'), may hold values from -0.75 to 0.75
- gain_trans: float32 [128], replicated, may hold values from 0.5 to 1.5
- w_trans_in: bfloat16 [128, 512], P(None, 'chan'), may hold values from -0.5 to 0.5
- w_trans_out: bfloat16 [512, 128], P('chan'), may hold values from -0.5 to 0.5
- w_bias: bfloat16 [128, 8], P(None, 'chan'), may hold values from -0.5 to 0.5
- gain_node: float32 [256], replicated, may hold values from 0.5 to 1.5
- w_qkv: bfloat16 [3, 256, 256], P(None, None, 'chan'), may hold values from -0.375 to 0.375
- w_attn_out: bfloat16 [256, 256], P(None, 'chan'), may hold values from -1.5 to 1.5
- gain_node_trans: float32 [256], replicated, may hold values from 0.5 to 1.5
- w_node_in: bfloat16 [256, 1024], P(None, 'chan'), may hold values from -0.375 to 0.375
- w_node_out: bfloat16 [1024, 256], P('chan'), may hold values from -0.375 to 0.375
Outputs:
- pair_out: bfloat16 [16, 128, 128, 128], P('dp', 'rows', 'chan')
- node_out: bfloat16 [16, 128, 256], P('dp', 'rows', 'chan')
- pair_grad: bfloat16 [16, 128, 128, 128], P('dp', 'rows', 'chan')
- node_grad: bfloat16 [16, 128, 256], P('dp', 'rows', 'chan')
- grad_gain_pair: float32 [128], P('chan')
- grad_w_tri_in: float32 [2, 4, 128, 128], P(None, None, None, 'chan')
- grad_w_out_gate: float32 [2, 128, 128], P(None, None, 'chan')
- grad_gain_tri: float32 [2, 128], P(None, 'chan')
- grad_w_tri_out: float32 [2, 128, 128], P(None, None, 'chan')
- grad_gain_trans: float32 [128], P('chan')
- grad_w_trans_in: float32 [128, 512], P(None, 'chan')
- grad_w_trans_out: float32 [512, 128], P('chan')
- grad_w_bias: float32 [128, 8], P(None, 'chan')
- grad_gain_node: float32 [256], P('chan')
- grad_w_qkv: float32 [3, 256, 256], P(None, None, 'chan')
- grad_w_attn_out: float32 [256, 256], P(None, 'chan')
- grad_gain_node_trans: float32 [256], P('chan')
- grad_w_node_in: float32 [256, 1024], P(None, 'chan')
- grad_w_node_out: float32 [1024, 256], P('chan')
The draws below stay inside these ranges and needn't reach their ends.
Inputs may be any that keep to these rules, and one draw needn't show every extreme that they name: `lengths`: each group of 4 consecutive crops holds one crop of length 128.
All inputs are finite; a program needn't handle non-finite values. No bound on the sum of `present` on one device may be relied on, other than what follows from the above.
Results may differ from the reference program's by a relative error of at most 0.024.
Values may be sent and summed in bfloat16 or wider, within the bound.
No kernel may reach another device: no remote copies, remote signals or barrier semaphores. Data moves between devices by JAX's collectives and lax.ppermute only.
A program may use at most 384 MiB of HBM per device.

```python
import math
import jax
import jax.numpy as jnp
from jax import lax

PAIR = 128
TRI = 128
TRANS = 512
NODE = 256
HEADS = 8
NODE_HID = 1024
CROP = 128
CROPS = 4
ATT = 256
ALL_CROPS = 16


def draw_lengths(key, part):
    key = jax.random.fold_in(key, 11)
    first_key, second_key = jax.random.split(key)
    base = jax.random.randint(first_key, (ALL_CROPS,), CROP // 4, CROP + 1)
    groups = ALL_CROPS // CROPS
    chosen = jax.random.randint(second_key, (groups,), 0, CROPS)
    index = jnp.arange(ALL_CROPS)
    within = index % CROPS
    owner = chosen[index // CROPS]
    return jnp.where(within == owner, CROP, base).astype(jnp.int32)


def touch_ends(entries, own_key, smallest, high):
    index_at = [jax.random.randint(jax.random.fold_in(own_key, axis), (), 0, length) for axis, length in enumerate(entries.shape)]
    widest = entries.shape.index(max(entries.shape))
    neighbour = index_at[:widest] + [(index_at[widest] + 1) % entries.shape[widest]] + index_at[widest + 1:]
    return entries.at[tuple(index_at)].set(smallest).at[tuple(neighbour)].set(high)


def shard_levels(stream_key, dims, shards, low, top_value):
    level, own = 1.0, jax.random.fold_in(stream_key, 6)
    for position, blocks in shards:
        draws = jnp.exp(jax.random.uniform(jax.random.fold_in(own, position), (blocks,), jnp.float32, low / len(shards), top_value / len(shards)))
        level = level * jnp.repeat(draws, dims[position] // blocks).reshape([-1 if axis == position else 1 for axis in range(len(dims))])
    return level


def gaussian(own_key, shape, spread, limit, cuts=(), held_as=jnp.bfloat16):
    level = shard_levels(own_key, shape, cuts, -0.22, 0.18) if cuts else 1.0
    drawn = jax.random.normal(own_key, shape, jnp.float32) * spread * level
    return jnp.minimum(jnp.maximum(drawn, -limit), limit).astype(held_as)


def setup_inputs(seed: int = 0) -> dict:
    key_list = jax.random.split(jax.random.key(seed), 22)
    pair = gaussian(key_list[0], (ALL_CROPS, CROP, PAIR, CROP), 1.0, 6.0, ((0, 4), (1, 2), (2, 4)))
    node = gaussian(key_list[1], (ALL_CROPS, CROP, NODE), 1.0, 6.0, ((0, 4), (1, 2), (2, 4)))
    pair_cot = gaussian(key_list[2], (ALL_CROPS, CROP, PAIR, CROP), 1.0, 6.0, ((0, 4), (1, 2), (2, 4)))
    node_cot = gaussian(key_list[3], (ALL_CROPS, CROP, NODE), 1.0, 6.0, ((0, 4), (1, 2), (2, 4)))
    lengths = draw_lengths(jax.random.fold_in(key_list[21], 71), 0)
    present = touch_ends((jax.random.randint(key_list[5], (ALL_CROPS, CROP), 0, 8) < 7).astype(jnp.int32), jax.random.fold_in(key_list[5], 1), 0, 1)
    gain_pair = jnp.clip(1.0 + 0.1 * jax.random.normal(key_list[6], (PAIR,), jnp.float32), 0.5, 1.5)
    w_tri_in = gaussian(key_list[7], (2, 4, PAIR, TRI), PAIR ** -0.5, 0.5, ((3, 4),))
    w_out_gate = gaussian(key_list[8], (2, PAIR, PAIR), PAIR ** -0.5, 0.5, ((2, 4),))
    gain_tri = jnp.clip(1.0 + 0.1 * jax.random.normal(key_list[9], (2, TRI), jnp.float32), 0.5, 1.5)
    w_tri_out = gaussian(key_list[10], (2, TRI, PAIR), (TRI // 2) ** -0.5, 0.75, ((2, 4),))
    gain_trans = jnp.clip(1.0 + 0.1 * jax.random.normal(key_list[11], (PAIR,), jnp.float32), 0.5, 1.5)
    w_trans_in = gaussian(key_list[12], (PAIR, TRANS), PAIR ** -0.5, 0.5, ((1, 4),))
    w_trans_out = gaussian(key_list[13], (TRANS, PAIR), (TRANS // 4) ** -0.5, 0.5, ((0, 4),))
    w_bias = gaussian(key_list[14], (PAIR, HEADS), PAIR ** -0.5, 0.5, ((1, 4),))
    gain_node = jnp.clip(1.0 + 0.1 * jax.random.normal(key_list[15], (NODE,), jnp.float32), 0.5, 1.5)
    w_qkv = gaussian(key_list[16], (3, NODE, ATT), NODE ** -0.5, 0.375, ((2, 4),))
    w_attn_out = gaussian(key_list[17], (ATT, NODE), (ATT // 16) ** -0.5, 1.5, ((1, 4),))
    gain_node_trans = jnp.clip(1.0 + 0.1 * jax.random.normal(key_list[18], (NODE,), jnp.float32), 0.5, 1.5)
    w_node_in = gaussian(key_list[19], (NODE, NODE_HID), NODE ** -0.5, 0.375, ((1, 4),))
    w_node_out = gaussian(key_list[20], (NODE_HID, NODE), (NODE_HID // 4) ** -0.5, 0.375, ((0, 4),))
    return {"pair": pair, "node": node, "pair_cot": pair_cot, "node_cot": node_cot, "lengths": lengths, "present": present, "gain_pair": gain_pair, "w_tri_in": w_tri_in, "w_out_gate": w_out_gate, "gain_tri": gain_tri, "w_tri_out": w_tri_out, "gain_trans": gain_trans, "w_trans_in": w_trans_in, "w_trans_out": w_trans_out, "w_bias": w_bias, "gain_node": gain_node, "w_qkv": w_qkv, "w_attn_out": w_attn_out, "gain_node_trans": gain_node_trans, "w_node_in": w_node_in, "w_node_out": w_node_out}


@jax.custom_vjp
def low(v):
    return lax.optimization_barrier(v.astype(jnp.bfloat16)).astype(jnp.float32)

@jax.custom_vjp
def low_back(v):
    return v

def low_keep(v):
    return (low(v), None)

def low_pass(kept, grad):
    return (grad,)

def back_keep(v):
    return (v, None)

def back_low(kept, grad):
    return (low(grad),)
low.defvjp(low_keep, low_pass)
low_back.defvjp(back_keep, back_low)
epsilon = 1e-05
masked_score = -1000000000.0
highest = lax.Precision.HIGHEST

def layer_norm(value, gain):
    mean = lax.optimization_barrier(jnp.mean(value, axis=-1, keepdims=True))
    centered = value - mean
    variance = lax.optimization_barrier(jnp.mean(centered * centered, axis=-1, keepdims=True))
    return centered * lax.rsqrt(variance + epsilon) * gain

def gelu_exact(value):
    return jax.nn.gelu(value, approximate=False)

def softmax_rows(scores):
    top = lax.optimization_barrier(jnp.max(scores, axis=-1, keepdims=True))
    exps = jnp.exp(scores - top)
    return exps / lax.optimization_barrier(jnp.sum(exps, axis=-1, keepdims=True))

def crop_forward(stream_in, node_in, residue, params):
    gain_pair, w_tri_in, w_out_gate, gain_tri, w_tri_out, gain_trans, w_trans_in, w_trans_out, w_bias, gain_node, w_qkv, w_attn_out, gain_node_trans, w_node_in, w_node_out = params
    normed_in = low(layer_norm(stream_in, gain_pair))
    projected = low_back(jnp.einsum('ijc,dgch->dgijh', normed_in, w_tri_in, precision=highest))
    gate_pre = low_back(jnp.einsum('ijc,dcx->dijx', normed_in, w_out_gate, precision=highest))
    pair_mask = residue[:, None, None] * residue[None, :, None]
    left_out = low(jax.nn.sigmoid(projected[0, 0]) * projected[0, 1] * pair_mask)
    right_out = low(jax.nn.sigmoid(projected[0, 2]) * projected[0, 3] * pair_mask)
    left_in = low(jax.nn.sigmoid(projected[1, 0]) * projected[1, 1] * pair_mask)
    right_in = low(jax.nn.sigmoid(projected[1, 2]) * projected[1, 3] * pair_mask)
    tri_out = low_back(jnp.einsum('ikh,jkh->ijh', left_out, right_out, precision=highest))
    tri_in = low_back(jnp.einsum('kih,kjh->ijh', left_in, right_in, precision=highest))
    normed_out = low(layer_norm(tri_out, gain_tri[0]))
    normed_inc = low(layer_norm(tri_in, gain_tri[1]))
    branch_out = low_back(jnp.einsum('ijh,hc->ijc', normed_out, w_tri_out[0], precision=highest))
    branch_inc = low_back(jnp.einsum('ijh,hc->ijc', normed_inc, w_tri_out[1], precision=highest))
    gate_sig = jax.nn.sigmoid(gate_pre)
    stream_mid = stream_in + gate_sig[0] * branch_out + gate_sig[1] * branch_inc
    normed_mid = low(layer_norm(stream_mid, gain_trans))
    pre_hidden = low_back(jnp.einsum('ijc,cf->ijf', normed_mid, w_trans_in, precision=highest))
    hidden = low(gelu_exact(pre_hidden))
    pair_branch = low_back(jnp.einsum('ijf,fc->ijc', hidden, w_trans_out, precision=highest))
    stream_out = stream_mid + pair_branch
    heads = w_bias.shape[1]
    head_dim = w_qkv.shape[2] // heads
    normed_node = low(layer_norm(node_in, gain_node))
    qkv = low(low_back(jnp.einsum('in,gna->gia', normed_node, w_qkv, precision=highest)))
    queries = qkv[0].reshape(CROP, heads, head_dim)
    keys = qkv[1].reshape(CROP, heads, head_dim)
    values = qkv[2].reshape(CROP, heads, head_dim)
    bias = jnp.einsum('ijc,ch->hij', normed_in, w_bias, precision=highest)
    raw = jnp.einsum('ihd,jhd->hij', queries, keys, precision=highest) * (1.0 / math.sqrt(head_dim)) + bias
    scores = low_back(jnp.where(residue[None, None, :] > 0.5, raw, masked_score))
    probs_low = low(softmax_rows(scores))
    attn = low(low_back(jnp.einsum('hij,jhd->ihd', probs_low, values, precision=highest))).reshape(CROP, heads * head_dim)
    node_mid = node_in + low_back(jnp.einsum('ia,an->in', attn, w_attn_out, precision=highest))
    normed_node_mid = low(layer_norm(node_mid, gain_node_trans))
    node_pre = low_back(jnp.einsum('in,nf->if', normed_node_mid, w_node_in, precision=highest))
    node_hidden = low(gelu_exact(node_pre))
    node_branch = low_back(jnp.einsum('if,fn->in', node_hidden, w_node_out, precision=highest))
    return (stream_out, node_mid + node_branch)

def reference(pair, node, pair_cot, node_cot, lengths, present, gain_pair, w_tri_in, w_out_gate, gain_tri, w_tri_out, gain_trans, w_trans_in, w_trans_out, w_bias, gain_node, w_qkv, w_attn_out, gain_node_trans, w_node_in, w_node_out):
    params = tuple((item.astype(jnp.float32) for item in (gain_pair, w_tri_in, w_out_gate, gain_tri, w_tri_out, gain_trans, w_trans_in, w_trans_out, w_bias, gain_node, w_qkv, w_attn_out, gain_node_trans, w_node_in, w_node_out)))
    positions = jnp.arange(CROP, dtype=jnp.int32)
    residues = present.astype(jnp.float32) * (positions[None, :] < lengths[:, None]).astype(jnp.float32)

    def per_crop(totals, item):
        stream, nodes, cotangent, node_cotangent, residue = item
        stream_last = jnp.swapaxes(stream.astype(jnp.float32), 1, 2)
        cot_last = jnp.swapaxes(cotangent.astype(jnp.float32), 1, 2)

        def forward(value, node_value, weights):
            return crop_forward(value, node_value, residue, weights)
        result, pull = jax.vjp(forward, stream_last, nodes.astype(jnp.float32), params)
        grad_stream, grad_nodes, grad_params = pull((cot_last, node_cotangent.astype(jnp.float32)))
        totals = jax.tree.map(jnp.add, totals, grad_params)
        pair_result = jnp.swapaxes(result[0], 1, 2).astype(jnp.bfloat16)
        node_result = result[1].astype(jnp.bfloat16)
        pair_back = jnp.swapaxes(grad_stream, 1, 2).astype(jnp.bfloat16)
        node_back = grad_nodes.astype(jnp.bfloat16)
        return (totals, (pair_result, node_result, pair_back, node_back))
    start_totals = jax.tree.map(jnp.zeros_like, params)
    totals, outputs = lax.scan(per_crop, start_totals, (pair, node, pair_cot, node_cot, residues))
    return (outputs[0], outputs[1], outputs[2], outputs[3], totals[0], totals[1], totals[2], totals[3], totals[4], totals[5], totals[6], totals[7], totals[8], totals[9], totals[10], totals[11], totals[12], totals[13], totals[14])
```

```python
import functools
import math

import jax
import jax.numpy as jnp
from jax import lax
from jax.experimental import pallas as pl
from jax.experimental.pallas import tpu as pltpu
from jax.sharding import PartitionSpec as P

f32, bf16 = jnp.float32, jnp.bfloat16
epsilon = 1e-05
DP, ROWS, CHAN = "dp", "rows", "chan"
masked_score = -1000000000.0


def norm_parts(full):
    mean = jnp.mean(full, axis=2, keepdims=True)
    centered = full - mean
    variance = jnp.mean(centered * centered, axis=2, keepdims=True)
    inverse = lax.rsqrt(variance + epsilon)
    return (centered * inverse, inverse)


def shaped(gain, full):
    return gain.reshape(gain.shape + (1,) * (full.ndim - 3))


def normed(full, gain):
    scaled, inverse = norm_parts(full)
    return scaled * shaped(gain, full)


def stat_terms(full, gain, partial_value, groups):
    scaled, inverse = norm_parts(full)
    weighted = shaped(gain, full) * partial_value
    first_sum = jnp.sum(weighted, axis=2)
    second_sum = jnp.sum(weighted * scaled, axis=2)
    stacked = jnp.stack([first_sum, second_sum], axis=2)
    repeats = (1, 1, groups) + (1,) * (full.ndim - 3)
    return jnp.tile(stacked, repeats)


def norm_finish(full, gain, grad_here, totals, chan_index):
    width = full.shape[2]
    here = grad_here.shape[2]
    scaled, inverse = norm_parts(full)
    scaled_here = lax.dynamic_slice_in_dim(scaled, chan_index * here, here, 2)
    gain_here = lax.dynamic_slice_in_dim(gain, chan_index * here, here, 0)
    first_mean = totals[:, :, 0:1] / width
    second_mean = totals[:, :, 1:2] / width
    grad_input = inverse * (
        shaped(gain_here, full) * grad_here - first_mean - scaled_here * second_mean
    )
    summed_axes = (0, 1) + tuple(range(3, full.ndim))
    grad_gain = jnp.sum(grad_here * scaled_here, axis=summed_axes)
    return (grad_input, grad_gain)


def gelu_exact(value):
    return jax.nn.gelu(value, approximate=False)


def softmax_rows(scores):
    top = jnp.max(scores, axis=-1, keepdims=True)
    exps = jnp.exp(scores - top)
    return exps / jnp.sum(exps, axis=-1, keepdims=True)


def shards(
    pair,
    node,
    pair_cot,
    node_cot,
    lengths,
    present,
    gain_pair,
    w_tri_in,
    w_out_gate,
    gain_tri,
    w_tri_out,
    gain_trans,
    w_trans_in,
    w_trans_out,
    w_bias,
    gain_node,
    w_qkv,
    w_attn_out,
    gain_node_trans,
    w_node_in,
    w_node_out,
):
    batch = pair.shape[0]
    rows_here = pair.shape[1]
    crop_len = pair.shape[3]
    groups = lax.axis_size(CHAN)
    chan_index = lax.axis_index(CHAN)
    row_start = lax.axis_index(ROWS) * rows_here
    heads_here = w_bias.shape[1]
    head_dim = w_qkv.shape[2] // heads_here
    scale = 1.0 / math.sqrt(head_dim)
    positions = jnp.arange(crop_len, dtype=jnp.int32)
    mask_all = present.astype(jnp.float32) * (positions[None, :] < lengths[:, None]).astype(
        jnp.float32
    )
    mask_rows = lax.dynamic_slice_in_dim(mask_all, row_start, rows_here, 1)
    pair_mask = mask_rows[:, :, None, None] * mask_all[:, None, None, :]
    key_live = mask_all[:, None, None, :] > 0.5

    def gating(gate, value):
        return jax.nn.sigmoid(gate) * value * pair_mask

    pair_whole, node_whole = (
        lax.all_gather(pair, CHAN, axis=2, tiled=True),
        lax.all_gather(node, CHAN, axis=2, tiled=True),
    )
    full_in = pair_whole.astype(jnp.float32)
    node_full = node_whole.astype(jnp.float32)
    stream_in = pair.astype(jnp.float32)
    node_in = node.astype(jnp.float32)
    normed_in = normed(full_in, gain_pair).astype(jnp.bfloat16)
    projected = jnp.einsum(
        "bicj,dgch->dgbihj", normed_in, w_tri_in, preferred_element_type=jnp.float32
    )
    gate_pre = jnp.einsum(
        "bicj,dcx->dbixj", normed_in, w_out_gate, preferred_element_type=jnp.float32
    )
    bias = jnp.einsum("bicj,ch->bhij", normed_in, w_bias, preferred_element_type=jnp.float32)
    left_out = gating(projected[0, 0], projected[0, 1]).astype(jnp.bfloat16)
    right_out = gating(projected[0, 2], projected[0, 3]).astype(jnp.bfloat16)
    left_in = gating(projected[1, 0], projected[1, 1]).astype(jnp.bfloat16)
    right_in = gating(projected[1, 2], projected[1, 3]).astype(jnp.bfloat16)
    normed_node = normed(node_full, gain_node).astype(jnp.bfloat16)
    qkv = jnp.einsum(
        "bin,gna->gbia", normed_node, w_qkv, preferred_element_type=jnp.float32
    ).astype(jnp.bfloat16)
    whole_right_out, whole_right_in, whole_keys, whole_values = (
        lax.all_gather(right_out, ROWS, axis=1, tiled=True),
        lax.all_gather(right_in, ROWS, axis=1, tiled=True),
        lax.all_gather(qkv[1], ROWS, axis=1, tiled=True),
        lax.all_gather(qkv[2], ROWS, axis=1, tiled=True),
    )
    left_cols = lax.all_to_all(left_in, ROWS, split_axis=3, concat_axis=1, tiled=True)
    queries = qkv[0].reshape(batch, rows_here, heads_here, head_dim)
    keys = whole_keys.reshape(batch, crop_len, heads_here, head_dim)
    values = whole_values.reshape(batch, crop_len, heads_here, head_dim)
    raw = (
        jnp.einsum("bihd,bjhd->bhij", queries, keys, preferred_element_type=jnp.float32) * scale
        + bias
    )
    probs = softmax_rows(jnp.where(key_live, raw, masked_score))
    probs_low = probs.astype(jnp.bfloat16)
    attn = jnp.einsum(
        "bhij,bjhd->bihd", probs_low, values, preferred_element_type=jnp.float32
    ).astype(jnp.bfloat16)
    attn = attn.reshape(batch, rows_here, heads_here * head_dim)
    tri_out = jnp.einsum(
        "bihk,bjhk->bihj", left_out, whole_right_out, preferred_element_type=jnp.float32
    )
    tri_in = jnp.einsum(
        "bkhi,bkhj->bihj", left_cols, whole_right_in, preferred_element_type=jnp.float32
    )
    tri_full_out, tri_full_in, attn_whole = (
        lax.all_gather(tri_out.astype(jnp.bfloat16), CHAN, axis=2, tiled=True).astype(
            tri_out.dtype
        ),
        lax.all_gather(tri_in.astype(jnp.bfloat16), CHAN, axis=2, tiled=True).astype(
            tri_in.dtype
        ),
        lax.all_gather(
            attn.astype(jnp.float32).astype(jnp.bfloat16), CHAN, axis=2, tiled=True
        ).astype(jnp.float32),
    )
    normed_out = normed(tri_full_out, gain_tri[0]).astype(jnp.bfloat16)
    normed_inc = normed(tri_full_in, gain_tri[1]).astype(jnp.bfloat16)
    branch_out = jnp.einsum(
        "bihj,hc->bicj", normed_out, w_tri_out[0], preferred_element_type=jnp.float32
    )
    branch_inc = jnp.einsum(
        "bihj,hc->bicj", normed_inc, w_tri_out[1], preferred_element_type=jnp.float32
    )
    gate_sig = jax.nn.sigmoid(gate_pre)
    stream_mid = stream_in + gate_sig[0] * branch_out + gate_sig[1] * branch_inc
    attn_low = attn_whole.astype(jnp.bfloat16)
    node_mid = node_in + jnp.einsum(
        "bia,an->bin", attn_low, w_attn_out, preferred_element_type=jnp.float32
    )
    full_mid, node_full_mid = (
        lax.all_gather(stream_mid.astype(jnp.bfloat16), CHAN, axis=2, tiled=True).astype(
            stream_mid.dtype
        ),
        lax.all_gather(node_mid.astype(jnp.bfloat16), CHAN, axis=2, tiled=True).astype(
            node_mid.dtype
        ),
    )
    normed_mid = normed(full_mid, gain_trans).astype(jnp.bfloat16)
    pre_hidden = jnp.einsum(
        "bicj,cf->bifj", normed_mid, w_trans_in, preferred_element_type=jnp.float32
    )
    hidden, gelu_pull = jax.vjp(gelu_exact, pre_hidden)
    hidden_low = hidden.astype(jnp.bfloat16)
    out_terms = jnp.einsum(
        "bifj,fc->bicj", hidden_low, w_trans_out, preferred_element_type=jnp.float32
    )
    normed_node_mid = normed(node_full_mid, gain_node_trans).astype(jnp.bfloat16)
    node_pre = jnp.einsum(
        "bin,nf->bif", normed_node_mid, w_node_in, preferred_element_type=jnp.float32
    )
    node_hidden, node_gelu_pull = jax.vjp(gelu_exact, node_pre)
    node_hidden_low = node_hidden.astype(jnp.bfloat16)
    node_terms = jnp.einsum(
        "bif,fn->bin", node_hidden_low, w_node_out, preferred_element_type=jnp.float32
    )
    pair_sum, node_sum = (
        lax.psum_scatter(
            out_terms.astype(jnp.bfloat16), CHAN, scatter_dimension=2, tiled=True
        ).astype(jnp.float32),
        lax.psum_scatter(
            node_terms.astype(jnp.bfloat16), CHAN, scatter_dimension=2, tiled=True
        ).astype(jnp.float32),
    )
    stream_out = stream_mid + pair_sum
    node_out = node_mid + node_sum
    cot_full, node_cot_full = (
        lax.all_gather(pair_cot, CHAN, axis=2, tiled=True),
        lax.all_gather(node_cot, CHAN, axis=2, tiled=True),
    )
    grad_trans_out = jnp.einsum(
        "bifj,bicj->fc", hidden_low, cot_full, preferred_element_type=jnp.float32
    )
    grad_hidden = jnp.einsum(
        "bicj,fc->bifj", cot_full, w_trans_out, preferred_element_type=jnp.float32
    )
    grad_pre = gelu_pull(grad_hidden)[0].astype(jnp.bfloat16)
    grad_trans_in = jnp.einsum(
        "bicj,bifj->cf", normed_mid, grad_pre, preferred_element_type=jnp.float32
    )
    grad_normed_mid = jnp.einsum(
        "bifj,cf->bicj", grad_pre, w_trans_in, preferred_element_type=jnp.float32
    )
    mid_terms = stat_terms(full_mid, gain_trans, grad_normed_mid, groups)
    grad_node_out_w = jnp.einsum(
        "bif,bin->fn", node_hidden_low, node_cot_full, preferred_element_type=jnp.float32
    )
    grad_node_hidden = jnp.einsum(
        "bin,fn->bif", node_cot_full, w_node_out, preferred_element_type=jnp.float32
    )
    grad_node_pre = node_gelu_pull(grad_node_hidden)[0].astype(jnp.bfloat16)
    grad_node_in_w = jnp.einsum(
        "bin,bif->nf", normed_node_mid, grad_node_pre, preferred_element_type=jnp.float32
    )
    grad_normed_node_mid = jnp.einsum(
        "bif,nf->bin", grad_node_pre, w_node_in, preferred_element_type=jnp.float32
    )
    node_mid_terms = stat_terms(node_full_mid, gain_node_trans, grad_normed_node_mid, groups)
    mid_here, mid_totals, node_mid_here, node_mid_totals = (
        lax.psum_scatter(
            grad_normed_mid.astype(jnp.bfloat16), CHAN, scatter_dimension=2, tiled=True
        ).astype(jnp.float32),
        lax.psum_scatter(
            mid_terms.astype(jnp.bfloat16), CHAN, scatter_dimension=2, tiled=True
        ).astype(jnp.float32),
        lax.psum_scatter(
            grad_normed_node_mid.astype(jnp.bfloat16), CHAN, scatter_dimension=2, tiled=True
        ).astype(jnp.float32),
        lax.psum_scatter(
            node_mid_terms.astype(jnp.bfloat16), CHAN, scatter_dimension=2, tiled=True
        ).astype(jnp.float32),
    )
    mid_extra, grad_gain_trans = norm_finish(full_mid, gain_trans, mid_here, mid_totals, chan_index)
    node_mid_extra, grad_gain_node_trans = norm_finish(
        node_full_mid, gain_node_trans, node_mid_here, node_mid_totals, chan_index
    )
    grad_mid = pair_cot.astype(jnp.float32) + mid_extra
    grad_node_mid = node_cot.astype(jnp.float32) + node_mid_extra
    branches = jnp.stack([branch_out, branch_inc])
    grad_branch = (gate_sig * grad_mid[None]).astype(jnp.bfloat16)
    grad_gate = (grad_mid[None] * branches * gate_sig * (1.0 - gate_sig)).astype(jnp.bfloat16)
    tri_normed_both = jnp.stack([normed_out, normed_inc])
    grad_w_tri_out = jnp.einsum(
        "dbihj,dbicj->dhc", tri_normed_both, grad_branch, preferred_element_type=jnp.float32
    )
    grad_out_gate = jnp.einsum(
        "bicj,dbixj->dcx", normed_in, grad_gate, preferred_element_type=jnp.float32
    )
    grad_tri_normed = jnp.einsum(
        "dbicj,dhc->dbihj", grad_branch, w_tri_out, preferred_element_type=jnp.float32
    )
    out_stats = stat_terms(tri_full_out, gain_tri[0], grad_tri_normed[0], groups)
    inc_stats = stat_terms(tri_full_in, gain_tri[1], grad_tri_normed[1], groups)
    grad_attn_branch = grad_node_mid.astype(jnp.bfloat16)
    grad_w_attn_out = jnp.einsum(
        "bia,bin->an", attn_low, grad_attn_branch, preferred_element_type=jnp.float32
    )
    attn_terms = jnp.einsum(
        "bin,an->bia", grad_attn_branch, w_attn_out, preferred_element_type=jnp.float32
    )
    out_here, out_totals, inc_here, inc_totals, attn_here = (
        lax.psum_scatter(
            grad_tri_normed[0].astype(jnp.bfloat16), CHAN, scatter_dimension=2, tiled=True
        ).astype(jnp.float32),
        lax.psum_scatter(
            out_stats.astype(jnp.bfloat16), CHAN, scatter_dimension=2, tiled=True
        ).astype(jnp.float32),
        lax.psum_scatter(
            grad_tri_normed[1].astype(jnp.bfloat16), CHAN, scatter_dimension=2, tiled=True
        ).astype(jnp.float32),
        lax.psum_scatter(
            inc_stats.astype(jnp.bfloat16), CHAN, scatter_dimension=2, tiled=True
        ).astype(jnp.float32),
        lax.psum_scatter(
            attn_terms.astype(jnp.bfloat16), CHAN, scatter_dimension=2, tiled=True
        ).astype(jnp.float32),
    )
    grad_tri_a, gain_grad_out = norm_finish(
        tri_full_out, gain_tri[0], out_here, out_totals, chan_index
    )
    grad_tri_b, gain_grad_inc = norm_finish(
        tri_full_in, gain_tri[1], inc_here, inc_totals, chan_index
    )
    grad_gain_tri = jnp.stack([gain_grad_out, gain_grad_inc])
    grad_out_low = grad_tri_a.astype(jnp.bfloat16)
    grad_inc_low = grad_tri_b.astype(jnp.bfloat16)
    grad_attn = attn_here.astype(jnp.bfloat16).reshape(batch, rows_here, heads_here, head_dim)
    grad_probs = jnp.einsum(
        "bihd,bjhd->bhij", grad_attn, values, preferred_element_type=jnp.float32
    )
    delta = jnp.sum(probs * grad_probs, axis=3, keepdims=True)
    grad_scores = (probs * (grad_probs - delta)).astype(jnp.bfloat16)
    grad_queries = (
        jnp.einsum("bhij,bjhd->bihd", grad_scores, keys, preferred_element_type=jnp.float32) * scale
    )
    key_terms = (
        jnp.einsum("bhij,bihd->bjhd", grad_scores, queries, preferred_element_type=jnp.float32)
        * scale
    )
    value_terms = jnp.einsum(
        "bhij,bihd->bjhd", probs_low, grad_attn, preferred_element_type=jnp.float32
    )
    grad_w_bias = jnp.einsum(
        "bicj,bhij->ch", normed_in, grad_scores, preferred_element_type=jnp.float32
    )
    bias_back = jnp.einsum("bhij,ch->bicj", grad_scores, w_bias, preferred_element_type=jnp.float32)
    grad_left_out = jnp.einsum(
        "bihj,bjhk->bihk", grad_out_low, whole_right_out, preferred_element_type=jnp.float32
    )
    right_terms = jnp.einsum(
        "bihj,bihk->bjhk", grad_out_low, left_out, preferred_element_type=jnp.float32
    )
    grad_right_out, key_grads, value_grads = (
        lax.psum_scatter(
            right_terms.astype(jnp.bfloat16), ROWS, scatter_dimension=1, tiled=True
        ).astype(jnp.float32),
        lax.psum_scatter(
            key_terms.astype(jnp.bfloat16), ROWS, scatter_dimension=1, tiled=True
        ).astype(jnp.float32),
        lax.psum_scatter(
            value_terms.astype(jnp.bfloat16), ROWS, scatter_dimension=1, tiled=True
        ).astype(jnp.float32),
    )
    whole_grad_in = lax.all_gather(grad_inc_low, ROWS, axis=1, tiled=True)
    grad_left_in = jnp.einsum(
        "bihj,bkhj->bkhi", whole_grad_in, right_in, preferred_element_type=jnp.float32
    )
    grad_right_in = jnp.einsum(
        "bkhi,bihj->bkhj", left_in, whole_grad_in, preferred_element_type=jnp.float32
    )

    def gate_back(first, second, grad):
        kept_value, pull = jax.vjp(gating, first, second)
        return pull(grad)

    left_gate_out, left_value_out = gate_back(projected[0, 0], projected[0, 1], grad_left_out)
    right_gate_out, right_value_out = gate_back(projected[0, 2], projected[0, 3], grad_right_out)
    left_gate_in, left_value_in = gate_back(projected[1, 0], projected[1, 1], grad_left_in)
    right_gate_in, right_value_in = gate_back(projected[1, 2], projected[1, 3], grad_right_in)
    grad_proj = jnp.stack(
        [
            jnp.stack([left_gate_out, left_value_out, right_gate_out, right_value_out]),
            jnp.stack([left_gate_in, left_value_in, right_gate_in, right_value_in]),
        ]
    ).astype(jnp.bfloat16)
    grad_tri_in_w = jnp.einsum(
        "bicj,dgbihj->dgch", normed_in, grad_proj, preferred_element_type=jnp.float32
    )
    grad_normed_in = jnp.einsum(
        "dgbihj,dgch->bicj", grad_proj, w_tri_in, preferred_element_type=jnp.float32
    )
    grad_normed_in = grad_normed_in + jnp.einsum(
        "dbixj,dcx->bicj", grad_gate, w_out_gate, preferred_element_type=jnp.float32
    )
    grad_normed_in = grad_normed_in + bias_back
    grad_qkv = jnp.stack(
        [
            grad_queries.reshape(batch, rows_here, heads_here * head_dim),
            key_grads.reshape(batch, rows_here, heads_here * head_dim),
            value_grads.reshape(batch, rows_here, heads_here * head_dim),
        ]
    ).astype(jnp.bfloat16)
    grad_w_qkv = jnp.einsum(
        "bin,gbia->gna", normed_node, grad_qkv, preferred_element_type=jnp.float32
    )
    grad_normed_node = jnp.einsum(
        "gbia,gna->bin", grad_qkv, w_qkv, preferred_element_type=jnp.float32
    )
    in_terms = stat_terms(full_in, gain_pair, grad_normed_in, groups)
    node_in_terms = stat_terms(node_full, gain_node, grad_normed_node, groups)
    in_here, in_totals, node_in_here, node_in_totals = (
        lax.psum_scatter(
            grad_normed_in.astype(jnp.bfloat16), CHAN, scatter_dimension=2, tiled=True
        ).astype(jnp.float32),
        lax.psum_scatter(
            in_terms.astype(jnp.bfloat16), CHAN, scatter_dimension=2, tiled=True
        ).astype(jnp.float32),
        lax.psum_scatter(
            grad_normed_node.astype(jnp.bfloat16), CHAN, scatter_dimension=2, tiled=True
        ).astype(jnp.float32),
        lax.psum_scatter(
            node_in_terms.astype(jnp.bfloat16), CHAN, scatter_dimension=2, tiled=True
        ).astype(jnp.float32),
    )
    in_extra, grad_gain_pair = norm_finish(full_in, gain_pair, in_here, in_totals, chan_index)
    node_in_extra, grad_gain_node = norm_finish(
        node_full, gain_node, node_in_here, node_in_totals, chan_index
    )
    grad_stream = grad_mid + in_extra
    node_grad = grad_node_mid + node_in_extra
    summed = lax.psum(
        (
            grad_gain_pair,
            grad_tri_in_w,
            grad_out_gate,
            grad_gain_tri,
            grad_w_tri_out,
            grad_gain_trans,
            grad_trans_in,
            grad_trans_out,
            grad_w_bias,
            grad_gain_node,
            grad_w_qkv,
            grad_w_attn_out,
            grad_gain_node_trans,
            grad_node_in_w,
            grad_node_out_w,
        ),
        (DP, ROWS),
    )
    return (
        stream_out.astype(jnp.bfloat16),
        node_out.astype(jnp.bfloat16),
        grad_stream.astype(jnp.bfloat16),
        node_grad.astype(jnp.bfloat16),
        summed[0],
        summed[1],
        summed[2],
        summed[3],
        summed[4],
        summed[5],
        summed[6],
        summed[7],
        summed[8],
        summed[9],
        summed[10],
        summed[11],
        summed[12],
        summed[13],
        summed[14],
    )


def dot(a, b, ca=1, cb=0):
    return lax.dot_general(a, b, (((ca,), (cb,)), ((), ())), preferred_element_type=f32)

def sigmoid(v):
    return 0.5 * jnp.tanh(0.5 * v) + 0.5

def sub_norm(full):
    mean = jnp.mean(full, axis=0, keepdims=True)
    centered = full - mean
    inverse = lax.rsqrt(jnp.mean(centered * centered, axis=0, keepdims=True) + epsilon)
    return centered * inverse, inverse

def project_kernel(zc_ref, p0, p1, p2, p3, mask_ref, gain_ref, w_ref, wb_ref,
                   lo_ref, ro_ref, li_ref, ri_ref, norm_ref, pair_ref, bias_ref, xs, *scratch):
    pieces = (p0, p1, p2, p3)
    outs = (lo_ref, ro_ref, li_ref, ri_ref)
    rows, quarter, width = p0.shape
    chans = 4 * quarter
    z = zc_ref[0]
    gain = gain_ref[...]

    @pl.loop(0, rows // 2)
    def _(step):
        for half in range(2):
            row = 2 * step + half
            for m in range(4):
                at = pl.multiple_of(lax.bitwise_xor(z, m) * quarter, quarter)
                piece = pieces[m][row]
                pair_ref[row, pl.ds(at, quarter), :] = piece
                xs[pl.ds(at, quarter), half * width:(half + 1) * width] = piece.astype(f32)
        scaled, _ = sub_norm(xs[...])
        low = (scaled * gain).astype(bf16)
        for half in range(2):
            norm_ref[2 * step + half] = low[:, half * width:(half + 1) * width]
        mask = jnp.concatenate([mask_ref[pl.ds(2 * step + half, 1), :] for half in range(2)], axis=1)
        b = dot(wb_ref[...], low)
        for half in range(2):
            bias_ref[2 * step + half] = b[:, half * width:(half + 1) * width]
        for block in range(4):
            proj = dot(w_ref[block], low)
            for k in range(4):
                gate = proj[(2 * k) * quarter:(2 * k + 1) * quarter]
                value = proj[(2 * k + 1) * quarter:(2 * k + 2) * quarter]
                kept = sigmoid(gate) * value * mask
                for half in range(2):
                    at = pl.multiple_of((2 * step + half) * chans + block * quarter, quarter)
                    scratch[k][pl.ds(at, quarter), :] = kept[:, half * width:(half + 1) * width]

    @pl.loop(0, chans, unroll=8)
    def _(h):
        for k in range(4):
            outs[k][h] = scratch[k][pl.ds(h, rows, stride=chans), :].astype(bf16)

def project(zc, pieces, mask_rows, gain, w, wb, step_rows=16):
    rows, quarter, width = pieces[0].shape
    chans = 4 * quarter
    heads = wb.shape[0]
    grid = (rows // step_rows,)
    tri = jax.ShapeDtypeStruct((chans, rows, width), bf16)
    tri_spec = pl.BlockSpec((chans, step_rows, width), lambda i: (0, i, 0))
    row_spec = pl.BlockSpec((step_rows, chans, width), lambda i: (i, 0, 0))
    pair = jax.ShapeDtypeStruct((rows, chans, width), bf16)
    return pl.pallas_call(
        project_kernel,
        grid=grid,
        in_specs=[pl.BlockSpec(memory_space=pltpu.SMEM)]
        + [pl.BlockSpec((step_rows, quarter, width), lambda i: (i, 0, 0))] * 4
        + [pl.BlockSpec((step_rows, width), lambda i: (i, 0)),
           pl.BlockSpec(gain.shape, lambda i: (0, 0)),
           pl.BlockSpec(w.shape, lambda i: (0, 0, 0)),
           pl.BlockSpec(wb.shape, lambda i: (0, 0))],
        out_specs=[tri_spec] * 4 + [row_spec, row_spec,
                                    pl.BlockSpec((step_rows, heads, width), lambda i: (i, 0, 0))],
        out_shape=[tri] * 4 + [pair, pair, jax.ShapeDtypeStruct((rows, heads, width), f32)],
        scratch_shapes=[pltpu.VMEM((chans, 2 * width), f32)]
        + [pltpu.VMEM((step_rows * chans, width), f32)] * 4,
        compiler_params=pltpu.CompilerParams(vmem_limit_bytes=48 * 2**20),
        cost_estimate=pl.CostEstimate(flops=2 * rows * width * chans * 8 * chans, bytes_accessed=20 * 2**20, transcendentals=rows * width * chans * 4),
        name="project",
    )(zc, *pieces, mask_rows, gain, w, wb)

def gelu_both(value):
    cdf = 0.5 * (1.0 + lax.erf(value * (0.5 ** 0.5)))
    density = jnp.exp(-0.5 * value * value) * (1.0 / math.sqrt(2.0 * math.pi))
    return value * cdf, cdf + value * density

def norm_back(gain, scaled, inverse, grad):
    weighted = gain * grad
    first = jnp.mean(weighted, axis=0, keepdims=True)
    second = jnp.mean(weighted * scaled, axis=0, keepdims=True)
    return inverse * (weighted - first - scaled * second)

def middle_kernel(h_steps, place_ref, lo, ro, ro_far, li, li_far, ri, ri_far,
                  pair_ref, norm_ref, c0, c1, c2, c3,
                  gain_tri_ref, gain_trans_ref, wg_ref, wto_ref, wti_ref, wout_ref,
                  p0, p1, p2, p3, mid_ref, gate_ref, go_ref, gi_ref,
                  gw_in_ref, gw_out_ref, gw_tri_ref, gg_trans_ref, gg_tri_ref,
                  tri0, tri1, wout_t, wti_t, wto_t, right_s, xs, cot_s, po_s, tn0, tn1, nm, hid, gp, gb0, gb1, gs0, gs1):
    z, core = place_ref[0], place_ref[1]
    step = pl.program_id(0)
    half_rows = lo.shape[1]
    width = lo.shape[2]
    chans = wg_ref.shape[1]
    tris = (tri0, tri1)

    @pl.when(step == 0)
    def _():
        for f in range(4):
            wout_t[:, f * 128:(f + 1) * 128] = wout_ref[f * 128:(f + 1) * 128].astype(f32).T.astype(bf16)
            wti_t[:, f * 128:(f + 1) * 128] = wti_ref[f * 128:(f + 1) * 128].astype(f32).T.astype(bf16)
        for d in range(2):
            wto_t[d] = wto_ref[d].astype(f32).T.astype(bf16)
        for ref in (gw_in_ref, gw_out_ref, gw_tri_ref, gg_trans_ref, gg_tri_ref):
            ref[...] = jnp.zeros_like(ref)

    @pl.when(step < h_steps)
    def _():
        here = lo.shape[0]
        first = core == 0

        @pl.loop(0, here, unroll=4)
        def _(h):
            at = pl.multiple_of((step * here + h) * half_rows, half_rows)
            mine, far = ro[h], ro_far[h]
            right = jnp.concatenate([jnp.where(first, mine, far), jnp.where(first, far, mine)], axis=0)
            tri0[pl.ds(at, half_rows), :] = dot(lo[h], right, 1, 1)
            left = jnp.concatenate([li[h], li_far[h]], axis=0)
            right = jnp.concatenate([ri[h], ri_far[h]], axis=0)
            both = dot(left, right, 0, 0)
            tri1[pl.ds(at, half_rows), :] = jnp.where(first, both[:half_rows], both[half_rows:])

    @pl.when(step >= h_steps)
    def _():
        rows = pair_ref.shape[0]
        quarter = chans // 4
        first_row = (step - h_steps) * rows
        cots, outs = (c0, c1, c2, c3), (p0, p1, p2, p3)
        tns, gbs, gss, grads = (tn0, tn1), (gb0, gb1), (gs0, gs1), (go_ref, gi_ref)
        gain_trans = gain_trans_ref[...]

        @pl.loop(0, rows // 2)
        def _(s2):
            lanes = pl.ds(pl.multiple_of(s2 * 2 * width, 2 * width), 2 * width)

            def wide(get):
                return jnp.concatenate([get(2 * s2), get(2 * s2 + 1)], axis=1)

            inner = wide(lambda r: norm_ref[r])
            gate = sigmoid(dot(wg_ref[...].reshape(2 * chans, chans), inner))
            total = wide(lambda r: pair_ref[r]).astype(f32)
            kept = []
            for d in range(2):
                tri = wide(lambda r: tris[d][pl.ds(first_row + r, chans, stride=half_rows), :])
                scaled, inverse = sub_norm(tri)
                low = (scaled * gain_tri_ref[d]).astype(bf16)
                tns[d][:, lanes] = low
                branch = dot(wto_ref[d], low)
                total = total + gate[d * chans:(d + 1) * chans] * branch
                kept.append((scaled, inverse, branch))
            scaled, inverse = sub_norm(total)
            low = (scaled * gain_trans).astype(bf16)
            nm[:, lanes] = low
            for half in range(2):
                for m in range(4):
                    at = pl.multiple_of(lax.bitwise_xor(z, m) * quarter, quarter)
                    cot_s[pl.ds(at, quarter), pl.ds(pl.multiple_of((2 * s2 + half) * width, width), width)] = cots[m][2 * s2 + half]
            cot = cot_s[:, lanes]
            for f in range(4):
                block = slice(f * 128, (f + 1) * 128)
                act, slope = gelu_both(dot(wti_ref[block], low))
                hid[block, lanes] = act.astype(bf16)
                gp[block, lanes] = (dot(wout_ref[block], cot) * slope).astype(bf16)
            po_s[...] = (total + dot(wout_t[...], hid[:, lanes])).astype(bf16)
            for half in range(2):
                for m in range(4):
                    at = pl.multiple_of(lax.bitwise_xor(z, m) * quarter, quarter)
                    outs[m][2 * s2 + half] = po_s[pl.ds(at, quarter), half * width:(half + 1) * width]
            back = dot(wti_t[...], gp[:, lanes])
            gg_trans_ref[...] += back * scaled
            grad = cot.astype(f32) + norm_back(gain_trans, scaled, inverse, back)
            for half in range(2):
                mid_ref[2 * s2 + half] = grad[:, half * width:(half + 1) * width]
            for d in range(2):
                scaled, inverse, branch = kept[d]
                sig = gate[d * chans:(d + 1) * chans]
                grad_branch = sig * grad
                grad_gate = (grad_branch * branch * (1.0 - sig)).astype(bf16)
                grad_branch = grad_branch.astype(bf16)
                for half in range(2):
                    gate_ref[2 * s2 + half, d * chans:(d + 1) * chans] = grad_gate[:, half * width:(half + 1) * width]
                gbs[d][:, lanes] = grad_branch
                back = dot(wto_t[d], grad_branch)
                gg_tri_ref[d] += back * scaled
                out = norm_back(gain_tri_ref[d], scaled, inverse, back)
                for half in range(2):
                    gss[d][pl.ds(2 * s2 + half, chans, stride=rows), :] = out[:, half * width:(half + 1) * width]

        gw_out_ref[...] += dot(hid[...], cot_s[...], 1, 1)
        gw_in_ref[...] += dot(gp[...], nm[...], 1, 1)
        for d in range(2):
            gw_tri_ref[d] += dot(gbs[d][...], tns[d][...], 1, 1)

            @pl.loop(0, chans, unroll=8)
            def _(h):
                grads[d][h] = gss[d][pl.ds(pl.multiple_of(h * rows, rows), rows), :].astype(bf16)

def middle(place, tri_in, pair, norm, cots, gain_tri, gain_trans, wg, wto, wti, wout, step_rows=16, step_h=16):
    chans, rows, width = tri_in[0].shape
    hidden = wti.shape[0]
    quarter = chans // 4
    h_steps, i_steps = chans // step_h, rows // step_rows
    h_spec = pl.BlockSpec((step_h, rows, width), lambda s: (jnp.minimum(s, h_steps - 1), 0, 0))

    def at(s):
        return jnp.maximum(s - h_steps, 0)

    def whole(a):
        zeros = (0,) * len(a.shape)
        return pl.BlockSpec(a.shape, lambda s: zeros)

    row_spec = pl.BlockSpec((step_rows, chans, width), lambda s: (at(s), 0, 0))
    piece_spec = pl.BlockSpec((step_rows, quarter, width), lambda s: (at(s), 0, 0))
    tri_spec = pl.BlockSpec((chans, step_rows, width), lambda s: (0, at(s), 0))
    piece = jax.ShapeDtypeStruct((rows, quarter, width), bf16)
    tri = jax.ShapeDtypeStruct((chans, rows, width), bf16)
    sums = [jax.ShapeDtypeStruct(s, f32) for s in ((hidden, chans), (hidden, chans), (2, chans, chans), (chans, 2 * width), (2, chans, 2 * width))]
    lanes = step_rows * width
    return pl.pallas_call(
        functools.partial(middle_kernel, h_steps),
        grid=(h_steps + i_steps,),
        in_specs=[pl.BlockSpec(memory_space=pltpu.SMEM)] + [h_spec] * 7 + [row_spec, row_spec] + [piece_spec] * 4
        + [whole(a) for a in (gain_tri, gain_trans, wg, wto, wti, wout)],
        out_specs=[piece_spec] * 4 + [row_spec, pl.BlockSpec((step_rows, 2 * chans, width), lambda s: (at(s), 0, 0)), tri_spec, tri_spec]
        + [whole(a) for a in sums],
        out_shape=[piece] * 4 + [jax.ShapeDtypeStruct((rows, chans, width), f32), jax.ShapeDtypeStruct((rows, 2 * chans, width), bf16), tri, tri] + sums,
        scratch_shapes=[pltpu.VMEM((chans * rows, width), f32)] * 2
        + [pltpu.VMEM((chans, hidden), bf16)] * 2 + [pltpu.VMEM((2, chans, chans), bf16), pltpu.VMEM((width, width), bf16),
           pltpu.VMEM((chans, 2 * width), f32), pltpu.VMEM((chans, lanes), bf16), pltpu.VMEM((chans, 2 * width), bf16)]
        + [pltpu.VMEM((chans, lanes), bf16)] * 3 + [pltpu.VMEM((hidden, lanes), bf16)] * 2 + [pltpu.VMEM((chans, lanes), bf16)] * 2
        + [pltpu.VMEM((chans * step_rows, width), f32)] * 2,
        compiler_params=pltpu.CompilerParams(vmem_limit_bytes=60 * 2**20),
        cost_estimate=pl.CostEstimate(flops=11 * 10**9, bytes_accessed=40 * 2**20, transcendentals=rows * width * hidden * 2),
        name="middle",
    )(place, *tri_in, pair, norm, *cots, gain_tri, gain_trans, wg, wto, wti, wout)

def finish_kernel(h_steps, place_ref, lo, lo_far, ro, ro_far, li, ri, go, go_far, gi, gi_far,
                  pair_ref, norm_ref, mid_ref, gate_ref, score_ref, mask_ref, gain_ref, w_ref, wall_ref,
                  p0, p1, p2, p3, gw_ref, gg_ref,
                  s0, s1, s2_, s3, wall_t, gall, nb, po_s):
    z, core = place_ref[0], place_ref[1]
    step = pl.program_id(0)
    half_rows, width = lo.shape[1:]
    chans = norm_ref.shape[1]
    sums = (s0, s1, s2_, s3)
    packed = wall_ref.shape[0]

    @pl.when(step == 0)
    def _():
        for f in range(packed // 128):
            wall_t[:, f * 128:(f + 1) * 128] = wall_ref[f * 128:(f + 1) * 128].astype(f32).T.astype(bf16)
        for ref in (gw_ref, gg_ref):
            ref[...] = jnp.zeros_like(ref)

    @pl.when(step < h_steps)
    def _():
        here = lo.shape[0]
        first = core == 0

        def ordered(mine, far):
            return jnp.concatenate([jnp.where(first, mine, far), jnp.where(first, far, mine)], axis=0)

        @pl.loop(0, here, unroll=4)
        def _(h):
            at = pl.ds(pl.multiple_of((step * here + h) * half_rows, half_rows), half_rows)
            s0[at, :] = dot(go[h], ordered(ro[h], ro_far[h]))
            both = dot(jnp.concatenate([go[h], go_far[h]], axis=0), jnp.concatenate([lo[h], lo_far[h]], axis=0), 0, 0)
            s1[at, :] = jnp.where(first, both[:half_rows], both[half_rows:])
            inc = ordered(gi[h], gi_far[h])
            s2_[at, :] = dot(ri[h], inc, 1, 1)
            s3[at, :] = dot(li[h], inc)

    @pl.when(step >= h_steps)
    def _():
        rows = pair_ref.shape[0]
        quarter = chans // 4
        first_row = (step - h_steps) * rows
        outs = (p0, p1, p2, p3)
        gain = gain_ref[...]
        heads = score_ref.shape[1]
        gall[packed - 128:, :] = jnp.zeros((128, gall.shape[1]), bf16)

        @pl.loop(0, rows // 2)
        def _(s2):
            lanes = pl.ds(pl.multiple_of(s2 * 2 * width, 2 * width), 2 * width)

            def wide(get):
                return jnp.concatenate([get(2 * s2), get(2 * s2 + 1)], axis=1)

            inner = wide(lambda r: norm_ref[r])
            nb[:, lanes] = inner
            mask = wide(lambda r: mask_ref[pl.ds(r, 1), :])
            for block in range(4):
                proj = dot(w_ref[block], inner)
                for k in range(4):
                    gate = proj[(2 * k) * quarter:(2 * k + 1) * quarter]
                    value = proj[(2 * k + 1) * quarter:(2 * k + 2) * quarter]
                    grad = wide(lambda r: sums[k][pl.ds(block * quarter * half_rows + first_row + r, quarter, stride=half_rows), :])
                    sig = sigmoid(gate)
                    back = grad * mask * sig
                    base = block * 8 * quarter + 2 * k * quarter
                    gall[base:base + quarter, lanes] = (back * value * (1.0 - sig)).astype(bf16)
                    gall[base + quarter:base + 2 * quarter, lanes] = back.astype(bf16)
            gall[8 * chans:10 * chans, lanes] = wide(lambda r: gate_ref[r])
            gall[10 * chans:10 * chans + 2 * heads, lanes] = jnp.concatenate([wide(lambda r: score_ref[r]), jnp.zeros((heads, 2 * width), f32)], axis=0).astype(bf16)
            back = dot(wall_t[...], gall[:, lanes])
            scaled, inverse = sub_norm(wide(lambda r: pair_ref[r]).astype(f32))
            gg_ref[...] += back * scaled
            out = wide(lambda r: mid_ref[r]) + norm_back(gain, scaled, inverse, back)
            po_s[...] = out.astype(bf16)
            for half in range(2):
                for m in range(4):
                    at = pl.multiple_of(lax.bitwise_xor(z, m) * quarter, quarter)
                    outs[m][2 * s2 + half] = po_s[pl.ds(at, quarter), half * width:(half + 1) * width]

        gw_ref[...] += dot(gall[...], nb[...], 1, 1)

def finish(place, tri_in, pair, norm, mid, gate, scores, mask_rows, gain, w, wall, step_rows=16, step_h=16):
    chans, rows, width = tri_in[0].shape
    quarter = chans // 4
    heads = scores.shape[1]
    packed = wall.shape[0]
    h_steps, i_steps = chans // step_h, rows // step_rows
    h_spec = pl.BlockSpec((step_h, rows, width), lambda s: (jnp.minimum(s, h_steps - 1), 0, 0))

    def at(s):
        return jnp.maximum(s - h_steps, 0)

    def whole(a):
        zeros = (0,) * len(a.shape)
        return pl.BlockSpec(a.shape, lambda s: zeros)

    row_spec = pl.BlockSpec((step_rows, chans, width), lambda s: (at(s), 0, 0))
    piece_spec = pl.BlockSpec((step_rows, quarter, width), lambda s: (at(s), 0, 0))
    piece = jax.ShapeDtypeStruct((rows, quarter, width), bf16)
    sums = [jax.ShapeDtypeStruct(s, f32) for s in ((packed, chans), (chans, 2 * width))]
    lanes = step_rows * width
    return pl.pallas_call(
        functools.partial(finish_kernel, h_steps),
        grid=(h_steps + i_steps,),
        in_specs=[pl.BlockSpec(memory_space=pltpu.SMEM)] + [h_spec] * 10 + [row_spec] * 3
        + [pl.BlockSpec((step_rows, 2 * chans, width), lambda s: (at(s), 0, 0)),
           pl.BlockSpec((step_rows, heads, width), lambda s: (at(s), 0, 0)),
           pl.BlockSpec((step_rows, width), lambda s: (at(s), 0))]
        + [whole(a) for a in (gain, w, wall)],
        out_specs=[piece_spec] * 4 + [whole(a) for a in sums],
        out_shape=[piece] * 4 + sums,
        scratch_shapes=[pltpu.VMEM((chans * rows, width), f32)] * 4
        + [pltpu.VMEM((chans, packed), bf16), pltpu.VMEM((packed, lanes), bf16), pltpu.VMEM((chans, lanes), bf16), pltpu.VMEM((chans, 2 * width), bf16)],
        compiler_params=pltpu.CompilerParams(vmem_limit_bytes=60 * 2**20),
        cost_estimate=pl.CostEstimate(flops=8 * 10**9, bytes_accessed=40 * 2**20, transcendentals=rows * width * chans * 4),
        name="finish",
    )(place, *tri_in, pair, norm, mid, gate, scores, mask_rows, gain, w, wall)


def shards_by_crop(
    pair,
    node,
    pair_cot,
    node_cot,
    lengths,
    present,
    gain_pair,
    w_tri_in,
    w_out_gate,
    gain_tri,
    w_tri_out,
    gain_trans,
    w_trans_in,
    w_trans_out,
    w_bias,
    gain_node,
    w_qkv,
    w_attn_out,
    gain_node_trans,
    w_node_in,
    w_node_out,
):
    groups = lax.axis_size(CHAN)
    rows_here = pair.shape[1]
    chans = groups * pair.shape[2]
    crop_len = pair.shape[3]
    nodes = groups * node.shape[2]
    z = lax.axis_index(CHAN)
    core = lax.axis_index(DP) % 2
    x = lax.axis_index(ROWS)
    place = jnp.stack([z, core]).astype(jnp.int32)
    mesh_shape = (lax.axis_size(DP), lax.axis_size(ROWS), groups)

    def device(d, r, c):
        return (d * mesh_shape[1] + r) * groups + c

    def home_perm(m):
        return [
            (device(d, r, c), device(d - d % 2 + r, d % 2, c ^ m))
            for d in range(mesh_shape[0])
            for r in range(mesh_shape[1])
            for c in range(groups)
        ]

    core_pairs = [(d, d ^ 1) for d in range(mesh_shape[0])]
    row_pairs = [(0, 1), (1, 0)]

    def send_home(pieces):
        return [
            lax.ppermute(piece, (DP, ROWS, CHAN), home_perm(m))
            for m, piece in enumerate(pieces)
        ]

    def crops_home(value):
        return send_home(
            [lax.dynamic_index_in_dim(value, z ^ m, 0, keepdims=False) for m in range(groups)]
        )

    def swap_core(value):
        return lax.ppermute(value, DP, core_pairs)

    def in_order(pieces, axis):
        stacked = jnp.stack(pieces)
        return jnp.concatenate(
            [lax.dynamic_index_in_dim(stacked, z ^ m, 0, keepdims=False) for m in range(groups)],
            axis=axis,
        )

    def own_and_far(value, axis):
        far = swap_core(value)
        return jnp.concatenate(
            [jnp.where(core == 0, value, far), jnp.where(core == 0, far, value)], axis=axis
        )

    def own_rows(value, axis):
        return lax.dynamic_slice_in_dim(value, core * rows_here, rows_here, axis)

    def gather(parts):
        packed = jnp.concatenate([part.reshape(-1, chans) for part in parts])
        whole = lax.all_gather(packed, CHAN, axis=0)
        cuts, at = [], 0
        for part in parts:
            size = part.size // chans
            cuts.append(whole[:, at : at + size])
            at += size
        return cuts

    w8, wg, wb = gather(
        [w_tri_in.transpose(0, 1, 3, 2), w_out_gate.transpose(0, 2, 1), w_bias.T]
    )
    wg = wg.reshape(groups, 2, -1, chans).transpose(1, 0, 2, 3).reshape(2, chans, chans)
    heads = groups * w_bias.shape[1]
    wb = wb.reshape(heads, chans)
    pieces = crops_home(pair)
    positions = jnp.arange(crop_len, dtype=jnp.int32)
    live = present.astype(jnp.float32) * (positions[None, :] < lengths[:, None]).astype(jnp.float32)
    live = lax.dynamic_index_in_dim(live, z, 0, keepdims=False)
    live = jnp.where(x == core, live, swap_core(live))
    live_rows = own_rows(live, 0)
    mask_rows = live_rows[:, None] * live[None, :]
    node_pieces = crops_home(node)

    lo, ro, li, ri, norm_in, pair_home, bias = project(
        place, pieces, mask_rows, gain_pair.reshape(-1, 1), w8, wb
    )
    ro_far, ri_far, li_far, lo_far = swap_core(ro), swap_core(ri), swap_core(li), swap_core(lo)

    wto, wti, wout, wq, wa, wni, wno = gather(
        [
            w_tri_out.transpose(0, 2, 1),
            w_trans_in.T,
            w_trans_out,
            w_qkv.transpose(0, 2, 1),
            w_attn_out.T,
            w_node_in.T,
            w_node_out,
        ]
    )
    wto = wto.reshape(groups, 2, -1, chans).transpose(1, 0, 2, 3).reshape(2, chans, chans)
    wti, wout = wti.reshape(-1, chans), wout.reshape(-1, chans)
    cot_pieces = crops_home(pair_cot)
    node_cot_pieces = crops_home(node_cot)

    out0, out1, out2, out3, grad_mid, grad_gate, go, gi, gw_in, gw_out, gw_tri, gg_trans, gg_tri = middle(
        place,
        (lo, ro, ro_far, li, li_far, ri, ri_far),
        pair_home,
        norm_in,
        cot_pieces,
        gain_tri.reshape(2, -1, 1),
        gain_trans.reshape(-1, 1),
        wg,
        wto,
        wti,
        wout,
    )
    go_far, gi_far = swap_core(go), swap_core(gi)
    out_back = send_home([out0, out1, out2, out3])

    wq = wq.reshape(groups, 3, -1, nodes).transpose(1, 0, 2, 3).reshape(3, -1, nodes)
    wa, wni, wno = wa.reshape(nodes, -1), wni.reshape(-1, nodes), wno.reshape(-1, nodes)
    node_in = own_and_far(in_order(node_pieces, 1), 0).astype(jnp.float32)
    cot = own_and_far(in_order(node_cot_pieces, 1), 0)
    bias = own_and_far(bias, 0).transpose(1, 0, 2)
    node_outs = node_track(node_in, cot, bias, live, wq, wa, wni, wno, gain_node, gain_node_trans)
    node_out, node_grad, scores, gw_node, gg_node = node_outs
    scores = own_rows(scores, 1).transpose(1, 0, 2).astype(jnp.float32)

    def node_back(value):
        value = own_rows(value.astype(jnp.bfloat16), 0)
        width = nodes // groups
        return send_home(
            [lax.dynamic_slice_in_dim(value, (z ^ m) * width, width, 1) for m in range(groups)]
        )

    node_out_back, node_grad_back = node_back(node_out), node_back(node_grad)

    wall = jnp.concatenate([w8.reshape(-1, chans), wg.reshape(-1, chans), wb])
    wall = jnp.pad(wall, ((0, -wall.shape[0] % 128), (0, 0)))
    g0, g1, g2, g3, gw, gg_pair = finish(
        place,
        (lo, lo_far, ro, ro_far, li, ri, go, go_far, gi, gi_far),
        pair_home,
        norm_in,
        grad_mid,
        grad_gate,
        scores,
        mask_rows,
        gain_pair.reshape(-1, 1),
        w8,
        wall,
    )
    grad_back = send_home([g0, g1, g2, g3])

    def reduce(parts):
        packed = jnp.concatenate(parts, axis=1).astype(jnp.float32)
        count = packed.shape[1]
        packed = jnp.pad(packed, ((0, 0), (0, -count % 128), (0, 0)))
        y = lax.axis_index(DP) // 2
        rounds = (
            (core, DP, core_pairs),
            (x, ROWS, row_pairs),
            (y, DP, [(d, d ^ 2) for d in range(mesh_shape[0])]),
        )
        for side, axis, pairs in rounds:
            half = packed.shape[1] // 2
            low, high = packed[:, :half], packed[:, half:]
            sent = jnp.where(side == 0, high, low).astype(jnp.bfloat16)
            kept = jnp.where(side == 0, low, high)
            packed = kept + lax.ppermute(sent, axis, pairs).astype(jnp.float32)
        low = packed.astype(jnp.bfloat16)
        total = lax.dynamic_index_in_dim(packed, z, 0, keepdims=False)
        for m in range(1, groups):
            sent = lax.dynamic_index_in_dim(low, z ^ m, 0, keepdims=False)
            total = total + lax.ppermute(
                sent, CHAN, [(c, c ^ m) for c in range(groups)]
            ).astype(jnp.float32)
        total = total.astype(jnp.bfloat16)
        for side, axis, pairs in rounds[::-1]:
            far = lax.ppermute(total, axis, pairs)
            total = jnp.concatenate(
                [jnp.where(side == 0, total, far), jnp.where(side == 0, far, total)]
            )
        total = total.astype(jnp.float32)
        cuts, at = [], 0
        for part in parts:
            cuts.append(total[at : at + part.shape[1]])
            at += part.shape[1]
        return cuts

    def by_chan(value):
        a, b, c = value.shape
        return value.reshape(a, groups, b // groups, c).transpose(1, 0, 2, 3).reshape(groups, -1, c)

    def gains(*values):
        return jnp.concatenate(
            [value.reshape(-1, groups, value.shape[-1] // groups).transpose(1, 0, 2).reshape(groups, -1) for value in values],
            axis=1,
        ).reshape(groups, -1, chans)

    gq, ga, gni, gno = gw_node
    early = reduce(
        [
            gw_in.reshape(groups, -1, chans),
            gw_out.reshape(groups, -1, chans),
            by_chan(gw_tri),
            by_chan(gq).reshape(groups, -1, chans),
            ga.reshape(groups, -1, chans),
            gni.reshape(groups, -1, chans),
            gno.reshape(groups, -1, chans),
            gains(*gg_node),
            gains(jnp.sum(gg_trans, axis=-1), jnp.sum(gg_tri, axis=-1), jnp.zeros_like(gain_trans)),
        ]
    )
    tri_rows, gate_rows = 8 * chans, 10 * chans
    late = reduce(
        [
            gw[:tri_rows].reshape(groups, -1, chans),
            by_chan(gw[tri_rows:gate_rows].reshape(2, chans, chans)),
            gw[gate_rows : gate_rows + heads].reshape(groups, -1, chans),
            gains(jnp.sum(gg_pair, axis=-1), jnp.zeros((3, chans), jnp.float32)),
        ]
    )
    quarter = chans // groups

    def assemble(pieces):
        return jnp.stack(
            [lax.dynamic_index_in_dim(jnp.stack(pieces), z ^ k, 0, keepdims=False) for k in range(groups)]
        )

    node_quarter = nodes // groups
    return (
        assemble(out_back),
        assemble(node_out_back),
        assemble(grad_back),
        assemble(node_grad_back),
        late[3].reshape(4, quarter)[0],
        late[0].reshape(2, 4, quarter, chans).transpose(0, 1, 3, 2),
        late[1].reshape(2, quarter, chans).transpose(0, 2, 1),
        early[8].reshape(4, quarter)[1:3],
        early[2].reshape(2, quarter, chans).transpose(0, 2, 1),
        early[8].reshape(4, quarter)[0],
        early[0].T,
        early[1],
        late[2].T,
        early[7].reshape(2, node_quarter)[0],
        early[3].reshape(3, node_quarter, nodes).transpose(0, 2, 1),
        early[4].reshape(node_quarter, nodes).T,
        early[7].reshape(2, node_quarter)[1],
        early[5].reshape(-1, nodes).T,
        early[6].reshape(-1, nodes),
    )


def node_track(node_in, cot, bias, live, wq, wa, wni, wno, gain_node, gain_node_trans):
    length, nodes = node_in.shape
    heads = bias.shape[0]
    head_dim = wq.shape[1] // heads
    scale = 1.0 / math.sqrt(head_dim)
    key_live = live[None, None, :] > 0.5

    def parts(value):
        centered = value - jnp.mean(value, axis=-1, keepdims=True)
        inverse = lax.rsqrt(jnp.mean(centered * centered, axis=-1, keepdims=True) + epsilon)
        return centered * inverse, inverse

    def back(gain, scaled, inverse, grad):
        weighted = gain * grad
        first = jnp.mean(weighted, axis=-1, keepdims=True)
        second = jnp.mean(weighted * scaled, axis=-1, keepdims=True)
        return inverse * (weighted - first - scaled * second)

    def mul(spec, a, b):
        return jnp.einsum(spec, a, b, preferred_element_type=jnp.float32)

    scaled_in, inverse_in = parts(node_in)
    low_in = (scaled_in * gain_node).astype(jnp.bfloat16)
    qkv = mul("in,gan->gia", low_in, wq).astype(jnp.bfloat16)
    queries, keys, values = (qkv[g].reshape(length, heads, head_dim) for g in range(3))
    raw = mul("ihd,jhd->hij", queries, keys) * scale + bias
    probs = softmax_rows(jnp.where(key_live, raw, masked_score))
    probs_low = probs.astype(jnp.bfloat16)
    attn = mul("hij,jhd->ihd", probs_low, values).astype(jnp.bfloat16).reshape(length, -1)
    mid = node_in + mul("ia,na->in", attn, wa)
    scaled_mid, inverse_mid = parts(mid)
    low_mid = (scaled_mid * gain_node_trans).astype(jnp.bfloat16)
    pre = mul("in,fn->if", low_mid, wni)
    act, slope = gelu_both(pre)
    act = act.astype(jnp.bfloat16)
    node_out = mid + mul("if,fn->in", act, wno)
    grad_pre = (mul("in,fn->if", cot, wno) * slope).astype(jnp.bfloat16)
    gno = mul("if,in->fn", act, cot)
    gni = mul("if,in->fn", grad_pre, low_mid)
    grad = mul("if,fn->in", grad_pre, wni)
    gg_mid = jnp.sum(grad * scaled_mid, axis=0)
    grad_mid = cot.astype(jnp.float32) + back(gain_node_trans, scaled_mid, inverse_mid, grad)
    grad_low = grad_mid.astype(jnp.bfloat16)
    ga = mul("in,ia->na", grad_low, attn)
    grad_attn = mul("in,na->ia", grad_low, wa).astype(jnp.bfloat16).reshape(length, heads, head_dim)
    grad_probs = mul("ihd,jhd->hij", grad_attn, values)
    delta = jnp.sum(probs * grad_probs, axis=2, keepdims=True)
    scores = (probs * (grad_probs - delta)).astype(jnp.bfloat16)
    grad_q = mul("hij,jhd->ihd", scores, keys) * scale
    grad_k = mul("hij,ihd->jhd", scores, queries) * scale
    grad_v = mul("hij,ihd->jhd", probs_low, grad_attn)
    grad_qkv = jnp.stack([v.reshape(length, -1) for v in (grad_q, grad_k, grad_v)]).astype(jnp.bfloat16)
    gq = mul("gia,in->gan", grad_qkv, low_in)
    grad = mul("gia,gan->in", grad_qkv, wq)
    gg_in = jnp.sum(grad * scaled_in, axis=0)
    node_grad = grad_mid + back(gain_node, scaled_in, inverse_in, grad)
    halves = [0.5 * v for v in (gq, ga, gni, gno)]
    return node_out, node_grad, scores, halves, (0.5 * gg_in, 0.5 * gg_mid)


def solution(mesh):
    in_specs = (
        P(DP, ROWS, CHAN, None),
        P(DP, ROWS, CHAN),
        P(DP, ROWS, CHAN, None),
        P(DP, ROWS, CHAN),
        P(DP),
        P(DP, None),
        P(),
        P(None, None, None, CHAN),
        P(None, None, CHAN),
        P(),
        P(None, None, CHAN),
        P(),
        P(None, CHAN),
        P(CHAN, None),
        P(None, CHAN),
        P(),
        P(None, None, CHAN),
        P(None, CHAN),
        P(),
        P(None, CHAN),
        P(CHAN, None),
    )
    out_specs = (
        P(DP, ROWS, CHAN, None),
        P(DP, ROWS, CHAN),
        P(DP, ROWS, CHAN, None),
        P(DP, ROWS, CHAN),
        P(CHAN),
        P(None, None, None, CHAN),
        P(None, None, CHAN),
        P(None, CHAN),
        P(None, None, CHAN),
        P(CHAN),
        P(None, CHAN),
        P(CHAN, None),
        P(None, CHAN),
        P(CHAN),
        P(None, None, CHAN),
        P(None, CHAN),
        P(CHAN),
        P(None, CHAN),
        P(CHAN, None),
    )
    sizes = dict(mesh.shape)
    by_crop = sizes[ROWS] == 2 and sizes[DP] == 4 and sizes[CHAN] == 4
    body = shards_by_crop if by_crop else shards
    return jax.shard_map(body, mesh=mesh, in_specs=in_specs, out_specs=out_specs, check_vma=False)
```

```python
import functools
import math

import jax
import jax.numpy as jnp
from jax import lax
from jax.experimental import pallas as pl
from jax.experimental.pallas import tpu as pltpu
from jax.sharding import PartitionSpec as P

f32, bf16 = jnp.float32, jnp.bfloat16
epsilon = 1e-05
DP, ROWS, CHAN = "dp", "rows", "chan"
masked_score = -1000000000.0


def norm_parts(full):
    mean = jnp.mean(full, axis=2, keepdims=True)
    centered = full - mean
    variance = jnp.mean(centered * centered, axis=2, keepdims=True)
    inverse = lax.rsqrt(variance + epsilon)
    return (centered * inverse, inverse)


def shaped(gain, full):
    return gain.reshape(gain.shape + (1,) * (full.ndim - 3))


def normed(full, gain):
    scaled, inverse = norm_parts(full)
    return scaled * shaped(gain, full)


def stat_terms(full, gain, partial_value, groups):
    scaled, inverse = norm_parts(full)
    weighted = shaped(gain, full) * partial_value
    first_sum = jnp.sum(weighted, axis=2)
    second_sum = jnp.sum(weighted * scaled, axis=2)
    stacked = jnp.stack([first_sum, second_sum], axis=2)
    repeats = (1, 1, groups) + (1,) * (full.ndim - 3)
    return jnp.tile(stacked, repeats)


def norm_finish(full, gain, grad_here, totals, chan_index):
    width = full.shape[2]
    here = grad_here.shape[2]
    scaled, inverse = norm_parts(full)
    scaled_here = lax.dynamic_slice_in_dim(scaled, chan_index * here, here, 2)
    gain_here = lax.dynamic_slice_in_dim(gain, chan_index * here, here, 0)
    first_mean = totals[:, :, 0:1] / width
    second_mean = totals[:, :, 1:2] / width
    grad_input = inverse * (
        shaped(gain_here, full) * grad_here - first_mean - scaled_here * second_mean
    )
    summed_axes = (0, 1) + tuple(range(3, full.ndim))
    grad_gain = jnp.sum(grad_here * scaled_here, axis=summed_axes)
    return (grad_input, grad_gain)


def gelu_exact(value):
    return jax.nn.gelu(value, approximate=False)


def softmax_rows(scores):
    top = jnp.max(scores, axis=-1, keepdims=True)
    exps = jnp.exp(scores - top)
    return exps / jnp.sum(exps, axis=-1, keepdims=True)


def shards(
    pair,
    node,
    pair_cot,
    node_cot,
    lengths,
    present,
    gain_pair,
    w_tri_in,
    w_out_gate,
    gain_tri,
    w_tri_out,
    gain_trans,
    w_trans_in,
    w_trans_out,
    w_bias,
    gain_node,
    w_qkv,
    w_attn_out,
    gain_node_trans,
    w_node_in,
    w_node_out,
):
    batch = pair.shape[0]
    rows_here = pair.shape[1]
    crop_len = pair.shape[3]
    groups = lax.axis_size(CHAN)
    chan_index = lax.axis_index(CHAN)
    row_start = lax.axis_index(ROWS) * rows_here
    heads_here = w_bias.shape[1]
    head_dim = w_qkv.shape[2] // heads_here
    scale = 1.0 / math.sqrt(head_dim)
    positions = jnp.arange(crop_len, dtype=jnp.int32)
    mask_all = present.astype(jnp.float32) * (positions[None, :] < lengths[:, None]).astype(
        jnp.float32
    )
    mask_rows = lax.dynamic_slice_in_dim(mask_all, row_start, rows_here, 1)
    pair_mask = mask_rows[:, :, None, None] * mask_all[:, None, None, :]
    key_live = mask_all[:, None, None, :] > 0.5

    def gating(gate, value):
        return jax.nn.sigmoid(gate) * value * pair_mask

    pair_whole, node_whole = (
        lax.all_gather(pair, CHAN, axis=2, tiled=True),
        lax.all_gather(node, CHAN, axis=2, tiled=True),
    )
    full_in = pair_whole.astype(jnp.float32)
    node_full = node_whole.astype(jnp.float32)
    stream_in = pair.astype(jnp.float32)
    node_in = node.astype(jnp.float32)
    normed_in = normed(full_in, gain_pair).astype(jnp.bfloat16)
    projected = jnp.einsum(
        "bicj,dgch->dgbihj", normed_in, w_tri_in, preferred_element_type=jnp.float32
    )
    gate_pre = jnp.einsum(
        "bicj,dcx->dbixj", normed_in, w_out_gate, preferred_element_type=jnp.float32
    )
    bias = jnp.einsum("bicj,ch->bhij", normed_in, w_bias, preferred_element_type=jnp.float32)
    left_out = gating(projected[0, 0], projected[0, 1]).astype(jnp.bfloat16)
    right_out = gating(projected[0, 2], projected[0, 3]).astype(jnp.bfloat16)
    left_in = gating(projected[1, 0], projected[1, 1]).astype(jnp.bfloat16)
    right_in = gating(projected[1, 2], projected[1, 3]).astype(jnp.bfloat16)
    normed_node = normed(node_full, gain_node).astype(jnp.bfloat16)
    qkv = jnp.einsum(
        "bin,gna->gbia", normed_node, w_qkv, preferred_element_type=jnp.float32
    ).astype(jnp.bfloat16)
    whole_right_out, whole_right_in, whole_keys, whole_values = (
        lax.all_gather(right_out, ROWS, axis=1, tiled=True),
        lax.all_gather(right_in, ROWS, axis=1, tiled=True),
        lax.all_gather(qkv[1], ROWS, axis=1, tiled=True),
        lax.all_gather(qkv[2], ROWS, axis=1, tiled=True),
    )
    left_cols = lax.all_to_all(left_in, ROWS, split_axis=3, concat_axis=1, tiled=True)
    queries = qkv[0].reshape(batch, rows_here, heads_here, head_dim)
    keys = whole_keys.reshape(batch, crop_len, heads_here, head_dim)
    values = whole_values.reshape(batch, crop_len, heads_here, head_dim)
    raw = (
        jnp.einsum("bihd,bjhd->bhij", queries, keys, preferred_element_type=jnp.float32) * scale
        + bias
    )
    probs = softmax_rows(jnp.where(key_live, raw, masked_score))
    probs_low = probs.astype(jnp.bfloat16)
    attn = jnp.einsum(
        "bhij,bjhd->bihd", probs_low, values, preferred_element_type=jnp.float32
    ).astype(jnp.bfloat16)
    attn = attn.reshape(batch, rows_here, heads_here * head_dim)
    tri_out = jnp.einsum(
        "bihk,bjhk->bihj", left_out, whole_right_out, preferred_element_type=jnp.float32
    )
    tri_in = jnp.einsum(
        "bkhi,bkhj->bihj", left_cols, whole_right_in, preferred_element_type=jnp.float32
    )
    tri_full_out, tri_full_in, attn_whole = (
        lax.all_gather(tri_out.astype(jnp.bfloat16), CHAN, axis=2, tiled=True).astype(
            tri_out.dtype
        ),
        lax.all_gather(tri_in.astype(jnp.bfloat16), CHAN, axis=2, tiled=True).astype(
            tri_in.dtype
        ),
        lax.all_gather(
            attn.astype(jnp.float32).astype(jnp.bfloat16), CHAN, axis=2, tiled=True
        ).astype(jnp.float32),
    )
    normed_out = normed(tri_full_out, gain_tri[0]).astype(jnp.bfloat16)
    normed_inc = normed(tri_full_in, gain_tri[1]).astype(jnp.bfloat16)
    branch_out = jnp.einsum(
        "bihj,hc->bicj", normed_out, w_tri_out[0], preferred_element_type=jnp.float32
    )
    branch_inc = jnp.einsum(
        "bihj,hc->bicj", normed_inc, w_tri_out[1], preferred_element_type=jnp.float32
    )
    gate_sig = jax.nn.sigmoid(gate_pre)
    stream_mid = stream_in + gate_sig[0] * branch_out + gate_sig[1] * branch_inc
    attn_low = attn_whole.astype(jnp.bfloat16)
    node_mid = node_in + jnp.einsum(
        "bia,an->bin", attn_low, w_attn_out, preferred_element_type=jnp.float32
    )
    full_mid, node_full_mid = (
        lax.all_gather(stream_mid.astype(jnp.bfloat16), CHAN, axis=2, tiled=True).astype(
            stream_mid.dtype
        ),
        lax.all_gather(node_mid.astype(jnp.bfloat16), CHAN, axis=2, tiled=True).astype(
            node_mid.dtype
        ),
    )
    normed_mid = normed(full_mid, gain_trans).astype(jnp.bfloat16)
    pre_hidden = jnp.einsum(
        "bicj,cf->bifj", normed_mid, w_trans_in, preferred_element_type=jnp.float32
    )
    hidden, gelu_pull = jax.vjp(gelu_exact, pre_hidden)
    hidden_low = hidden.astype(jnp.bfloat16)
    out_terms = jnp.einsum(
        "bifj,fc->bicj", hidden_low, w_trans_out, preferred_element_type=jnp.float32
    )
    normed_node_mid = normed(node_full_mid, gain_node_trans).astype(jnp.bfloat16)
    node_pre = jnp.einsum(
        "bin,nf->bif", normed_node_mid, w_node_in, preferred_element_type=jnp.float32
    )
    node_hidden, node_gelu_pull = jax.vjp(gelu_exact, node_pre)
    node_hidden_low = node_hidden.astype(jnp.bfloat16)
    node_terms = jnp.einsum(
        "bif,fn->bin", node_hidden_low, w_node_out, preferred_element_type=jnp.float32
    )
    pair_sum, node_sum = (
        lax.psum_scatter(
            out_terms.astype(jnp.bfloat16), CHAN, scatter_dimension=2, tiled=True
        ).astype(jnp.float32),
        lax.psum_scatter(
            node_terms.astype(jnp.bfloat16), CHAN, scatter_dimension=2, tiled=True
        ).astype(jnp.float32),
    )
    stream_out = stream_mid + pair_sum
    node_out = node_mid + node_sum
    cot_full, node_cot_full = (
        lax.all_gather(pair_cot, CHAN, axis=2, tiled=True),
        lax.all_gather(node_cot, CHAN, axis=2, tiled=True),
    )
    grad_trans_out = jnp.einsum(
        "bifj,bicj->fc", hidden_low, cot_full, preferred_element_type=jnp.float32
    )
    grad_hidden = jnp.einsum(
        "bicj,fc->bifj", cot_full, w_trans_out, preferred_element_type=jnp.float32
    )
    grad_pre = gelu_pull(grad_hidden)[0].astype(jnp.bfloat16)
    grad_trans_in = jnp.einsum(
        "bicj,bifj->cf", normed_mid, grad_pre, preferred_element_type=jnp.float32
    )
    grad_normed_mid = jnp.einsum(
        "bifj,cf->bicj", grad_pre, w_trans_in, preferred_element_type=jnp.float32
    )
    mid_terms = stat_terms(full_mid, gain_trans, grad_normed_mid, groups)
    grad_node_out_w = jnp.einsum(
        "bif,bin->fn", node_hidden_low, node_cot_full, preferred_element_type=jnp.float32
    )
    grad_node_hidden = jnp.einsum(
        "bin,fn->bif", node_cot_full, w_node_out, preferred_element_type=jnp.float32
    )
    grad_node_pre = node_gelu_pull(grad_node_hidden)[0].astype(jnp.bfloat16)
    grad_node_in_w = jnp.einsum(
        "bin,bif->nf", normed_node_mid, grad_node_pre, preferred_element_type=jnp.float32
    )
    grad_normed_node_mid = jnp.einsum(
        "bif,nf->bin", grad_node_pre, w_node_in, preferred_element_type=jnp.float32
    )
    node_mid_terms = stat_terms(node_full_mid, gain_node_trans, grad_normed_node_mid, groups)
    mid_here, mid_totals, node_mid_here, node_mid_totals = (
        lax.psum_scatter(
            grad_normed_mid.astype(jnp.bfloat16), CHAN, scatter_dimension=2, tiled=True
        ).astype(jnp.float32),
        lax.psum_scatter(
            mid_terms.astype(jnp.bfloat16), CHAN, scatter_dimension=2, tiled=True
        ).astype(jnp.float32),
        lax.psum_scatter(
            grad_normed_node_mid.astype(jnp.bfloat16), CHAN, scatter_dimension=2, tiled=True
        ).astype(jnp.float32),
        lax.psum_scatter(
            node_mid_terms.astype(jnp.bfloat16), CHAN, scatter_dimension=2, tiled=True
        ).astype(jnp.float32),
    )
    mid_extra, grad_gain_trans = norm_finish(full_mid, gain_trans, mid_here, mid_totals, chan_index)
    node_mid_extra, grad_gain_node_trans = norm_finish(
        node_full_mid, gain_node_trans, node_mid_here, node_mid_totals, chan_index
    )
    grad_mid = pair_cot.astype(jnp.float32) + mid_extra
    grad_node_mid = node_cot.astype(jnp.float32) + node_mid_extra
    branches = jnp.stack([branch_out, branch_inc])
    grad_branch = (gate_sig * grad_mid[None]).astype(jnp.bfloat16)
    grad_gate = (grad_mid[None] * branches * gate_sig * (1.0 - gate_sig)).astype(jnp.bfloat16)
    tri_normed_both = jnp.stack([normed_out, normed_inc])
    grad_w_tri_out = jnp.einsum(
        "dbihj,dbicj->dhc", tri_normed_both, grad_branch, preferred_element_type=jnp.float32
    )
    grad_out_gate = jnp.einsum(
        "bicj,dbixj->dcx", normed_in, grad_gate, preferred_element_type=jnp.float32
    )
    grad_tri_normed = jnp.einsum(
        "dbicj,dhc->dbihj", grad_branch, w_tri_out, preferred_element_type=jnp.float32
    )
    out_stats = stat_terms(tri_full_out, gain_tri[0], grad_tri_normed[0], groups)
    inc_stats = stat_terms(tri_full_in, gain_tri[1], grad_tri_normed[1], groups)
    grad_attn_branch = grad_node_mid.astype(jnp.bfloat16)
    grad_w_attn_out = jnp.einsum(
        "bia,bin->an", attn_low, grad_attn_branch, preferred_element_type=jnp.float32
    )
    attn_terms = jnp.einsum(
        "bin,an->bia", grad_attn_branch, w_attn_out, preferred_element_type=jnp.float32
    )
    out_here, out_totals, inc_here, inc_totals, attn_here = (
        lax.psum_scatter(
            grad_tri_normed[0].astype(jnp.bfloat16), CHAN, scatter_dimension=2, tiled=True
        ).astype(jnp.float32),
        lax.psum_scatter(
            out_stats.astype(jnp.bfloat16), CHAN, scatter_dimension=2, tiled=True
        ).astype(jnp.float32),
        lax.psum_scatter(
            grad_tri_normed[1].astype(jnp.bfloat16), CHAN, scatter_dimension=2, tiled=True
        ).astype(jnp.float32),
        lax.psum_scatter(
            inc_stats.astype(jnp.bfloat16), CHAN, scatter_dimension=2, tiled=True
        ).astype(jnp.float32),
        lax.psum_scatter(
            attn_terms.astype(jnp.bfloat16), CHAN, scatter_dimension=2, tiled=True
        ).astype(jnp.float32),
    )
    grad_tri_a, gain_grad_out = norm_finish(
        tri_full_out, gain_tri[0], out_here, out_totals, chan_index
    )
    grad_tri_b, gain_grad_inc = norm_finish(
        tri_full_in, gain_tri[1], inc_here, inc_totals, chan_index
    )
    grad_gain_tri = jnp.stack([gain_grad_out, gain_grad_inc])
    grad_out_low = grad_tri_a.astype(jnp.bfloat16)
    grad_inc_low = grad_tri_b.astype(jnp.bfloat16)
    grad_attn = attn_here.astype(jnp.bfloat16).reshape(batch, rows_here, heads_here, head_dim)
    grad_probs = jnp.einsum(
        "bihd,bjhd->bhij", grad_attn, values, preferred_element_type=jnp.float32
    )
    delta = jnp.sum(probs * grad_probs, axis=3, keepdims=True)
    grad_scores = (probs * (grad_probs - delta)).astype(jnp.bfloat16)
    grad_queries = (
        jnp.einsum("bhij,bjhd->bihd", grad_scores, keys, preferred_element_type=jnp.float32) * scale
    )
    key_terms = (
        jnp.einsum("bhij,bihd->bjhd", grad_scores, queries, preferred_element_type=jnp.float32)
        * scale
    )
    value_terms = jnp.einsum(
        "bhij,bihd->bjhd", probs_low, grad_attn, preferred_element_type=jnp.float32
    )
    grad_w_bias = jnp.einsum(
        "bicj,bhij->ch", normed_in, grad_scores, preferred_element_type=jnp.float32
    )
    bias_back = jnp.einsum("bhij,ch->bicj", grad_scores, w_bias, preferred_element_type=jnp.float32)
    grad_left_out = jnp.einsum(
        "bihj,bjhk->bihk", grad_out_low, whole_right_out, preferred_element_type=jnp.float32
    )
    right_terms = jnp.einsum(
        "bihj,bihk->bjhk", grad_out_low, left_out, preferred_element_type=jnp.float32
    )
    grad_right_out, key_grads, value_grads = (
        lax.psum_scatter(
            right_terms.astype(jnp.bfloat16), ROWS, scatter_dimension=1, tiled=True
        ).astype(jnp.float32),
        lax.psum_scatter(
            key_terms.astype(jnp.bfloat16), ROWS, scatter_dimension=1, tiled=True
        ).astype(jnp.float32),
        lax.psum_scatter(
            value_terms.astype(jnp.bfloat16), ROWS, scatter_dimension=1, tiled=True
        ).astype(jnp.float32),
    )
    whole_grad_in = lax.all_gather(grad_inc_low, ROWS, axis=1, tiled=True)
    grad_left_in = jnp.einsum(
        "bihj,bkhj->bkhi", whole_grad_in, right_in, preferred_element_type=jnp.float32
    )
    grad_right_in = jnp.einsum(
        "bkhi,bihj->bkhj", left_in, whole_grad_in, preferred_element_type=jnp.float32
    )

    def gate_back(first, second, grad):
        kept_value, pull = jax.vjp(gating, first, second)
        return pull(grad)

    left_gate_out, left_value_out = gate_back(projected[0, 0], projected[0, 1], grad_left_out)
    right_gate_out, right_value_out = gate_back(projected[0, 2], projected[0, 3], grad_right_out)
    left_gate_in, left_value_in = gate_back(projected[1, 0], projected[1, 1], grad_left_in)
    right_gate_in, right_value_in = gate_back(projected[1, 2], projected[1, 3], grad_right_in)
    grad_proj = jnp.stack(
        [
            jnp.stack([left_gate_out, left_value_out, right_gate_out, right_value_out]),
            jnp.stack([left_gate_in, left_value_in, right_gate_in, right_value_in]),
        ]
    ).astype(jnp.bfloat16)
    grad_tri_in_w = jnp.einsum(
        "bicj,dgbihj->dgch", normed_in, grad_proj, preferred_element_type=jnp.float32
    )
    grad_normed_in = jnp.einsum(
        "dgbihj,dgch->bicj", grad_proj, w_tri_in, preferred_element_type=jnp.float32
    )
    grad_normed_in = grad_normed_in + jnp.einsum(
        "dbixj,dcx->bicj", grad_gate, w_out_gate, preferred_element_type=jnp.float32
    )
    grad_normed_in = grad_normed_in + bias_back
    grad_qkv = jnp.stack(
        [
            grad_queries.reshape(batch, rows_here, heads_here * head_dim),
            key_grads.reshape(batch, rows_here, heads_here * head_dim),
            value_grads.reshape(batch, rows_here, heads_here * head_dim),
        ]
    ).astype(jnp.bfloat16)
    grad_w_qkv = jnp.einsum(
        "bin,gbia->gna", normed_node, grad_qkv, preferred_element_type=jnp.float32
    )
    grad_normed_node = jnp.einsum(
        "gbia,gna->bin", grad_qkv, w_qkv, preferred_element_type=jnp.float32
    )
    in_terms = stat_terms(full_in, gain_pair, grad_normed_in, groups)
    node_in_terms = stat_terms(node_full, gain_node, grad_normed_node, groups)
    in_here, in_totals, node_in_here, node_in_totals = (
        lax.psum_scatter(
            grad_normed_in.astype(jnp.bfloat16), CHAN, scatter_dimension=2, tiled=True
        ).astype(jnp.float32),
        lax.psum_scatter(
            in_terms.astype(jnp.bfloat16), CHAN, scatter_dimension=2, tiled=True
        ).astype(jnp.float32),
        lax.psum_scatter(
            grad_normed_node.astype(jnp.bfloat16), CHAN, scatter_dimension=2, tiled=True
        ).astype(jnp.float32),
        lax.psum_scatter(
            node_in_terms.astype(jnp.bfloat16), CHAN, scatter_dimension=2, tiled=True
        ).astype(jnp.float32),
    )
    in_extra, grad_gain_pair = norm_finish(full_in, gain_pair, in_here, in_totals, chan_index)
    node_in_extra, grad_gain_node = norm_finish(
        node_full, gain_node, node_in_here, node_in_totals, chan_index
    )
    grad_stream = grad_mid + in_extra
    node_grad = grad_node_mid + node_in_extra
    summed = lax.psum(
        (
            grad_gain_pair,
            grad_tri_in_w,
            grad_out_gate,
            grad_gain_tri,
            grad_w_tri_out,
            grad_gain_trans,
            grad_trans_in,
            grad_trans_out,
            grad_w_bias,
            grad_gain_node,
            grad_w_qkv,
            grad_w_attn_out,
            grad_gain_node_trans,
            grad_node_in_w,
            grad_node_out_w,
        ),
        (DP, ROWS),
    )
    return (
        stream_out.astype(jnp.bfloat16),
        node_out.astype(jnp.bfloat16),
        grad_stream.astype(jnp.bfloat16),
        node_grad.astype(jnp.bfloat16),
        summed[0],
        summed[1],
        summed[2],
        summed[3],
        summed[4],
        summed[5],
        summed[6],
        summed[7],
        summed[8],
        summed[9],
        summed[10],
        summed[11],
        summed[12],
        summed[13],
        summed[14],
    )


ORDER = (3, 2, 0, 1)
IN_LEFT, IN_RIGHT, OUT_RIGHT, OUT_LEFT = range(4)

group = 8


def dot(a, b, ca=1, cb=0):
    return lax.dot_general(a, b, (((ca,), (cb,)), ((), ())), preferred_element_type=f32)


def sigmoid(v):
    return 0.5 * jnp.tanh(0.5 * v) + 0.5


def sub_norm(full):
    mean = jnp.mean(full, axis=0, keepdims=True)
    centered = full - mean
    inverse = lax.rsqrt(jnp.mean(centered * centered, axis=0, keepdims=True) + epsilon)
    return centered * inverse, inverse


def sub_norm_back(gain, scaled, inverse, grad):
    weighted = gain * grad
    first = jnp.mean(weighted, axis=0, keepdims=True)
    second = jnp.mean(weighted * scaled, axis=0, keepdims=True)
    return inverse * (weighted - first - scaled * second)


def gelu_both(value):
    cdf = 0.5 * (1.0 + lax.erf(value * (0.5**0.5)))
    density = jnp.exp(-0.5 * value * value) * (1.0 / math.sqrt(2.0 * math.pi))
    return value * cdf, cdf + value * density


def lane_sums(value):
    value = sum(value[:, at : at + 128] for at in range(0, value.shape[1], 128))
    ones = jnp.ones((8, value.shape[1]), f32)
    sums = lax.dot_general(
        ones,
        value,
        (((1,), (1,)), ((), ())),
        precision=lax.Precision.HIGHEST,
        preferred_element_type=f32,
    )
    return sums[:1]


def place_spec():
    return pl.BlockSpec(memory_space=pltpu.SMEM)


def whole_spec(a):
    zeros = (0,) * len(a.shape)
    return pl.BlockSpec(a.shape, lambda s: zeros)


def in_hbm(shape, dtype):
    return pltpu.HBM(shape, dtype)


def held(arrays):
    return [pltpu.with_memory_space_constraint(a, pltpu.HBM) for a in arrays]


def params(mib):
    return pltpu.CompilerParams(vmem_limit_bytes=mib * 2**20)


quick = pl.CostEstimate(flops=1, bytes_accessed=1, transcendentals=0)


def pack_kernel(first_row, rows, live_rows, place_ref, *refs):
    z, part = place_ref[0], 2 * place_ref[2] + place_ref[1]
    sems = refs[-1]
    outs = refs[-7:-3] if live_rows else refs[-5:-1]
    more = outs[0].shape[0] - rows
    copies = []
    for m in range(4):
        rows_of = refs[0].at[lax.bitwise_xor(z, m), pl.ds(first_row, rows)]
        copies.append(pltpu.make_async_copy(rows_of, outs[m].at[pl.ds(0, rows)], sems.at[m]))
    if more and not live_rows:
        for m in range(4):
            rows_of = refs[1].at[pl.ds(part * more, more)]
            copies.append(pltpu.make_async_copy(rows_of, outs[m].at[pl.ds(rows, more)], sems.at[4 + m]))
    for copy in copies:
        copy.start()
    if live_rows:
        lengths, present, node, node_cot, tri_in, gate, bias, tri_out, trans_in, trans_out = refs[1:11]
        extra, weights = refs[-3:-1]
        quarter, width = extra.shape[2:]
        position = lax.broadcasted_iota(jnp.int32, (1, width), 1)
        for crop in range(4):
            for n, ref in enumerate((node, node_cot)):
                value = ref[crop].astype(f32)
                extra[crop, 1 + n] = jnp.concatenate([value[:quarter], value[quarter:]], axis=1).astype(bf16)
            there = jnp.where(position < lengths[crop], present[crop : crop + 1], 0).astype(f32)
            extra[crop, 0] = jnp.broadcast_to(there, (quarter, width)).astype(bf16)
        parts = [tri_in[...], gate[...]]
        low = bias[...].astype(f32)
        parts.append(jnp.concatenate([low, jnp.zeros((32 - low.shape[0], width), f32)], axis=0).astype(bf16))
        parts += [tri_out[...], trans_in[...].astype(f32).T.astype(bf16), trans_out[...]]
        count = sum(part.shape[0] for part in parts)
        parts.append(jnp.zeros((quarter * weights.shape[0] - count, width), bf16))
        weights[...] = jnp.concatenate(parts, axis=0).reshape(weights.shape)
        for m in range(4):
            outs[m][rows : rows + 3] = extra[lax.bitwise_xor(z, m)]
            outs[m][rows + 3 :] = weights[pl.ds(place_ref[2] * (more - 3), more - 3)]
    for copy in copies:
        copy.wait()


def pack(place, source, first_row, rows, weights=None, first=None):
    _, _, quarter, width = source.shape
    vmem = pl.BlockSpec(memory_space=pltpu.VMEM)
    operands, specs, scratch, more = [place, *held([source])], [place_spec(), any_spec()], [], 0
    if first is not None:
        count = sum(a.shape[0] for a in first[4:]) + 32 - first[6].shape[0]
        count = -(-count // (2 * quarter)) * 2
        operands += first[:1] + held(first[1:])
        specs += [place_spec()] + [vmem] * (len(first) - 1)
        scratch = [pltpu.VMEM((4, 3, quarter, width), bf16), pltpu.VMEM((count, quarter, width), bf16)]
        more = 3 + count // 2
    elif weights is not None:
        operands += held([weights])
        specs.append(any_spec())
        more = weights.shape[0] // 4
    return pl.pallas_call(
        functools.partial(pack_kernel, first_row, rows, first is not None),
        in_specs=specs,
        out_specs=[vmem] * 4,
        out_shape=[in_hbm((rows + more, quarter, width), bf16)] * 4,
        scratch_shapes=scratch + [pltpu.SemaphoreType.DMA((8,))],
        compiler_params=params(24),
        cost_estimate=quick,
        name="pack",
    )(*operands)


def project_kernel(
    place_ref, p0, p1, p2, p3, wall_ref, mask_ref, gain_ref, tri_ref, norm_ref, pair_ref, bias_ref, pc, w_s, wb_s, bs, *kept_s
):
    pieces = (p0, p1, p2, p3)
    rows, quarter, width = p0.shape
    chans = 4 * quarter
    z = place_ref[0]
    gain = jnp.concatenate([gain_ref[...]] * group, axis=1)
    heads = bias_ref.shape[0]
    tri_rows = 8 * quarter

    @pl.when(pl.program_id(0) == 0)
    def _():
        for g in range(4):
            w_s[g * tri_rows : (g + 1) * tri_rows] = wall_ref[lax.bitwise_xor(z, g), :tri_rows]
            wb_s[g * 16 : (g + 1) * 16] = wall_ref[lax.bitwise_xor(z, g), 10 * quarter : 10 * quarter + 16]

    for m in range(4):
        pc[lax.bitwise_xor(z, m)] = pieces[m][...]

    @pl.loop(0, rows // group)
    def _(step):
        first = step * group

        def wide(get):
            return jnp.concatenate([get(first + n) for n in range(group)], axis=1)

        rows_in = [jnp.concatenate([pc[q, first + n] for q in range(4)], axis=0) for n in range(group)]
        for n in range(group):
            pair_ref[first + n] = rows_in[n]
        scaled, _ = sub_norm(jnp.concatenate(rows_in, axis=1).astype(f32))
        low = (scaled * gain).astype(bf16)
        for n in range(group):
            norm_ref[first + n] = low[:, n * width : (n + 1) * width]
        mask = wide(lambda r: mask_ref[pl.ds(r, 1), :])
        bias = dot(wb_s[...], low)
        for n in range(group):
            for g in range(4):
                at = (first + n) * heads + g * (heads // 4)
                bs[pl.ds(at, heads // 4), :] = bias[g * 16 : g * 16 + heads // 4, n * width : (n + 1) * width]
        for g in range(4):
            proj = dot(w_s[g * tri_rows : (g + 1) * tri_rows], low)
            for k in range(4):
                gate = proj[(2 * k) * quarter : (2 * k + 1) * quarter]
                value = proj[(2 * k + 1) * quarter : (2 * k + 2) * quarter]
                kept = sigmoid(gate) * value * mask
                for n in range(group):
                    at = (first + n) * (chans + 1) + g * quarter
                    kept_s[ORDER[k]][pl.ds(at, quarter), :] = kept[:, n * width : (n + 1) * width]

    @pl.loop(0, chans, unroll=8)
    def _(h):
        for k in range(4):
            tri_ref[k, h] = kept_s[k][pl.ds(h, rows, stride=chans + 1), :].astype(bf16)

    for h in range(heads):
        bias_ref[h] = bs[pl.ds(h, rows, stride=heads), :]


def any_spec():
    return pl.BlockSpec(memory_space=pl.ANY)


def project(place, pieces, wall, mask_rows, gain, heads, rows, first_row, step_rows=16):
    _, quarter, width = pieces[0].shape
    chans = 4 * quarter
    start = first_row // step_rows
    row_spec = pl.BlockSpec((step_rows, chans, width), lambda i: (i, 0, 0))
    pair = in_hbm((rows, chans, width), bf16)
    return pl.pallas_call(
        project_kernel,
        grid=(rows // step_rows,),
        in_specs=[place_spec()]
        + [pl.BlockSpec((step_rows, quarter, width), lambda i: (i, 0, 0))] * 4
        + [whole_spec(wall), pl.BlockSpec((step_rows, width), lambda i: (i + start, 0)), whole_spec(gain)],
        out_specs=[
            pl.BlockSpec((4, chans, step_rows, width), lambda i: (0, 0, i, 0)),
            row_spec,
            row_spec,
            pl.BlockSpec((heads, step_rows, width), lambda i: (0, i, 0)),
        ],
        out_shape=[
            in_hbm((4, chans, rows, width), bf16),
            pair,
            pair,
            jax.ShapeDtypeStruct((heads, rows, width), f32),
        ],
        scratch_shapes=[
            pltpu.VMEM((4, step_rows, quarter, width), bf16),
            pltpu.VMEM((8 * chans, chans), bf16),
            pltpu.VMEM((64, chans), bf16),
            pltpu.VMEM((step_rows * heads, width), f32),
        ]
        + [pltpu.VMEM((step_rows * (chans + 8), width), f32)] * 4,
        compiler_params=params(40),
        cost_estimate=quick,
        name="project",
    )(place, *pieces, wall, mask_rows, gain)


def in_core_order(core, mine, far):
    first = core == 0
    blocks = [jnp.where(first, a, b) for a, b in zip(mine, far)]
    return jnp.concatenate(blocks + [jnp.where(first, b, a) for a, b in zip(mine, far)], axis=0)


def tri_forward_kernel(count, place_ref, *refs):
    core = place_ref[1]
    mine, far, out_ref = refs[:count], refs[count : 2 * count], refs[-1]
    rows = out_ref.shape[2]

    @pl.loop(0, out_ref.shape[1], unroll=4)
    def _(h):
        left = jnp.concatenate([t[OUT_LEFT, h] for t in mine], axis=0)
        right = in_core_order(core, [t[OUT_RIGHT, h] for t in mine], [t[OUT_RIGHT, h] for t in far])
        out_ref[0, h] = dot(left, right, 1, 1).astype(bf16)
        left = jnp.concatenate([t[IN_LEFT, h] for t in mine + far], axis=0)
        right = jnp.concatenate([t[IN_RIGHT, h] for t in mine + far], axis=0)
        both = dot(left, right, 0, 0)
        out_ref[1, h] = jnp.where(core == 0, both[:rows], both[rows:]).astype(bf16)


def tri_forward(place, mine, far, step_h=16):
    _, chans, rows, width = mine[0].shape
    rows = rows * len(mine)
    spec = pl.BlockSpec((4, step_h) + mine[0].shape[2:], lambda s: (0, s, 0, 0))
    far_spec = pl.BlockSpec((3, step_h) + mine[0].shape[2:], lambda s: (0, s, 0, 0))
    return pl.pallas_call(
        functools.partial(tri_forward_kernel, len(mine)),
        grid=(chans // step_h,),
        in_specs=[place_spec()] + [spec] * len(mine) + [far_spec] * len(mine),
        out_specs=pl.BlockSpec((2, step_h, rows, width), lambda s: (0, s, 0, 0)),
        out_shape=in_hbm((2, chans, rows, width), bf16),
        compiler_params=params(40),
        cost_estimate=quick,
        name="tri_forward",
    )(place, *held(mine), *far)


def middle_kernel(
    fresh, place_ref, tri_ref, pair_ref, norm_ref, c0, c1, c2, c3, gain_tri_ref, gain_trans_ref, wall_ref, rest_ref, prev_ref,
    p0, p1, p2, p3, mid_ref, gate_ref, gtri_ref, gw_out_ref,
    gw_ref, tri_s0, tri_s1, wg_s, wto_s, wti_s, wout_s, wout_t, wti_t, wto_t, gg_trans_s, gg_tri_s,
    cot_s, pc, po, tn0, tn1, nm, hid, gp, gb0, gb1, gs0, gs1,
):
    z = place_ref[0]
    step = pl.program_id(0)
    rows, chans, width = pair_ref.shape
    quarter = chans // 4
    cots, outs = (c0, c1, c2, c3), (p0, p1, p2, p3)
    tris, tns, gbs, gss = (tri_s0, tri_s1), (tn0, tn1), (gb0, gb1), (gs0, gs1)
    gains_at = 2 * quarter + 2 * chans

    @pl.when(step == 0)
    def _():
        for g in range(4):
            for d in range(2):
                wg_s[d * chans + g * quarter : d * chans + (g + 1) * quarter] = wall_ref[
                    lax.bitwise_xor(z, g), (8 + d) * quarter : (9 + d) * quarter
                ]
                wto_s[d, g * quarter : (g + 1) * quarter] = rest_ref[lax.bitwise_xor(z, g), d * quarter : (d + 1) * quarter]
            wti_s[g * chans : (g + 1) * chans] = rest_ref[lax.bitwise_xor(z, g), 2 * quarter : 2 * quarter + chans]
            wout_s[g * chans : (g + 1) * chans] = rest_ref[lax.bitwise_xor(z, g), 2 * quarter + chans : gains_at]
        for f in range(4):
            block = slice(f * chans, (f + 1) * chans)
            wout_t[:, block] = wout_s[block].astype(f32).T.astype(bf16)
            wti_t[:, block] = wti_s[block].astype(f32).T.astype(bf16)
        for d in range(2):
            wto_t[d] = wto_s[d].astype(f32).T.astype(bf16)
        gw_ref[...] = jnp.zeros_like(gw_ref) if fresh else prev_ref[...]
        gg_trans_s[...] = jnp.zeros_like(gg_trans_s)
        gg_tri_s[...] = jnp.zeros_like(gg_tri_s)

    @pl.loop(0, chans, unroll=8)
    def _(h):
        for d in range(2):
            tris[d][pl.ds(h * (rows + 1), rows), :] = tri_ref[d, h].astype(f32)

    gain_trans = jnp.concatenate([gain_trans_ref[...]] * group, axis=1)
    gain_tri = [jnp.concatenate([gain_tri_ref[d]] * group, axis=1) for d in range(2)]

    for m in range(4):
        pc[lax.bitwise_xor(z, m)] = cots[m][...]

    @pl.loop(0, rows // group)
    def _(s2):
        first = s2 * group
        lanes = pl.ds(pl.multiple_of(first * width, group * width), group * width)

        def wide(get):
            return jnp.concatenate([get(first + n) for n in range(group)], axis=1)

        def cut(value, n):
            return value[:, n * width : (n + 1) * width]

        inner = wide(lambda r: norm_ref[r])
        gate = sigmoid(dot(wg_s[...], inner))
        total = wide(lambda r: pair_ref[r]).astype(f32)
        kept = []
        for d in range(2):
            tri = wide(lambda r: tris[d][pl.ds(r, chans, stride=rows + 1), :])
            scaled, inverse = sub_norm(tri)
            low = (scaled * gain_tri[d]).astype(bf16)
            tns[d][:, lanes] = low
            branch = dot(wto_s[d], low)
            total = total + gate[d * chans : (d + 1) * chans] * branch
            kept.append((scaled, inverse, branch))
        scaled, inverse = sub_norm(total)
        low = (scaled * gain_trans).astype(bf16)
        nm[:, lanes] = low
        cot = wide(lambda r: jnp.concatenate([pc[q, r] for q in range(4)], axis=0))
        cot_s[:, lanes] = cot
        acts, backs = [], []
        for f in range(4):
            block = slice(f * chans, (f + 1) * chans)
            act, slope = gelu_both(dot(wti_s[block], low))
            acts.append(act.astype(bf16))
            backs.append((dot(wout_s[block], cot) * slope).astype(bf16))
            hid[block, lanes] = acts[-1]
            gp[block, lanes] = backs[-1]
        out = (total + dot(wout_t[...], jnp.concatenate(acts, axis=0))).astype(bf16)
        for n in range(group):
            for q in range(4):
                po[q, first + n] = cut(out[q * quarter : (q + 1) * quarter], n)
        back = dot(wti_t[...], jnp.concatenate(backs, axis=0))
        gg_trans_s[...] += back * scaled
        grad = cot.astype(f32) + sub_norm_back(gain_trans, scaled, inverse, back)
        for n in range(group):
            mid_ref[first + n] = cut(grad, n).astype(bf16)
        for d in range(2):
            scaled, inverse, branch = kept[d]
            sig = gate[d * chans : (d + 1) * chans]
            grad_branch = sig * grad
            grad_gate = (grad_branch * branch * (1.0 - sig)).astype(bf16)
            grad_branch = grad_branch.astype(bf16)
            for n in range(group):
                gate_ref[first + n, d * chans : (d + 1) * chans] = cut(grad_gate, n)
            gbs[d][:, lanes] = grad_branch
            back = dot(wto_t[d], grad_branch)
            gg_tri_s[d] += back * scaled
            out = sub_norm_back(gain_tri[d], scaled, inverse, back)
            for n in range(group):
                gss[d][pl.ds(first + n, chans, stride=rows + 1), :] = cut(out, n)

    for m in range(4):
        outs[m][...] = po[lax.bitwise_xor(z, m)]
    gw_out = dot(hid[...], cot_s[...], 1, 1)
    gw_in = dot(gp[...], nm[...], 1, 1)
    for g in range(4):
        at = 2 * quarter
        gw_ref[g, at : at + chans] += gw_in[g * chans : (g + 1) * chans]
        gw_ref[g, at + chans : at + 2 * chans] += gw_out[g * chans : (g + 1) * chans]
    for d in range(2):
        gw_tri = dot(gbs[d][...], tns[d][...], 1, 1)
        for g in range(4):
            gw_ref[g, d * quarter : (d + 1) * quarter] += gw_tri[g * quarter : (g + 1) * quarter]

        @pl.loop(0, chans, unroll=8)
        def _(h):
            gtri_ref[d, h] = gss[d][pl.ds(h * (rows + 1), rows), :].astype(bf16)

    @pl.when(step == pl.num_programs(0) - 1)
    def _():
        for n, total in enumerate((gg_trans_s[...], gg_tri_s[0], gg_tri_s[1])):
            row = lane_sums(total)
            for g in range(4):
                gw_ref[g, gains_at + n : gains_at + n + 1] += row
        gw_out_ref[...] = gw_ref[...].astype(gw_out_ref.dtype)


def middle(place, tri, first_row, pair, norm, cots, gain_tri, gain_trans, wall, rest, prev, step_rows=16):
    rows, chans, width = pair.shape
    hidden, quarter = 4 * chans, chans // 4
    fresh = prev is None
    sums = in_hbm((4, 2 * quarter + 2 * chans + 16, chans), f32 if fresh else bf16)
    start = first_row // step_rows
    row_spec = pl.BlockSpec((step_rows, chans, width), lambda s: (s, 0, 0))
    piece_spec = pl.BlockSpec((step_rows, quarter, width), lambda s: (s, 0, 0))
    piece = in_hbm((rows, quarter, width), bf16)
    gate = in_hbm((rows, 2 * chans, width), bf16)
    lanes = step_rows * width
    operands = [place, *held([tri, pair, norm]), *cots, gain_tri, gain_trans, wall, rest]
    operands.append(gain_tri if fresh else prev)
    return pl.pallas_call(
        functools.partial(middle_kernel, fresh),
        grid=(rows // step_rows,),
        in_specs=[place_spec(), pl.BlockSpec((2, chans, step_rows, width), lambda s: (0, 0, s + start, 0)), row_spec, row_spec]
        + [piece_spec] * 4
        + [whole_spec(a) for a in operands[8:]],
        out_specs=[piece_spec] * 4
        + [
            row_spec,
            pl.BlockSpec((step_rows, 2 * chans, width), lambda s: (s, 0, 0)),
            pl.BlockSpec((2, chans, step_rows, width), lambda s: (0, 0, s, 0)),
            whole_spec(sums),
        ],
        out_shape=[piece] * 4
        + [
            in_hbm((rows, chans, width), bf16),
            gate,
            jax.ShapeDtypeStruct((2, chans, rows, width), bf16),
            sums,
        ],
        scratch_shapes=[pltpu.VMEM(sums.shape, f32)]
        + [pltpu.VMEM((chans * (step_rows + 1), width), f32)] * 2
        + [pltpu.VMEM((2 * chans, chans), bf16), pltpu.VMEM((2, chans, chans), bf16)]
        + [pltpu.VMEM((hidden, chans), bf16)] * 2
        + [pltpu.VMEM((chans, hidden), bf16)] * 2
        + [
            pltpu.VMEM((2, chans, chans), bf16),
            pltpu.VMEM((chans, group * width), f32),
            pltpu.VMEM((2, chans, group * width), f32),
            pltpu.VMEM((chans, lanes), bf16),
            pltpu.VMEM((4, step_rows, quarter, width), bf16),
            pltpu.VMEM((4, step_rows, quarter, width), bf16),
        ]
        + [pltpu.VMEM((chans, lanes), bf16)] * 3
        + [pltpu.VMEM((hidden, lanes), bf16)] * 2
        + [pltpu.VMEM((chans, lanes), bf16)] * 2
        + [pltpu.VMEM((chans * (step_rows + 1), width), f32)] * 2,
        compiler_params=params(56),
        cost_estimate=quick,
        name="middle",
    )(*operands)


def tri_backward_kernel(count, place_ref, *refs):
    core = place_ref[1]
    mine, far, gmine, gfar = (refs[n * count : (n + 1) * count] for n in range(4))
    out_ref = refs[-1]
    rows = out_ref.shape[2]

    def joined(a, k, h):
        return jnp.concatenate([t[k, h] for t in a], axis=0)

    @pl.loop(0, out_ref.shape[1], unroll=4)
    def _(h):
        right = in_core_order(core, [t[OUT_RIGHT, h] for t in mine], [t[0, h] for t in far])
        out_ref[0, h] = dot(joined(gmine, 0, h), right).astype(bf16)
        left = jnp.concatenate([t[OUT_LEFT, h] for t in mine] + [t[1, h] for t in far], axis=0)
        both = dot(joined(gmine + gfar, 0, h), left, 0, 0)
        out_ref[1, h] = jnp.where(core == 0, both[:rows], both[rows:]).astype(bf16)
        grad = in_core_order(core, [t[1, h] for t in gmine], [t[1, h] for t in gfar])
        out_ref[2, h] = dot(joined(mine, IN_RIGHT, h), grad, 1, 1).astype(bf16)
        out_ref[3, h] = dot(joined(mine, IN_LEFT, h), grad).astype(bf16)


def tri_backward(place, mine, far, gmine, gfar, step_h=16):
    _, chans, rows, width = mine[0].shape
    total = rows * len(mine)
    spec = pl.BlockSpec((4, step_h, rows, width), lambda s: (0, s, 0, 0))
    far_spec = pl.BlockSpec((2, step_h, rows, width), lambda s: (1, s, 0, 0))
    gspec = pl.BlockSpec((2, step_h, rows, width), lambda s: (0, s, 0, 0))
    operands = [place, *held(mine), *held(far), *gmine, *gfar]
    return pl.pallas_call(
        functools.partial(tri_backward_kernel, len(mine)),
        grid=(chans // step_h,),
        in_specs=[place_spec()] + [spec] * len(mine) + [far_spec] * len(mine) + [gspec] * (2 * len(mine)),
        out_specs=pl.BlockSpec((4, step_h, total, width), lambda s: (0, s, 0, 0)),
        out_shape=in_hbm((4, chans, total, width), bf16),
        compiler_params=params(40),
        cost_estimate=quick,
        name="tri_backward",
    )(*operands)


def finish_kernel(
    i_steps, fresh, place_ref, sum_ref, pair_ref, norm_ref, mid_ref, gate_ref, score_ref, mask_ref, gain_ref, wall_ref, prev_ref, extra_ref,
    p0, p1, p2, p3, gw_out_ref,
    gw_ref, s0, s1, s2_, s3, wall_t, w_s, gall, nb, po, sc_s, gg_s,
):
    z = place_ref[0]
    step = pl.program_id(0)
    rows, chans, width = pair_ref.shape
    quarter = chans // 4
    sums, outs = (s0, s1, s2_, s3), (p0, p1, p2, p3)
    block_rows = wall_ref.shape[1]
    packed = 4 * block_rows
    heads = score_ref.shape[1]
    here = heads // 4

    @pl.when(step == 0)
    def _():
        for g in range(4):
            gall[g * block_rows : (g + 1) * block_rows, :chans] = wall_ref[lax.bitwise_xor(z, g)]
            w_s[g * 8 * quarter : (g + 1) * 8 * quarter] = wall_ref[lax.bitwise_xor(z, g), : 8 * quarter]
        for f in range(0, packed, 128):
            end = min(f + 128, packed)
            wall_t[:, f:end] = gall[f:end, :chans].astype(f32).T.astype(bf16)
        gw_ref[...] = jnp.zeros_like(gw_ref) if fresh else prev_ref[...]
        gg_s[...] = jnp.zeros_like(gg_s)
        sc_s[...] = jnp.zeros_like(sc_s)

    @pl.when(step < i_steps)
    def _():
        @pl.loop(0, chans, unroll=8)
        def _(h):
            for k in range(4):
                sums[k][pl.ds(h * (rows + 1), rows), :] = sum_ref[k, h].astype(f32)

        gain = jnp.concatenate([gain_ref[...]] * group, axis=1)

        @pl.loop(0, rows // group)
        def _(s2):
            first = s2 * group
            lanes = pl.ds(pl.multiple_of(first * width, group * width), group * width)

            def wide(get):
                return jnp.concatenate([get(first + n) for n in range(group)], axis=1)

            def cut(value, n):
                return value[:, n * width : (n + 1) * width]

            inner = wide(lambda r: norm_ref[r])
            nb[:, lanes] = inner
            mask = wide(lambda r: mask_ref[pl.ds(r, 1), :])
            parts = []
            for g in range(4):
                proj = dot(w_s[g * 8 * quarter : (g + 1) * 8 * quarter], inner)
                for k in range(4):
                    gate = proj[(2 * k) * quarter : (2 * k + 1) * quarter]
                    value = proj[(2 * k + 1) * quarter : (2 * k + 2) * quarter]
                    grad = wide(lambda r: sums[k][pl.ds(g * quarter * (rows + 1) + r, quarter, stride=rows + 1), :])
                    sig = sigmoid(gate)
                    back = grad * mask * sig
                    parts.append((back * value * (1.0 - sig)).astype(bf16))
                    parts.append(back.astype(bf16))
                for d in range(2):
                    at = d * chans + g * quarter
                    parts.append(wide(lambda r: gate_ref[r, at : at + quarter]))
                for n in range(group):
                    sc_s[g * 16 : g * 16 + here, n * width : (n + 1) * width] = score_ref[
                        first + n, g * here : (g + 1) * here
                    ]
                parts.append(sc_s[g * 16 : (g + 1) * 16].astype(bf16))
                parts.append(jnp.zeros((block_rows - 10 * quarter - 16, group * width), bf16))
            every = jnp.concatenate(parts, axis=0)
            gall[:, lanes] = every
            back = dot(wall_t[...], every)
            scaled, inverse = sub_norm(wide(lambda r: pair_ref[r]).astype(f32))
            gg_s[...] += back * scaled
            out = wide(lambda r: mid_ref[r]).astype(f32) + sub_norm_back(gain, scaled, inverse, back)
            out = out.astype(bf16)
            for n in range(group):
                for q in range(4):
                    po[q, first + n] = cut(out[q * quarter : (q + 1) * quarter], n)

        for m in range(4):
            outs[m][...] = po[lax.bitwise_xor(z, m)]
        gw_ref[...] += dot(gall[...], nb[...], 1, 1)

    @pl.when(step == i_steps - 1)
    def _():
        row = lane_sums(gg_s[...])
        for g in range(4):
            at = (g + 1) * block_rows - 1
            gw_ref[at : at + 1] += row
        gw_out_ref[...] = gw_ref[...].astype(gw_out_ref.dtype)

    @pl.when(step == i_steps)
    def _():
        for m in range(4):
            outs[m][: extra_ref.shape[1]] = extra_ref[m]


def finish(place, sums, first_row, pair, norm, mid, gate, scores, mask_rows, gain, wall, prev, extra, step_rows=16):
    rows, chans, width = pair.shape
    quarter = chans // 4
    heads = scores.shape[1]
    packed = 4 * wall.shape[1]
    i_steps = rows // step_rows
    fresh = prev is None
    start = first_row // step_rows
    last = first_row + rows == mask_rows.shape[0]
    total = in_hbm((packed, chans), bf16 if last else f32)

    def at(s):
        return jnp.minimum(s, i_steps - 1)

    if fresh:
        prev = gain
    row_spec = pl.BlockSpec((step_rows, chans, width), lambda s: (at(s), 0, 0))
    piece_spec = pl.BlockSpec((step_rows, quarter, width), lambda s: (s, 0, 0))
    piece = in_hbm((rows + (extra.shape[1] if last else 0), quarter, width), bf16)
    lanes = step_rows * width
    return pl.pallas_call(
        functools.partial(finish_kernel, i_steps, fresh),
        grid=(i_steps + (1 if last else 0),),
        in_specs=[place_spec(), pl.BlockSpec((4, chans, step_rows, width), lambda s: (0, 0, at(s) + start, 0))]
        + [row_spec] * 3
        + [
            pl.BlockSpec((step_rows, 2 * chans, width), lambda s: (at(s), 0, 0)),
            pl.BlockSpec((step_rows, heads, width), lambda s: (at(s) + start, 0, 0)),
            pl.BlockSpec((step_rows, width), lambda s: (at(s) + start, 0)),
        ]
        + [whole_spec(a) for a in (gain, wall, prev, extra)],
        out_specs=[piece_spec] * 4 + [whole_spec(total)],
        out_shape=[piece] * 4 + [total],
        scratch_shapes=[pltpu.VMEM((packed, chans), f32)]
        + [pltpu.VMEM((chans * (step_rows + 1), width), f32)] * 4
        + [
            pltpu.VMEM((chans, packed), bf16),
            pltpu.VMEM((8 * chans, chans), bf16),
            pltpu.VMEM((packed, lanes), bf16),
            pltpu.VMEM((chans, lanes), bf16),
            pltpu.VMEM((4, step_rows, quarter, width), bf16),
            pltpu.VMEM((64, group * width), f32),
            pltpu.VMEM((chans, group * width), f32),
        ],
        compiler_params=params(56),
        cost_estimate=quick,
        name="finish",
    )(place, *held([sums, pair, norm, mid, gate]), scores, mask_rows, gain, wall, prev, extra)


def assemble_kernel(rows, count, nodes, place_ref, *refs):
    pieces, (out_ref, *node_refs) = refs[: 4 * count], refs[4 * count : 4 * count + (3 if nodes else 1)]
    sems, z = refs[-1], place_ref[0]
    copies = []
    for m in range(4):
        crop = lax.bitwise_xor(z, m)
        for n in range(count):
            source, target = pieces[4 * n + m], out_ref.at[crop, pl.ds(n * rows, rows)]
            copies.append(pltpu.make_async_copy(source.at[pl.ds(0, rows)], target, sems.at[m, n]))
        if nodes:
            source = pieces[4 * (count - 1) + m].at[pl.ds(rows, 2)]
            copies.append(pltpu.make_async_copy(source, refs[-2].at[crop], sems.at[m, count]))
    for copy in copies:
        copy.start()
    for copy in copies:
        copy.wait()
    for n, ref in enumerate(node_refs):
        for crop in range(4):
            value = refs[-2][crop, n]
            half, width = value.shape[0], value.shape[1] // 2
            ref[crop, :half] = value[:, :width]
            ref[crop, half:] = value[:, width:]


def assemble(place, chunks, rows, nodes):
    _, quarter, width = chunks[0][0].shape
    count = len(chunks)
    vmem = pl.BlockSpec(memory_space=pltpu.VMEM)
    shapes = [jax.ShapeDtypeStruct((4, rows * count, quarter, width), bf16)]
    scratch = [pltpu.SemaphoreType.DMA((4, count + 1))]
    if nodes:
        shapes += [jax.ShapeDtypeStruct((4, 2 * quarter, width // 2), bf16)] * 2
        scratch = [pltpu.VMEM((4, 2, quarter, width), bf16)] + scratch
    return pl.pallas_call(
        functools.partial(assemble_kernel, rows, count, nodes),
        in_specs=[place_spec()] + [any_spec()] * (4 * count),
        out_specs=[any_spec()] + [vmem] * (len(shapes) - 1),
        out_shape=shapes,
        scratch_shapes=scratch,
        compiler_params=params(16),
        cost_estimate=quick,
        name="assemble",
    )(place, *[piece for chunk in chunks for piece in chunk])


def unpack_kernel(early, node_rows, place_ref, own, far, tri_in, gate, bias, tri_out, trans_in, trans_out, qkv, attn, node_in, node_out, gains, node_gains):
    first = place_ref[1] == 0
    own, far = own[...].astype(f32), far[...].astype(f32)
    a, b = jnp.where(first, own[:early], far[:early]), jnp.where(first, far[:early], own[:early])
    last = own[early:] + far[early:]
    quarter = tri_out.shape[1]
    chans = trans_in.shape[0]
    half = chans + quarter + 8
    wide = jnp.concatenate([a[:node_rows], b[:node_rows]], axis=1)
    rest = jnp.concatenate([a[node_rows : node_rows + half], b[node_rows : node_rows + half]], axis=0)
    for d in range(2):
        for n in range(4):
            at = (4 * d + n) * quarter
            tri_in[d, n] = last[at : at + quarter]
        gate[d] = last[(8 + d) * quarter : (9 + d) * quarter]
        tri_out[d] = rest[d * quarter : (d + 1) * quarter]
    bias[...] = last[10 * quarter : 10 * quarter + bias.shape[0]]
    at = 2 * quarter
    trans_in[...] = rest[at : at + chans].T
    trans_out[...] = rest[at + chans : at + 2 * chans]
    at = at + 2 * chans
    gains[...] = jnp.concatenate([last[last.shape[0] - 1 :], rest[at : at + 7]], axis=0)
    size = qkv.shape[1]
    for n in range(3):
        qkv[n] = wide[n * size : (n + 1) * size]
    at = 3 * size
    attn[...] = wide[at : at + size]
    at = at + size
    size = node_in.shape[0]
    node_in[...] = wide[at : at + size].T
    node_out[...] = wide[at + size : at + 2 * size]
    at = at + 2 * size
    node_gains[...] = wide[at : at + 8]


def unpack(place, own, far, early, node_rows, heads):
    chans = own.shape[1]
    quarter, nodes = chans // 4, 2 * chans
    shapes = [
        (2, 4, quarter, chans), (2, quarter, chans), (heads, chans), (2, quarter, chans), (chans, chans), (chans, chans),
        (3, nodes // 4, nodes), (nodes // 4, nodes), (nodes, nodes), (nodes, nodes), (8, chans), (8, nodes),
    ]
    vmem = pl.BlockSpec(memory_space=pltpu.VMEM)
    return pl.pallas_call(
        functools.partial(unpack_kernel, early, node_rows),
        in_specs=[place_spec()] + [vmem] * 2,
        out_specs=[vmem] * len(shapes),
        out_shape=[jax.ShapeDtypeStruct(shape, f32) for shape in shapes],
        compiler_params=params(32),
        cost_estimate=quick,
        name="unpack",
    )(place, own, far)


def node_kernel(place_ref, bias_ref, bias_far, live_ref, gain_ref, gain_mid_ref, near_w, far_w,
                sent_ref, score_ref, gw_ref, w_all, att, gqkv):
    z, core, x = place_ref[0], place_ref[1], place_ref[2]
    first = core == 0
    groups, packed, _ = gw_ref.shape
    half_rows = bias_ref.shape[1]
    length, nodes = 2 * half_rows, gain_ref.shape[1]
    quarter = nodes // groups
    fold = quarter // 2
    count = near_w.shape[1] // 2 - fold
    for m in range(groups):
        for ref, side in ((near_w, core), (far_w, 1 - core)):
            for at, other in ((0, x), (count, 1 - x)):
                here = pl.ds(pl.multiple_of((2 * side + other) * count, count), count)
                w_all[lax.bitwise_xor(z, m), here] = ref[m, at:at + count]
    heads = bias_ref.shape[0]
    head_dim = nodes // heads
    hidden = nodes
    scale = 1.0 / math.sqrt(head_dim)

    def weight(at, size):
        return jnp.concatenate(
            [jnp.concatenate([w_all[g, half * packed + at:half * packed + at + size] for half in range(2)], axis=1) for g in range(groups)], axis=0)

    def ordered(mine, far):
        return jnp.concatenate([jnp.where(first, mine, far), jnp.where(first, far, mine)], axis=0)

    def rows(value):
        return jnp.where(first, value[:half_rows], value[half_rows:])

    def parts(value):
        centered = value - jnp.mean(value, axis=1, keepdims=True)
        inverse = lax.rsqrt(jnp.mean(centered * centered, axis=1, keepdims=True) + epsilon)
        return centered * inverse, inverse

    def back(gain, scaled, inverse, grad):
        weighted = gain * grad
        first_mean = jnp.mean(weighted, axis=1, keepdims=True)
        second_mean = jnp.mean(weighted * scaled, axis=1, keepdims=True)
        return inverse * (weighted - first_mean - scaled * second_mean)

    def own_half(value):
        return jnp.where(first, value[:, :128], value[:, 128:]).astype(bf16)

    def keep(at, value):
        size = value.shape[0] // groups
        for g in range(groups):
            gw_ref[g, at:at + size] = own_half(value[g * size:(g + 1) * size])

    def gain_row(grad, scaled):
        return jnp.sum(grad * scaled, axis=0, keepdims=True)


    def unfolded(ref, n):
        rows_of = slice(2 * count + n * fold, 2 * count + (n + 1) * fold)
        parts = [ref[lax.bitwise_xor(z, g), rows_of].astype(f32) for g in range(groups)]
        half = parts[0].shape[1] // 2
        return jnp.concatenate([jnp.concatenate([v[:, :half], v[:, half:]], axis=0) for v in parts], axis=1)

    def sent(n, value):
        for g in range(groups):
            part = value[:, g * quarter:(g + 1) * quarter]
            half = part.shape[0] // 2
            sent_ref[lax.bitwise_xor(z, g), n] = jnp.concatenate([part[:half], part[half:]], axis=1).astype(bf16)

    node_in = ordered(unfolded(near_w, 0), unfolded(far_w, 0))
    cot = ordered(unfolded(near_w, 1), unfolded(far_w, 1)).astype(bf16)
    scaled_in, inverse_in = parts(node_in)
    low_in = (scaled_in * gain_ref[...]).astype(bf16)
    q, k, v = (dot(low_in, weight(g * quarter, quarter), 1, 1).astype(bf16) for g in range(3))
    lane = lax.broadcasted_iota(jnp.int32, (1, nodes), 1)
    key_live = live_ref[...] > 0.5

    def of_head(value, h):
        here = (lane >= h * head_dim) & (lane < (h + 1) * head_dim)
        return jnp.where(here, value, jnp.zeros_like(value))

    def probs_of(h):
        raw = dot(of_head(q, h), k, 1, 1) * scale + ordered(bias_ref[h], bias_far[h])
        scores = jnp.where(key_live, raw, -1e9)
        exps = jnp.exp(scores - jnp.max(scores, axis=1, keepdims=True))
        return exps / jnp.sum(exps, axis=1, keepdims=True)

    total = jnp.zeros((length, nodes), f32)
    for h in range(heads):
        probs = probs_of(h)
        att[h] = probs
        total = total + dot(probs.astype(bf16), of_head(v, h))
    attn = total.astype(bf16)
    at_a, at_i, at_o = 3 * quarter, 4 * quarter, 4 * quarter + hidden
    mid = node_in + dot(attn, weight(at_a, quarter), 1, 1)
    scaled_mid, inverse_mid = parts(mid)
    low_mid = (scaled_mid * gain_mid_ref[...]).astype(bf16)
    out = mid
    grad = jnp.zeros((length, nodes), f32)
    for g in range(groups):
        w_in = jnp.concatenate([w_all[g, half * packed + at_i:half * packed + at_i + hidden] for half in range(2)], axis=1)
        w_out = jnp.concatenate([w_all[g, half * packed + at_o:half * packed + at_o + hidden] for half in range(2)], axis=1)
        act, slope = gelu_both(dot(low_mid, w_in, 1, 1))
        act = act.astype(bf16)
        out = out + dot(act, w_out)
        grad_pre = (dot(cot, w_out, 1, 1) * slope).astype(bf16)
        grad = grad + dot(grad_pre, w_in)
        gi, go = dot(grad_pre, low_mid, 0, 0), dot(act, cot, 0, 0)
        gw_ref[g, at_i:at_i + hidden] = own_half(gi)
        gw_ref[g, at_o:at_o + hidden] = own_half(go)
    sent(0, rows(out))
    mid_row = gain_row(grad, scaled_mid)
    grad_mid = cot.astype(f32) + back(gain_mid_ref[...], scaled_mid, inverse_mid, grad)
    grad_low = grad_mid.astype(bf16)
    keep(at_a, dot(grad_low, attn, 0, 0))
    grad_attn = dot(grad_low, weight(at_a, quarter)).astype(bf16)
    for g in range(3):
        gqkv[g] = jnp.zeros((length, nodes), f32)
    for h in range(heads):
        probs = att[h]
        grad_probs = dot(of_head(grad_attn, h), v, 1, 1)
        delta = jnp.sum(probs * grad_probs, axis=1, keepdims=True)
        scores = probs * (grad_probs - delta)
        score_ref[:, h, :] = rows(scores)
        scores = scores.astype(bf16)
        gqkv[0] += dot(scores, of_head(k, h))
        gqkv[1] += dot(scores, of_head(q, h), 0, 0)
        gqkv[2] += dot(probs.astype(bf16), of_head(grad_attn, h), 0, 0)
    grad = jnp.zeros((length, nodes), f32)
    for g, factor in enumerate((scale, scale, 1.0)):
        low = (gqkv[g] * factor).astype(bf16)
        keep(g * quarter, dot(low, low_in, 0, 0))
        grad = grad + dot(low, weight(g * quarter, quarter))
    tail = jnp.concatenate([gain_row(grad, scaled_in), mid_row, jnp.zeros((14, nodes), f32)], axis=0)
    for g in range(groups):
        gw_ref[g, packed - 16:] = own_half(tail)
    sent(1, rows(grad_mid + back(gain_ref[...], scaled_in, inverse_in, grad)))

def node_track(place, bias, bias_far, live, gain, gain_mid, near_w, far_w, rows):
    half_rows, length = bias.shape[1], live.shape[1]
    nodes = gain.shape[1]
    heads = bias.shape[0]
    arrays = (bias, bias_far, live, gain, gain_mid, near_w, far_w)
    shapes = [
        jax.ShapeDtypeStruct((near_w.shape[0], 2, half_rows // 2, 128), bf16),
        jax.ShapeDtypeStruct((half_rows, heads, length), f32),
        jax.ShapeDtypeStruct((near_w.shape[0], rows, 128), bf16),
    ]
    vmem = pl.BlockSpec(memory_space=pltpu.VMEM)
    return pl.pallas_call(
        node_kernel,
        in_specs=[pl.BlockSpec(memory_space=pltpu.SMEM)] + [vmem] * len(arrays),
        out_specs=[vmem] * len(shapes),
        out_shape=shapes,
        scratch_shapes=[pltpu.VMEM((near_w.shape[0], 2 * near_w.shape[1], 128), bf16), pltpu.VMEM((heads, length, length), f32), pltpu.VMEM((3, length, nodes), f32)],
        compiler_params=params(40),
        cost_estimate=quick,
        name="node_track",
    )(place, *arrays)


def shards_by_crop(
    pair,
    node,
    pair_cot,
    node_cot,
    lengths,
    present,
    gain_pair,
    w_tri_in,
    w_out_gate,
    gain_tri,
    w_tri_out,
    gain_trans,
    w_trans_in,
    w_trans_out,
    w_bias,
    gain_node,
    w_qkv,
    w_attn_out,
    gain_node_trans,
    w_node_in,
    w_node_out,
):
    groups = lax.axis_size(CHAN)
    rows_here = pair.shape[1]
    chans = groups * pair.shape[2]
    crop_len = pair.shape[3]
    nodes = groups * node.shape[2]
    heads = groups * w_bias.shape[1]
    quarter, node_quarter = chans // groups, nodes // groups
    z = lax.axis_index(CHAN)
    core = lax.axis_index(DP) % 2
    x = lax.axis_index(ROWS)
    y = lax.axis_index(DP) // 2
    place = jnp.stack([z, core, x, y]).astype(jnp.int32)
    mesh_shape = (lax.axis_size(DP), lax.axis_size(ROWS), groups)

    def device(d, r, c):
        return (d * mesh_shape[1] + r) * groups + c

    def home_perm(m):
        return [
            (device(d, r, c), device(d - d % 2 + r, d % 2, c ^ m))
            for d in range(mesh_shape[0])
            for r in range(mesh_shape[1])
            for c in range(groups)
        ]

    core_pairs = [(d, d ^ 1) for d in range(mesh_shape[0])]
    row_pairs = [(0, 1), (1, 0)]

    def send_home(pieces):
        return [
            lax.ppermute(piece, (DP, ROWS, CHAN), home_perm(m))
            for m, piece in enumerate(pieces)
        ]

    def to_chan(value, m):
        return lax.ppermute(value, CHAN, [(c, c ^ m) for c in range(groups)])

    def swap_core(value):
        return lax.ppermute(value, DP, core_pairs)

    def pick(value, index):
        return lax.dynamic_index_in_dim(value, index, 0, keepdims=False)

    def own_rows(value, axis):
        return lax.dynamic_slice_in_dim(value, core * rows_here, rows_here, axis)

    def packed(parts):
        return jnp.concatenate([part.reshape(-1, chans) for part in parts])

    def split(value):
        return jnp.concatenate([value[:, :chans], value[:, chans:]])

    chunk = min(32, rows_here)
    tied = lax.optimization_barrier

    def blocks(rows):
        rows = jnp.pad(rows, ((0, -rows.shape[0] % (4 * quarter)), (0, 0)))
        return rows.reshape(-1, quarter, chans)

    def with_far(own, far, side):
        return jnp.concatenate([jnp.where(side == 0, own, far), jnp.where(side == 0, far, own)], axis=1)

    def swap_rows(value):
        return lax.ppermute(value, ROWS, row_pairs)

    node_rest = jnp.concatenate(
        [w_qkv.transpose(0, 2, 1).reshape(-1, nodes), w_attn_out.T, w_node_in.T, w_node_out]
    )
    node_rest = jnp.pad(node_rest, ((0, 16), (0, 0)))
    first_rows, pair_rows, node_rows = 10 * quarter + 32, 2 * quarter + 2 * chans, node_rest.shape[0]

    def tiles(values):
        return jnp.broadcast_to(values[..., None], values.shape + (chans,))

    gains = [tiles(values) for values in (gain_pair, gain_tri, gain_trans)]
    sent = pack(
        place,
        pair,
        0,
        chunk,
        first=[
            lengths,
            present,
            node,
            node_cot,
            w_tri_in.transpose(0, 1, 3, 2).reshape(-1, chans),
            w_out_gate.transpose(0, 2, 1).reshape(-1, chans),
            w_bias.T,
            w_tri_out.transpose(0, 2, 1).reshape(-1, chans),
            w_trans_in,
            w_trans_out,
        ],
    )
    sent, pair, pair_cot = tied((sent, pair, pair_cot))
    pieces0 = send_home(sent)
    sent = pack(place, pair, chunk, chunk)
    sent_cots = pack(place, pair_cot, 0, chunk)
    sent_later = pack(place, pair_cot, chunk, chunk, blocks(split(node_rest)))
    sent, sent_cots, sent_later, gains, pieces0 = tied((sent, sent_cots, sent_later, gains, pieces0))
    pieces1 = send_home(sent)
    node_own = jnp.stack([piece[chunk + 1 : chunk + 3] for piece in pieces0])
    weights = jnp.stack([piece[chunk + 3 :] for piece in pieces0]).reshape(groups, -1, chans)
    weights = with_far(weights, swap_core(weights), core)
    wall, rest = weights[:, :first_rows], weights[:, first_rows : first_rows + pair_rows]
    gain, gains_mid = gains[0], gains[1:]
    live = pieces0[0][chunk, 0].astype(jnp.float32)
    mask_rows = own_rows(live, 0)[:, None] * live[None, :]
    tri0, norm0, pair0, bias0 = project(place, pieces0, wall, mask_rows, gain, heads, chunk, 0)
    tri0, pieces1, rest = tied((tri0, pieces1, rest))
    far0 = swap_core(tri0)
    tri1, norm1, pair1, bias1 = project(place, pieces1, wall, mask_rows, gain, heads, chunk, chunk)
    tri1, far0, sent = tied((tri1, far0, sent_cots))
    far1 = swap_core(tri1)
    cots0 = send_home(sent)
    bias = jnp.concatenate([bias0, bias1], axis=1)
    bias, far1 = tied((bias, far1))
    bias_far = swap_core(bias)
    tri = tri_forward(place, (tri0, tri1), (far0, far1))
    sent, bias_far, cots0, tri = tied((sent_later, bias_far, cots0, tri))
    cots1 = send_home(sent)
    norms, pairs = (norm0, norm1), (pair0, pair1)

    core_round, row_round = (core, DP, core_pairs), (x, ROWS, row_pairs)
    y_round = (y, DP, [(d, d ^ 2) for d in range(mesh_shape[0])])

    def halve(value, side, axis, pairs, at=1):
        low, high = jnp.split(value, 2, at)
        far = lax.ppermute(jnp.where(side == 0, high, low).astype(jnp.bfloat16), axis, pairs)
        return jnp.where(side == 0, low, high).astype(jnp.float32), far

    def added(kept, far):
        return (kept + far).astype(jnp.bfloat16)

    def both(value, far, side):
        return jnp.concatenate([jnp.where(side == 0, value, far), jnp.where(side == 0, far, value)])

    def run_middle(n, cots, prev):
        return middle(
            place, tri, n * chunk, pairs[n], norms[n], cots, *gains_mid, wall, rest, prev
        )

    *out0, mid0, gate0, gtri0, gw_rest = run_middle(0, cots0, None)
    out0, gtri0, cots1 = tied((out0, gtri0, cots1))
    out0 = send_home(out0)
    node_rest = jnp.stack([cot[chunk:] for cot in cots1]).reshape(groups, -1, chans)
    node_rest = jnp.concatenate(
        [node_rest, swap_rows(node_rest), node_own.reshape(groups, -1, chans)], axis=1
    )
    *out1, mid1, gate1, gtri1, gw_rest = run_middle(1, cots1, gw_rest)
    gtri0, gtri1, out0, node_rest = tied((gtri0, gtri1, out0, node_rest))
    node_rest_far = swap_core(node_rest)
    rest_half = added(*halve(gw_rest, *core_round))
    gtri0, gtri1, node_rest_far, rest_half = tied((gtri0, gtri1, node_rest_far, rest_half))
    gtris = (gtri0, gtri1)
    gtris_far = [swap_core(gtri) for gtri in gtris]
    mids, gates = (mid0, mid1), (gate0, gate1)

    node_sent, scores, gw_node = node_track(
        place,
        bias,
        bias_far,
        live[None, :],
        gain_node[None, :],
        gain_node_trans[None, :],
        node_rest,
        node_rest_far,
        node_rows,
    )
    early = [gw_node, rest_half]
    early_rows = sum(part.shape[1] for part in early)
    early.append(jnp.zeros((groups, -early_rows % 64, chans), jnp.bfloat16))
    early = jnp.concatenate(early, axis=1)
    out1, gtris_far = tied((out1, gtris_far))
    out1 = send_home(out1)
    kept, far = halve(early, *row_round)
    sums = tri_backward(place, (tri0, tri1), (far0, far1), gtris, gtris_far)

    def run_finish(n, prev):
        return finish(
            place, sums, n * chunk, pairs[n], norms[n], mids[n], gates[n], scores, mask_rows, gain, wall, prev, node_sent
        )

    sums, kept, far = tied((sums, kept, far))
    kept, far = halve(added(kept, far), *y_round)
    *grad0, gw_first = run_finish(0, None)
    grad0, out1, kept, far = tied((grad0, out1, kept, far))
    grad0 = send_home(grad0)
    *grad1, gw_first = run_finish(1, gw_first)
    grad1, gw_first, grad0 = tied((grad1, gw_first, grad0))
    grad1 = send_home(grad1)
    early = added(kept, far)
    shard = early.shape[1]
    low = jnp.concatenate([early, gw_first.reshape(groups, -1, chans)], axis=1)
    total = pick(low, z).astype(jnp.float32)
    for m in range(1, groups):
        total = total + to_chan(pick(low, z ^ m), m)
    total = total.astype(jnp.bfloat16)
    total, out0, out1 = tied((total, out0, out1))
    early, late = total[:shard], total[shard:]
    for side, axis, pairs in (y_round, row_round):
        far = lax.ppermute(jnp.concatenate([early, late]), axis, pairs)
        if axis != ROWS:
            grad1, far = tied((grad1, far))
        late = added(late.astype(jnp.float32), far[early.shape[0] :])
        early = both(early, far[: early.shape[0]], side)
    own = jnp.concatenate([early, late])
    far = swap_core(own)
    tri_in, out_gate, bias_w, tri_out, trans_in, trans_out, qkv, attn, node_in, node_out, gain_rows, node_gains = unpack(
        place, own, far, early.shape[0], node_rows, w_bias.shape[1]
    )
    def xassemble(chunks):
        rows = [jnp.concatenate([c[m][:chunk] for c in chunks]) for m in range(groups)]
        stacked = jnp.stack(rows)
        return jnp.stack([pick(stacked, z ^ k) for k in range(groups)])

    pair_out = xassemble((out0, out1))
    pair_grad, node_result, node_grad = assemble(place, (grad0, grad1), chunk, True)

    def own_block(row, size):
        return lax.dynamic_slice_in_dim(row, z * size, size, row.ndim - 1)

    gain_rows, node_gains = own_block(gain_rows, quarter), own_block(node_gains, node_quarter)
    return (
        pair_out,
        node_result,
        pair_grad,
        node_grad,
        gain_rows[0],
        tri_in.transpose(0, 1, 3, 2),
        out_gate.transpose(0, 2, 1),
        gain_rows[2:4],
        tri_out.transpose(0, 2, 1),
        gain_rows[1],
        trans_in,
        trans_out,
        bias_w.T,
        node_gains[0],
        qkv.transpose(0, 2, 1),
        attn.T,
        node_gains[1],
        node_in,
        node_out,
    )


def solution(mesh):
    in_specs = (
        P(DP, ROWS, CHAN, None),
        P(DP, ROWS, CHAN),
        P(DP, ROWS, CHAN, None),
        P(DP, ROWS, CHAN),
        P(DP),
        P(DP, None),
        P(),
        P(None, None, None, CHAN),
        P(None, None, CHAN),
        P(),
        P(None, None, CHAN),
        P(),
        P(None, CHAN),
        P(CHAN, None),
        P(None, CHAN),
        P(),
        P(None, None, CHAN),
        P(None, CHAN),
        P(),
        P(None, CHAN),
        P(CHAN, None),
    )
    out_specs = (
        P(DP, ROWS, CHAN, None),
        P(DP, ROWS, CHAN),
        P(DP, ROWS, CHAN, None),
        P(DP, ROWS, CHAN),
        P(CHAN),
        P(None, None, None, CHAN),
        P(None, None, CHAN),
        P(None, CHAN),
        P(None, None, CHAN),
        P(CHAN),
        P(None, CHAN),
        P(CHAN, None),
        P(None, CHAN),
        P(CHAN),
        P(None, None, CHAN),
        P(None, CHAN),
        P(CHAN),
        P(None, CHAN),
        P(CHAN, None),
    )
    sizes = dict(mesh.shape)
    by_crop = sizes[ROWS] == 2 and sizes[DP] == 4 and sizes[CHAN] == 4
    body = shards_by_crop if by_crop else shards
    return jax.shard_map(body, mesh=mesh, in_specs=in_specs, out_specs=out_specs, check_vma=False)
```

```python
import functools
import math

import jax
import jax.numpy as jnp
from jax import lax
from jax.experimental import pallas as pl
from jax.experimental.pallas import tpu as pltpu
from jax.sharding import PartitionSpec as P

f32, bf16 = jnp.float32, jnp.bfloat16
epsilon = 1e-05
DP, ROWS, CHAN = "dp", "rows", "chan"
masked_score = -1000000000.0


def norm_parts(full):
    mean = jnp.mean(full, axis=2, keepdims=True)
    centered = full - mean
    variance = jnp.mean(centered * centered, axis=2, keepdims=True)
    inverse = lax.rsqrt(variance + epsilon)
    return (centered * inverse, inverse)


def shaped(gain, full):
    return gain.reshape(gain.shape + (1,) * (full.ndim - 3))


def normed(full, gain):
    scaled, inverse = norm_parts(full)
    return scaled * shaped(gain, full)


def stat_terms(full, gain, partial_value, groups):
    scaled, inverse = norm_parts(full)
    weighted = shaped(gain, full) * partial_value
    first_sum = jnp.sum(weighted, axis=2)
    second_sum = jnp.sum(weighted * scaled, axis=2)
    stacked = jnp.stack([first_sum, second_sum], axis=2)
    repeats = (1, 1, groups) + (1,) * (full.ndim - 3)
    return jnp.tile(stacked, repeats)


def norm_finish(full, gain, grad_here, totals, chan_index):
    width = full.shape[2]
    here = grad_here.shape[2]
    scaled, inverse = norm_parts(full)
    scaled_here = lax.dynamic_slice_in_dim(scaled, chan_index * here, here, 2)
    gain_here = lax.dynamic_slice_in_dim(gain, chan_index * here, here, 0)
    first_mean = totals[:, :, 0:1] / width
    second_mean = totals[:, :, 1:2] / width
    grad_input = inverse * (
        shaped(gain_here, full) * grad_here - first_mean - scaled_here * second_mean
    )
    summed_axes = (0, 1) + tuple(range(3, full.ndim))
    grad_gain = jnp.sum(grad_here * scaled_here, axis=summed_axes)
    return (grad_input, grad_gain)


def gelu_exact(value):
    return jax.nn.gelu(value, approximate=False)


def softmax_rows(scores):
    top = jnp.max(scores, axis=-1, keepdims=True)
    exps = jnp.exp(scores - top)
    return exps / jnp.sum(exps, axis=-1, keepdims=True)


def shards(
    pair,
    node,
    pair_cot,
    node_cot,
    lengths,
    present,
    gain_pair,
    w_tri_in,
    w_out_gate,
    gain_tri,
    w_tri_out,
    gain_trans,
    w_trans_in,
    w_trans_out,
    w_bias,
    gain_node,
    w_qkv,
    w_attn_out,
    gain_node_trans,
    w_node_in,
    w_node_out,
):
    batch = pair.shape[0]
    rows_here = pair.shape[1]
    crop_len = pair.shape[3]
    groups = lax.axis_size(CHAN)
    chan_index = lax.axis_index(CHAN)
    row_start = lax.axis_index(ROWS) * rows_here
    heads_here = w_bias.shape[1]
    head_dim = w_qkv.shape[2] // heads_here
    scale = 1.0 / math.sqrt(head_dim)
    positions = jnp.arange(crop_len, dtype=jnp.int32)
    mask_all = present.astype(jnp.float32) * (positions[None, :] < lengths[:, None]).astype(
        jnp.float32
    )
    mask_rows = lax.dynamic_slice_in_dim(mask_all, row_start, rows_here, 1)
    pair_mask = mask_rows[:, :, None, None] * mask_all[:, None, None, :]
    key_live = mask_all[:, None, None, :] > 0.5

    def gating(gate, value):
        return jax.nn.sigmoid(gate) * value * pair_mask

    pair_whole, node_whole = (
        lax.all_gather(pair, CHAN, axis=2, tiled=True),
        lax.all_gather(node, CHAN, axis=2, tiled=True),
    )
    full_in = pair_whole.astype(jnp.float32)
    node_full = node_whole.astype(jnp.float32)
    stream_in = pair.astype(jnp.float32)
    node_in = node.astype(jnp.float32)
    normed_in = normed(full_in, gain_pair).astype(jnp.bfloat16)
    projected = jnp.einsum(
        "bicj,dgch->dgbihj", normed_in, w_tri_in, preferred_element_type=jnp.float32
    )
    gate_pre = jnp.einsum(
        "bicj,dcx->dbixj", normed_in, w_out_gate, preferred_element_type=jnp.float32
    )
    bias = jnp.einsum("bicj,ch->bhij", normed_in, w_bias, preferred_element_type=jnp.float32)
    left_out = gating(projected[0, 0], projected[0, 1]).astype(jnp.bfloat16)
    right_out = gating(projected[0, 2], projected[0, 3]).astype(jnp.bfloat16)
    left_in = gating(projected[1, 0], projected[1, 1]).astype(jnp.bfloat16)
    right_in = gating(projected[1, 2], projected[1, 3]).astype(jnp.bfloat16)
    normed_node = normed(node_full, gain_node).astype(jnp.bfloat16)
    qkv = jnp.einsum(
        "bin,gna->gbia", normed_node, w_qkv, preferred_element_type=jnp.float32
    ).astype(jnp.bfloat16)
    whole_right_out, whole_right_in, whole_keys, whole_values = (
        lax.all_gather(right_out, ROWS, axis=1, tiled=True),
        lax.all_gather(right_in, ROWS, axis=1, tiled=True),
        lax.all_gather(qkv[1], ROWS, axis=1, tiled=True),
        lax.all_gather(qkv[2], ROWS, axis=1, tiled=True),
    )
    left_cols = lax.all_to_all(left_in, ROWS, split_axis=3, concat_axis=1, tiled=True)
    queries = qkv[0].reshape(batch, rows_here, heads_here, head_dim)
    keys = whole_keys.reshape(batch, crop_len, heads_here, head_dim)
    values = whole_values.reshape(batch, crop_len, heads_here, head_dim)
    raw = (
        jnp.einsum("bihd,bjhd->bhij", queries, keys, preferred_element_type=jnp.float32) * scale
        + bias
    )
    probs = softmax_rows(jnp.where(key_live, raw, masked_score))
    probs_low = probs.astype(jnp.bfloat16)
    attn = jnp.einsum(
        "bhij,bjhd->bihd", probs_low, values, preferred_element_type=jnp.float32
    ).astype(jnp.bfloat16)
    attn = attn.reshape(batch, rows_here, heads_here * head_dim)
    tri_out = jnp.einsum(
        "bihk,bjhk->bihj", left_out, whole_right_out, preferred_element_type=jnp.float32
    )
    tri_in = jnp.einsum(
        "bkhi,bkhj->bihj", left_cols, whole_right_in, preferred_element_type=jnp.float32
    )
    tri_full_out, tri_full_in, attn_whole = (
        lax.all_gather(tri_out.astype(jnp.bfloat16), CHAN, axis=2, tiled=True).astype(
            tri_out.dtype
        ),
        lax.all_gather(tri_in.astype(jnp.bfloat16), CHAN, axis=2, tiled=True).astype(
            tri_in.dtype
        ),
        lax.all_gather(
            attn.astype(jnp.float32).astype(jnp.bfloat16), CHAN, axis=2, tiled=True
        ).astype(jnp.float32),
    )
    normed_out = normed(tri_full_out, gain_tri[0]).astype(jnp.bfloat16)
    normed_inc = normed(tri_full_in, gain_tri[1]).astype(jnp.bfloat16)
    branch_out = jnp.einsum(
        "bihj,hc->bicj", normed_out, w_tri_out[0], preferred_element_type=jnp.float32
    )
    branch_inc = jnp.einsum(
        "bihj,hc->bicj", normed_inc, w_tri_out[1], preferred_element_type=jnp.float32
    )
    gate_sig = jax.nn.sigmoid(gate_pre)
    stream_mid = stream_in + gate_sig[0] * branch_out + gate_sig[1] * branch_inc
    attn_low = attn_whole.astype(jnp.bfloat16)
    node_mid = node_in + jnp.einsum(
        "bia,an->bin", attn_low, w_attn_out, preferred_element_type=jnp.float32
    )
    full_mid, node_full_mid = (
        lax.all_gather(stream_mid.astype(jnp.bfloat16), CHAN, axis=2, tiled=True).astype(
            stream_mid.dtype
        ),
        lax.all_gather(node_mid.astype(jnp.bfloat16), CHAN, axis=2, tiled=True).astype(
            node_mid.dtype
        ),
    )
    normed_mid = normed(full_mid, gain_trans).astype(jnp.bfloat16)
    pre_hidden = jnp.einsum(
        "bicj,cf->bifj", normed_mid, w_trans_in, preferred_element_type=jnp.float32
    )
    hidden, gelu_pull = jax.vjp(gelu_exact, pre_hidden)
    hidden_low = hidden.astype(jnp.bfloat16)
    out_terms = jnp.einsum(
        "bifj,fc->bicj", hidden_low, w_trans_out, preferred_element_type=jnp.float32
    )
    normed_node_mid = normed(node_full_mid, gain_node_trans).astype(jnp.bfloat16)
    node_pre = jnp.einsum(
        "bin,nf->bif", normed_node_mid, w_node_in, preferred_element_type=jnp.float32
    )
    node_hidden, node_gelu_pull = jax.vjp(gelu_exact, node_pre)
    node_hidden_low = node_hidden.astype(jnp.bfloat16)
    node_terms = jnp.einsum(
        "bif,fn->bin", node_hidden_low, w_node_out, preferred_element_type=jnp.float32
    )
    pair_sum, node_sum = (
        lax.psum_scatter(
            out_terms.astype(jnp.bfloat16), CHAN, scatter_dimension=2, tiled=True
        ).astype(jnp.float32),
        lax.psum_scatter(
            node_terms.astype(jnp.bfloat16), CHAN, scatter_dimension=2, tiled=True
        ).astype(jnp.float32),
    )
    stream_out = stream_mid + pair_sum
    node_out = node_mid + node_sum
    cot_full, node_cot_full = (
        lax.all_gather(pair_cot, CHAN, axis=2, tiled=True),
        lax.all_gather(node_cot, CHAN, axis=2, tiled=True),
    )
    grad_trans_out = jnp.einsum(
        "bifj,bicj->fc", hidden_low, cot_full, preferred_element_type=jnp.float32
    )
    grad_hidden = jnp.einsum(
        "bicj,fc->bifj", cot_full, w_trans_out, preferred_element_type=jnp.float32
    )
    grad_pre = gelu_pull(grad_hidden)[0].astype(jnp.bfloat16)
    grad_trans_in = jnp.einsum(
        "bicj,bifj->cf", normed_mid, grad_pre, preferred_element_type=jnp.float32
    )
    grad_normed_mid = jnp.einsum(
        "bifj,cf->bicj", grad_pre, w_trans_in, preferred_element_type=jnp.float32
    )
    mid_terms = stat_terms(full_mid, gain_trans, grad_normed_mid, groups)
    grad_node_out_w = jnp.einsum(
        "bif,bin->fn", node_hidden_low, node_cot_full, preferred_element_type=jnp.float32
    )
    grad_node_hidden = jnp.einsum(
        "bin,fn->bif", node_cot_full, w_node_out, preferred_element_type=jnp.float32
    )
    grad_node_pre = node_gelu_pull(grad_node_hidden)[0].astype(jnp.bfloat16)
    grad_node_in_w = jnp.einsum(
        "bin,bif->nf", normed_node_mid, grad_node_pre, preferred_element_type=jnp.float32
    )
    grad_normed_node_mid = jnp.einsum(
        "bif,nf->bin", grad_node_pre, w_node_in, preferred_element_type=jnp.float32
    )
    node_mid_terms = stat_terms(node_full_mid, gain_node_trans, grad_normed_node_mid, groups)
    mid_here, mid_totals, node_mid_here, node_mid_totals = (
        lax.psum_scatter(
            grad_normed_mid.astype(jnp.bfloat16), CHAN, scatter_dimension=2, tiled=True
        ).astype(jnp.float32),
        lax.psum_scatter(
            mid_terms.astype(jnp.bfloat16), CHAN, scatter_dimension=2, tiled=True
        ).astype(jnp.float32),
        lax.psum_scatter(
            grad_normed_node_mid.astype(jnp.bfloat16), CHAN, scatter_dimension=2, tiled=True
        ).astype(jnp.float32),
        lax.psum_scatter(
            node_mid_terms.astype(jnp.bfloat16), CHAN, scatter_dimension=2, tiled=True
        ).astype(jnp.float32),
    )
    mid_extra, grad_gain_trans = norm_finish(full_mid, gain_trans, mid_here, mid_totals, chan_index)
    node_mid_extra, grad_gain_node_trans = norm_finish(
        node_full_mid, gain_node_trans, node_mid_here, node_mid_totals, chan_index
    )
    grad_mid = pair_cot.astype(jnp.float32) + mid_extra
    grad_node_mid = node_cot.astype(jnp.float32) + node_mid_extra
    branches = jnp.stack([branch_out, branch_inc])
    grad_branch = (gate_sig * grad_mid[None]).astype(jnp.bfloat16)
    grad_gate = (grad_mid[None] * branches * gate_sig * (1.0 - gate_sig)).astype(jnp.bfloat16)
    tri_normed_both = jnp.stack([normed_out, normed_inc])
    grad_w_tri_out = jnp.einsum(
        "dbihj,dbicj->dhc", tri_normed_both, grad_branch, preferred_element_type=jnp.float32
    )
    grad_out_gate = jnp.einsum(
        "bicj,dbixj->dcx", normed_in, grad_gate, preferred_element_type=jnp.float32
    )
    grad_tri_normed = jnp.einsum(
        "dbicj,dhc->dbihj", grad_branch, w_tri_out, preferred_element_type=jnp.float32
    )
    out_stats = stat_terms(tri_full_out, gain_tri[0], grad_tri_normed[0], groups)
    inc_stats = stat_terms(tri_full_in, gain_tri[1], grad_tri_normed[1], groups)
    grad_attn_branch = grad_node_mid.astype(jnp.bfloat16)
    grad_w_attn_out = jnp.einsum(
        "bia,bin->an", attn_low, grad_attn_branch, preferred_element_type=jnp.float32
    )
    attn_terms = jnp.einsum(
        "bin,an->bia", grad_attn_branch, w_attn_out, preferred_element_type=jnp.float32
    )
    out_here, out_totals, inc_here, inc_totals, attn_here = (
        lax.psum_scatter(
            grad_tri_normed[0].astype(jnp.bfloat16), CHAN, scatter_dimension=2, tiled=True
        ).astype(jnp.float32),
        lax.psum_scatter(
            out_stats.astype(jnp.bfloat16), CHAN, scatter_dimension=2, tiled=True
        ).astype(jnp.float32),
        lax.psum_scatter(
            grad_tri_normed[1].astype(jnp.bfloat16), CHAN, scatter_dimension=2, tiled=True
        ).astype(jnp.float32),
        lax.psum_scatter(
            inc_stats.astype(jnp.bfloat16), CHAN, scatter_dimension=2, tiled=True
        ).astype(jnp.float32),
        lax.psum_scatter(
            attn_terms.astype(jnp.bfloat16), CHAN, scatter_dimension=2, tiled=True
        ).astype(jnp.float32),
    )
    grad_tri_a, gain_grad_out = norm_finish(
        tri_full_out, gain_tri[0], out_here, out_totals, chan_index
    )
    grad_tri_b, gain_grad_inc = norm_finish(
        tri_full_in, gain_tri[1], inc_here, inc_totals, chan_index
    )
    grad_gain_tri = jnp.stack([gain_grad_out, gain_grad_inc])
    grad_out_low = grad_tri_a.astype(jnp.bfloat16)
    grad_inc_low = grad_tri_b.astype(jnp.bfloat16)
    grad_attn = attn_here.astype(jnp.bfloat16).reshape(batch, rows_here, heads_here, head_dim)
    grad_probs = jnp.einsum(
        "bihd,bjhd->bhij", grad_attn, values, preferred_element_type=jnp.float32
    )
    delta = jnp.sum(probs * grad_probs, axis=3, keepdims=True)
    grad_scores = (probs * (grad_probs - delta)).astype(jnp.bfloat16)
    grad_queries = (
        jnp.einsum("bhij,bjhd->bihd", grad_scores, keys, preferred_element_type=jnp.float32) * scale
    )
    key_terms = (
        jnp.einsum("bhij,bihd->bjhd", grad_scores, queries, preferred_element_type=jnp.float32)
        * scale
    )
    value_terms = jnp.einsum(
        "bhij,bihd->bjhd", probs_low, grad_attn, preferred_element_type=jnp.float32
    )
    grad_w_bias = jnp.einsum(
        "bicj,bhij->ch", normed_in, grad_scores, preferred_element_type=jnp.float32
    )
    bias_back = jnp.einsum("bhij,ch->bicj", grad_scores, w_bias, preferred_element_type=jnp.float32)
    grad_left_out = jnp.einsum(
        "bihj,bjhk->bihk", grad_out_low, whole_right_out, preferred_element_type=jnp.float32
    )
    right_terms = jnp.einsum(
        "bihj,bihk->bjhk", grad_out_low, left_out, preferred_element_type=jnp.float32
    )
    grad_right_out, key_grads, value_grads = (
        lax.psum_scatter(
            right_terms.astype(jnp.bfloat16), ROWS, scatter_dimension=1, tiled=True
        ).astype(jnp.float32),
        lax.psum_scatter(
            key_terms.astype(jnp.bfloat16), ROWS, scatter_dimension=1, tiled=True
        ).astype(jnp.float32),
        lax.psum_scatter(
            value_terms.astype(jnp.bfloat16), ROWS, scatter_dimension=1, tiled=True
        ).astype(jnp.float32),
    )
    whole_grad_in = lax.all_gather(grad_inc_low, ROWS, axis=1, tiled=True)
    grad_left_in = jnp.einsum(
        "bihj,bkhj->bkhi", whole_grad_in, right_in, preferred_element_type=jnp.float32
    )
    grad_right_in = jnp.einsum(
        "bkhi,bihj->bkhj", left_in, whole_grad_in, preferred_element_type=jnp.float32
    )

    def gate_back(first, second, grad):
        kept_value, pull = jax.vjp(gating, first, second)
        return pull(grad)

    left_gate_out, left_value_out = gate_back(projected[0, 0], projected[0, 1], grad_left_out)
    right_gate_out, right_value_out = gate_back(projected[0, 2], projected[0, 3], grad_right_out)
    left_gate_in, left_value_in = gate_back(projected[1, 0], projected[1, 1], grad_left_in)
    right_gate_in, right_value_in = gate_back(projected[1, 2], projected[1, 3], grad_right_in)
    grad_proj = jnp.stack(
        [
            jnp.stack([left_gate_out, left_value_out, right_gate_out, right_value_out]),
            jnp.stack([left_gate_in, left_value_in, right_gate_in, right_value_in]),
        ]
    ).astype(jnp.bfloat16)
    grad_tri_in_w = jnp.einsum(
        "bicj,dgbihj->dgch", normed_in, grad_proj, preferred_element_type=jnp.float32
    )
    grad_normed_in = jnp.einsum(
        "dgbihj,dgch->bicj", grad_proj, w_tri_in, preferred_element_type=jnp.float32
    )
    grad_normed_in = grad_normed_in + jnp.einsum(
        "dbixj,dcx->bicj", grad_gate, w_out_gate, preferred_element_type=jnp.float32
    )
    grad_normed_in = grad_normed_in + bias_back
    grad_qkv = jnp.stack(
        [
            grad_queries.reshape(batch, rows_here, heads_here * head_dim),
            key_grads.reshape(batch, rows_here, heads_here * head_dim),
            value_grads.reshape(batch, rows_here, heads_here * head_dim),
        ]
    ).astype(jnp.bfloat16)
    grad_w_qkv = jnp.einsum(
        "bin,gbia->gna", normed_node, grad_qkv, preferred_element_type=jnp.float32
    )
    grad_normed_node = jnp.einsum(
        "gbia,gna->bin", grad_qkv, w_qkv, preferred_element_type=jnp.float32
    )
    in_terms = stat_terms(full_in, gain_pair, grad_normed_in, groups)
    node_in_terms = stat_terms(node_full, gain_node, grad_normed_node, groups)
    in_here, in_totals, node_in_here, node_in_totals = (
        lax.psum_scatter(
            grad_normed_in.astype(jnp.bfloat16), CHAN, scatter_dimension=2, tiled=True
        ).astype(jnp.float32),
        lax.psum_scatter(
            in_terms.astype(jnp.bfloat16), CHAN, scatter_dimension=2, tiled=True
        ).astype(jnp.float32),
        lax.psum_scatter(
            grad_normed_node.astype(jnp.bfloat16), CHAN, scatter_dimension=2, tiled=True
        ).astype(jnp.float32),
        lax.psum_scatter(
            node_in_terms.astype(jnp.bfloat16), CHAN, scatter_dimension=2, tiled=True
        ).astype(jnp.float32),
    )
    in_extra, grad_gain_pair = norm_finish(full_in, gain_pair, in_here, in_totals, chan_index)
    node_in_extra, grad_gain_node = norm_finish(
        node_full, gain_node, node_in_here, node_in_totals, chan_index
    )
    grad_stream = grad_mid + in_extra
    node_grad = grad_node_mid + node_in_extra
    summed = lax.psum(
        (
            grad_gain_pair,
            grad_tri_in_w,
            grad_out_gate,
            grad_gain_tri,
            grad_w_tri_out,
            grad_gain_trans,
            grad_trans_in,
            grad_trans_out,
            grad_w_bias,
            grad_gain_node,
            grad_w_qkv,
            grad_w_attn_out,
            grad_gain_node_trans,
            grad_node_in_w,
            grad_node_out_w,
        ),
        (DP, ROWS),
    )
    return (
        stream_out.astype(jnp.bfloat16),
        node_out.astype(jnp.bfloat16),
        grad_stream.astype(jnp.bfloat16),
        node_grad.astype(jnp.bfloat16),
        summed[0],
        summed[1],
        summed[2],
        summed[3],
        summed[4],
        summed[5],
        summed[6],
        summed[7],
        summed[8],
        summed[9],
        summed[10],
        summed[11],
        summed[12],
        summed[13],
        summed[14],
    )


ORDER = (3, 2, 0, 1)
IN_LEFT, IN_RIGHT, OUT_RIGHT, OUT_LEFT = range(4)

group = 16


def dot(a, b, ca=1, cb=0):
    return lax.dot_general(a, b, (((ca,), (cb,)), ((), ())), preferred_element_type=f32)


def sigmoid(v):
    return 0.5 * jnp.tanh(0.5 * v) + 0.5


def sub_norm(full):
    mean = jnp.mean(full, axis=0, keepdims=True)
    centered = full - mean
    inverse = lax.rsqrt(jnp.mean(centered * centered, axis=0, keepdims=True) + epsilon)
    return centered * inverse, inverse


def sub_norm_back(gain, scaled, inverse, grad):
    weighted = gain * grad
    first = jnp.mean(weighted, axis=0, keepdims=True)
    second = jnp.mean(weighted * scaled, axis=0, keepdims=True)
    return inverse * (weighted - first - scaled * second)


def gelu_both(value):
    cdf = 0.5 * (1.0 + lax.erf(value * (0.5**0.5)))
    density = jnp.exp(-0.5 * value * value) * (1.0 / math.sqrt(2.0 * math.pi))
    return value * cdf, cdf + value * density


def lane_sums(value):
    value = sum(value[:, at : at + 128] for at in range(0, value.shape[1], 128))
    ones = jnp.ones((8, value.shape[1]), f32)
    sums = lax.dot_general(
        ones,
        value,
        (((1,), (1,)), ((), ())),
        precision=lax.Precision.HIGHEST,
        preferred_element_type=f32,
    )
    return sums[:1]


def place_spec():
    return pl.BlockSpec(memory_space=pltpu.SMEM)


def whole_spec(a):
    zeros = (0,) * len(a.shape)
    return pl.BlockSpec(a.shape, lambda s: zeros)


def in_hbm(shape, dtype):
    return pltpu.HBM(shape, dtype)


def held(arrays):
    return [pltpu.with_memory_space_constraint(a, pltpu.HBM) for a in arrays]


def params(mib):
    return pltpu.CompilerParams(vmem_limit_bytes=mib * 2**20)


quick = pl.CostEstimate(flops=1, bytes_accessed=1, transcendentals=0)


def pack_kernel(first_row, rows, live_rows, place_ref, *refs):
    z, part = place_ref[0], 2 * place_ref[2] + place_ref[1]
    sems = refs[-1]
    outs = refs[-7:-3] if live_rows else refs[-5:-1]
    more = outs[0].shape[0] - rows
    copies = []
    for m in range(4):
        rows_of = refs[0].at[lax.bitwise_xor(z, m), pl.ds(first_row, rows)]
        copies.append(pltpu.make_async_copy(rows_of, outs[m].at[pl.ds(0, rows)], sems.at[m]))
    if more and not live_rows:
        for m in range(4):
            rows_of = refs[1].at[pl.ds(part * more, more)]
            copies.append(pltpu.make_async_copy(rows_of, outs[m].at[pl.ds(rows, more)], sems.at[4 + m]))
    for copy in copies:
        copy.start()
    if live_rows:
        lengths, present, node, node_cot, tri_in, gate, bias, tri_out, trans_in, trans_out = refs[1:11]
        extra, weights = refs[-3:-1]
        quarter, width = extra.shape[2:]
        position = lax.broadcasted_iota(jnp.int32, (1, width), 1)
        for crop in range(4):
            for n, ref in enumerate((node, node_cot)):
                value = ref[crop].astype(f32)
                extra[crop, 1 + n] = jnp.concatenate([value[:quarter], value[quarter:]], axis=1).astype(bf16)
            there = jnp.where(position < lengths[crop], present[crop : crop + 1], 0).astype(f32)
            extra[crop, 0] = jnp.broadcast_to(there, (quarter, width)).astype(bf16)
        parts = [tri_in[...], gate[...]]
        low = bias[...].astype(f32)
        parts.append(jnp.concatenate([low, jnp.zeros((32 - low.shape[0], width), f32)], axis=0).astype(bf16))
        parts += [tri_out[...], trans_in[...].astype(f32).T.astype(bf16), trans_out[...]]
        count = sum(part.shape[0] for part in parts)
        parts.append(jnp.zeros((quarter * weights.shape[0] - count, width), bf16))
        weights[...] = jnp.concatenate(parts, axis=0).reshape(weights.shape)
        for m in range(4):
            outs[m][rows : rows + 3] = extra[lax.bitwise_xor(z, m)]
            outs[m][rows + 3 :] = weights[pl.ds(place_ref[2] * (more - 3), more - 3)]
    for copy in copies:
        copy.wait()


def pack(place, source, first_row, rows, weights=None, first=None):
    _, _, quarter, width = source.shape
    vmem = pl.BlockSpec(memory_space=pltpu.VMEM)
    operands, specs, scratch, more = [place, *held([source])], [place_spec(), any_spec()], [], 0
    if first is not None:
        count = sum(a.shape[0] for a in first[4:]) + 32 - first[6].shape[0]
        count = -(-count // (2 * quarter)) * 2
        operands += first[:1] + held(first[1:])
        specs += [place_spec()] + [vmem] * (len(first) - 1)
        scratch = [pltpu.VMEM((4, 3, quarter, width), bf16), pltpu.VMEM((count, quarter, width), bf16)]
        more = 3 + count // 2
    elif weights is not None:
        operands += held([weights])
        specs.append(any_spec())
        more = weights.shape[0] // 4
    return pl.pallas_call(
        functools.partial(pack_kernel, first_row, rows, first is not None),
        in_specs=specs,
        out_specs=[vmem] * 4,
        out_shape=[in_hbm((rows + more, quarter, width), bf16)] * 4,
        scratch_shapes=scratch + [pltpu.SemaphoreType.DMA((8,))],
        compiler_params=params(24),
        cost_estimate=quick,
        name="pack",
    )(*operands)


def project_kernel(
    place_ref, p0, p1, p2, p3, wall_ref, mask_ref, gain_ref, tri_ref, norm_ref, pair_ref, bias_ref, pc, w_s, wb_s, bs, *kept_s
):
    pieces = (p0, p1, p2, p3)
    rows, quarter, width = p0.shape
    chans = 4 * quarter
    z = place_ref[0]
    gain = jnp.concatenate([gain_ref[...]] * group, axis=1)
    heads = bias_ref.shape[0]
    tri_rows = 8 * quarter

    @pl.when(pl.program_id(0) == 0)
    def _():
        for g in range(4):
            w_s[g * tri_rows : (g + 1) * tri_rows] = wall_ref[lax.bitwise_xor(z, g), :tri_rows]
            wb_s[g * 16 : (g + 1) * 16] = wall_ref[lax.bitwise_xor(z, g), 10 * quarter : 10 * quarter + 16]

    for m in range(4):
        pc[lax.bitwise_xor(z, m)] = pieces[m][...]

    @pl.loop(0, rows // group)
    def _(step):
        first = step * group

        def wide(get):
            return jnp.concatenate([get(first + n) for n in range(group)], axis=1)

        rows_in = [jnp.concatenate([pc[q, first + n] for q in range(4)], axis=0) for n in range(group)]
        for n in range(group):
            pair_ref[first + n] = rows_in[n]
        scaled, _ = sub_norm(jnp.concatenate(rows_in, axis=1).astype(f32))
        low = (scaled * gain).astype(bf16)
        for n in range(group):
            norm_ref[first + n] = low[:, n * width : (n + 1) * width]
        mask = wide(lambda r: mask_ref[pl.ds(r, 1), :])
        bias = dot(wb_s[...], low)
        for n in range(group):
            for g in range(4):
                at = (first + n) * heads + g * (heads // 4)
                bs[pl.ds(at, heads // 4), :] = bias[g * 16 : g * 16 + heads // 4, n * width : (n + 1) * width]
        for g in range(4):
            proj = dot(w_s[g * tri_rows : (g + 1) * tri_rows], low)
            for k in range(4):
                gate = proj[(2 * k) * quarter : (2 * k + 1) * quarter]
                value = proj[(2 * k + 1) * quarter : (2 * k + 2) * quarter]
                kept = sigmoid(gate) * value * mask
                for n in range(group):
                    at = (first + n) * (chans + 1) + g * quarter
                    kept_s[ORDER[k]][pl.ds(at, quarter), :] = kept[:, n * width : (n + 1) * width]

    @pl.loop(0, chans, unroll=32)
    def _(h):
        for k in range(4):
            tri_ref[k, h] = kept_s[k][pl.ds(h, rows, stride=chans + 1), :].astype(bf16)

    for h in range(heads):
        bias_ref[h] = bs[pl.ds(h, rows, stride=heads), :]


def any_spec():
    return pl.BlockSpec(memory_space=pl.ANY)


def project(place, pieces, wall, mask_rows, gain, heads, rows, first_row, step_rows=16):
    _, quarter, width = pieces[0].shape
    chans = 4 * quarter
    start = first_row // step_rows
    row_spec = pl.BlockSpec((step_rows, chans, width), lambda i: (i, 0, 0))
    pair = in_hbm((rows, chans, width), bf16)
    return pl.pallas_call(
        project_kernel,
        grid=(rows // step_rows,),
        in_specs=[place_spec()]
        + [pl.BlockSpec((step_rows, quarter, width), lambda i: (i, 0, 0))] * 4
        + [whole_spec(wall), pl.BlockSpec((step_rows, width), lambda i: (i + start, 0)), whole_spec(gain)],
        out_specs=[
            pl.BlockSpec((4, chans, step_rows, width), lambda i: (0, 0, i, 0)),
            row_spec,
            row_spec,
            pl.BlockSpec((heads, step_rows, width), lambda i: (0, i, 0)),
        ],
        out_shape=[
            in_hbm((4, chans, rows, width), bf16),
            pair,
            pair,
            jax.ShapeDtypeStruct((heads, rows, width), f32),
        ],
        scratch_shapes=[
            pltpu.VMEM((4, step_rows, quarter, width), bf16),
            pltpu.VMEM((8 * chans, chans), bf16),
            pltpu.VMEM((64, chans), bf16),
            pltpu.VMEM((step_rows * heads, width), f32),
        ]
        + [pltpu.VMEM((step_rows * (chans + 8), width), f32)] * 4,
        compiler_params=params(40),
        cost_estimate=quick,
        name="project",
    )(place, *pieces, wall, mask_rows, gain)


def in_core_order(core, mine, far):
    first = core == 0
    blocks = [jnp.where(first, a, b) for a, b in zip(mine, far)]
    return jnp.concatenate(blocks + [jnp.where(first, b, a) for a, b in zip(mine, far)], axis=0)


def tri_forward_kernel(count, place_ref, *refs):
    core = place_ref[1]
    mine, far, out_ref = refs[:count], refs[count : 2 * count], refs[-1]
    rows = out_ref.shape[2]

    @pl.loop(0, out_ref.shape[1], unroll=32)
    def _(h):
        left = jnp.concatenate([t[OUT_LEFT, h] for t in mine], axis=0)
        right = in_core_order(core, [t[OUT_RIGHT, h] for t in mine], [t[OUT_RIGHT, h] for t in far])
        out_ref[0, h] = dot(left, right, 1, 1).astype(bf16)
        left = jnp.concatenate([t[IN_LEFT, h] for t in mine + far], axis=0)
        right = jnp.concatenate([t[IN_RIGHT, h] for t in mine + far], axis=0)
        both = dot(left, right, 0, 0)
        out_ref[1, h] = jnp.where(core == 0, both[:rows], both[rows:]).astype(bf16)


def tri_forward(place, mine, far, step_h=32):
    _, chans, rows, width = mine[0].shape
    rows = rows * len(mine)
    spec = pl.BlockSpec((4, step_h) + mine[0].shape[2:], lambda s: (0, s, 0, 0))
    far_spec = pl.BlockSpec((3, step_h) + mine[0].shape[2:], lambda s: (0, s, 0, 0))
    return pl.pallas_call(
        functools.partial(tri_forward_kernel, len(mine)),
        grid=(chans // step_h,),
        in_specs=[place_spec()] + [spec] * len(mine) + [far_spec] * len(mine),
        out_specs=pl.BlockSpec((2, step_h, rows, width), lambda s: (0, s, 0, 0)),
        out_shape=in_hbm((2, chans, rows, width), bf16),
        compiler_params=params(40),
        cost_estimate=quick,
        name="tri_forward",
    )(place, *held(mine), *far)


def middle_kernel(
    fresh, place_ref, tri_ref, pair_ref, norm_ref, c0, c1, c2, c3, gain_tri_ref, gain_trans_ref, wall_ref, rest_ref, prev_ref,
    p0, p1, p2, p3, mid_ref, gate_ref, gtri_ref, gw_out_ref,
    gw_ref, tri_s0, tri_s1, wg_s, wto_s, wti_s, wout_s, wout_t, wti_t, wto_t, gg_trans_s, gg_tri_s,
    cot_s, pc, po, tn0, tn1, nm, hid, gp, gb0, gb1, gs0, gs1,
):
    z = place_ref[0]
    step = pl.program_id(0)
    rows, chans, width = pair_ref.shape
    quarter = chans // 4
    cots, outs = (c0, c1, c2, c3), (p0, p1, p2, p3)
    tris, tns, gbs, gss = (tri_s0, tri_s1), (tn0, tn1), (gb0, gb1), (gs0, gs1)
    gains_at = 2 * quarter + 2 * chans

    @pl.when(step == 0)
    def _():
        for g in range(4):
            for d in range(2):
                wg_s[d * chans + g * quarter : d * chans + (g + 1) * quarter] = wall_ref[
                    lax.bitwise_xor(z, g), (8 + d) * quarter : (9 + d) * quarter
                ]
                wto_s[d, g * quarter : (g + 1) * quarter] = rest_ref[lax.bitwise_xor(z, g), d * quarter : (d + 1) * quarter]
            wti_s[g * chans : (g + 1) * chans] = rest_ref[lax.bitwise_xor(z, g), 2 * quarter : 2 * quarter + chans]
            wout_s[g * chans : (g + 1) * chans] = rest_ref[lax.bitwise_xor(z, g), 2 * quarter + chans : gains_at]
        for f in range(4):
            block = slice(f * chans, (f + 1) * chans)
            wout_t[:, block] = wout_s[block].astype(f32).T.astype(bf16)
            wti_t[:, block] = wti_s[block].astype(f32).T.astype(bf16)
        for d in range(2):
            wto_t[d] = wto_s[d].astype(f32).T.astype(bf16)
        gw_ref[...] = jnp.zeros_like(gw_ref) if fresh else prev_ref[...]
        gg_trans_s[...] = jnp.zeros_like(gg_trans_s)
        gg_tri_s[...] = jnp.zeros_like(gg_tri_s)

    @pl.loop(0, chans, unroll=32)
    def _(h):
        for d in range(2):
            tris[d][pl.ds(h * (rows + 1), rows), :] = tri_ref[d, h].astype(f32)

    gain_trans = jnp.concatenate([gain_trans_ref[...]] * group, axis=1)
    gain_tri = [jnp.concatenate([gain_tri_ref[d]] * group, axis=1) for d in range(2)]

    for m in range(4):
        pc[lax.bitwise_xor(z, m)] = cots[m][...]

    @pl.loop(0, rows // group)
    def _(s2):
        first = s2 * group
        lanes = pl.ds(pl.multiple_of(first * width, group * width), group * width)

        def wide(get):
            return jnp.concatenate([get(first + n) for n in range(group)], axis=1)

        def cut(value, n):
            return value[:, n * width : (n + 1) * width]

        inner = wide(lambda r: norm_ref[r])
        gate = sigmoid(dot(wg_s[...], inner))
        total = wide(lambda r: pair_ref[r]).astype(f32)
        kept = []
        for d in range(2):
            tri = wide(lambda r: tris[d][pl.ds(r, chans, stride=rows + 1), :])
            scaled, inverse = sub_norm(tri)
            low = (scaled * gain_tri[d]).astype(bf16)
            tns[d][:, lanes] = low
            branch = dot(wto_s[d], low)
            total = total + gate[d * chans : (d + 1) * chans] * branch
            kept.append((scaled, inverse, branch))
        scaled, inverse = sub_norm(total)
        low = (scaled * gain_trans).astype(bf16)
        nm[:, lanes] = low
        cot = wide(lambda r: jnp.concatenate([pc[q, r] for q in range(4)], axis=0))
        cot_s[:, lanes] = cot
        acts, backs = [], []
        for f in range(4):
            block = slice(f * chans, (f + 1) * chans)
            act, slope = gelu_both(dot(wti_s[block], low))
            acts.append(act.astype(bf16))
            backs.append((dot(wout_s[block], cot) * slope).astype(bf16))
            hid[block, lanes] = acts[-1]
            gp[block, lanes] = backs[-1]
        out = (total + dot(wout_t[...], jnp.concatenate(acts, axis=0))).astype(bf16)
        for n in range(group):
            for q in range(4):
                po[q, first + n] = cut(out[q * quarter : (q + 1) * quarter], n)
        back = dot(wti_t[...], jnp.concatenate(backs, axis=0))
        gg_trans_s[...] += back * scaled
        grad = cot.astype(f32) + sub_norm_back(gain_trans, scaled, inverse, back)
        for n in range(group):
            mid_ref[first + n] = cut(grad, n).astype(bf16)
        for d in range(2):
            scaled, inverse, branch = kept[d]
            sig = gate[d * chans : (d + 1) * chans]
            grad_branch = sig * grad
            grad_gate = (grad_branch * branch * (1.0 - sig)).astype(bf16)
            grad_branch = grad_branch.astype(bf16)
            for n in range(group):
                gate_ref[first + n, d * chans : (d + 1) * chans] = cut(grad_gate, n)
            gbs[d][:, lanes] = grad_branch
            back = dot(wto_t[d], grad_branch)
            gg_tri_s[d] += back * scaled
            out = sub_norm_back(gain_tri[d], scaled, inverse, back)
            for n in range(group):
                gss[d][pl.ds(first + n, chans, stride=rows + 1), :] = cut(out, n)

    for m in range(4):
        outs[m][...] = po[lax.bitwise_xor(z, m)]
    gw_out = dot(hid[...], cot_s[...], 1, 1)
    gw_in = dot(gp[...], nm[...], 1, 1)
    for g in range(4):
        at = 2 * quarter
        gw_ref[g, at : at + chans] += gw_in[g * chans : (g + 1) * chans]
        gw_ref[g, at + chans : at + 2 * chans] += gw_out[g * chans : (g + 1) * chans]
    for d in range(2):
        gw_tri = dot(gbs[d][...], tns[d][...], 1, 1)
        for g in range(4):
            gw_ref[g, d * quarter : (d + 1) * quarter] += gw_tri[g * quarter : (g + 1) * quarter]

        @pl.loop(0, chans, unroll=32)
        def _(h):
            gtri_ref[d, h] = gss[d][pl.ds(h * (rows + 1), rows), :].astype(bf16)

    @pl.when(step == pl.num_programs(0) - 1)
    def _():
        for n, total in enumerate((gg_trans_s[...], gg_tri_s[0], gg_tri_s[1])):
            row = lane_sums(total)
            for g in range(4):
                gw_ref[g, gains_at + n : gains_at + n + 1] += row
        gw_out_ref[...] = gw_ref[...].astype(gw_out_ref.dtype)


def middle(place, tri, first_row, pair, norm, cots, gain_tri, gain_trans, wall, rest, prev, step_rows=16):
    rows, chans, width = pair.shape
    hidden, quarter = 4 * chans, chans // 4
    fresh = prev is None
    sums = in_hbm((4, 2 * quarter + 2 * chans + 16, chans), f32 if fresh else bf16)
    start = first_row // step_rows
    row_spec = pl.BlockSpec((step_rows, chans, width), lambda s: (s, 0, 0))
    piece_spec = pl.BlockSpec((step_rows, quarter, width), lambda s: (s, 0, 0))
    piece = in_hbm((rows, quarter, width), bf16)
    gate = in_hbm((rows, 2 * chans, width), bf16)
    lanes = step_rows * width
    operands = [place, *held([tri, pair, norm]), *cots, gain_tri, gain_trans, wall, rest]
    operands.append(gain_tri if fresh else prev)
    return pl.pallas_call(
        functools.partial(middle_kernel, fresh),
        grid=(rows // step_rows,),
        in_specs=[place_spec(), pl.BlockSpec((2, chans, step_rows, width), lambda s: (0, 0, s + start, 0)), row_spec, row_spec]
        + [piece_spec] * 4
        + [whole_spec(a) for a in operands[8:]],
        out_specs=[piece_spec] * 4
        + [
            row_spec,
            pl.BlockSpec((step_rows, 2 * chans, width), lambda s: (s, 0, 0)),
            pl.BlockSpec((2, chans, step_rows, width), lambda s: (0, 0, s, 0)),
            whole_spec(sums),
        ],
        out_shape=[piece] * 4
        + [
            in_hbm((rows, chans, width), bf16),
            gate,
            jax.ShapeDtypeStruct((2, chans, rows, width), bf16),
            sums,
        ],
        scratch_shapes=[pltpu.VMEM(sums.shape, f32)]
        + [pltpu.VMEM((chans * (step_rows + 1), width), f32)] * 2
        + [pltpu.VMEM((2 * chans, chans), bf16), pltpu.VMEM((2, chans, chans), bf16)]
        + [pltpu.VMEM((hidden, chans), bf16)] * 2
        + [pltpu.VMEM((chans, hidden), bf16)] * 2
        + [
            pltpu.VMEM((2, chans, chans), bf16),
            pltpu.VMEM((chans, group * width), f32),
            pltpu.VMEM((2, chans, group * width), f32),
            pltpu.VMEM((chans, lanes), bf16),
            pltpu.VMEM((4, step_rows, quarter, width), bf16),
            pltpu.VMEM((4, step_rows, quarter, width), bf16),
        ]
        + [pltpu.VMEM((chans, lanes), bf16)] * 3
        + [pltpu.VMEM((hidden, lanes), bf16)] * 2
        + [pltpu.VMEM((chans, lanes), bf16)] * 2
        + [pltpu.VMEM((chans * (step_rows + 1), width), f32)] * 2,
        compiler_params=params(56),
        cost_estimate=quick,
        name="middle",
    )(*operands)


def tri_backward_kernel(count, place_ref, *refs):
    core = place_ref[1]
    mine, far, gmine, gfar = (refs[n * count : (n + 1) * count] for n in range(4))
    out_ref = refs[-1]
    rows = out_ref.shape[2]

    def joined(a, k, h):
        return jnp.concatenate([t[k, h] for t in a], axis=0)

    @pl.loop(0, out_ref.shape[1], unroll=32)
    def _(h):
        right = in_core_order(core, [t[OUT_RIGHT, h] for t in mine], [t[0, h] for t in far])
        out_ref[0, h] = dot(joined(gmine, 0, h), right).astype(bf16)
        left = jnp.concatenate([t[OUT_LEFT, h] for t in mine] + [t[1, h] for t in far], axis=0)
        both = dot(joined(gmine + gfar, 0, h), left, 0, 0)
        out_ref[1, h] = jnp.where(core == 0, both[:rows], both[rows:]).astype(bf16)
        grad = in_core_order(core, [t[1, h] for t in gmine], [t[1, h] for t in gfar])
        out_ref[2, h] = dot(joined(mine, IN_RIGHT, h), grad, 1, 1).astype(bf16)
        out_ref[3, h] = dot(joined(mine, IN_LEFT, h), grad).astype(bf16)


def tri_backward(place, mine, far, gmine, gfar, step_h=32):
    _, chans, rows, width = mine[0].shape
    total = rows * len(mine)
    spec = pl.BlockSpec((4, step_h, rows, width), lambda s: (0, s, 0, 0))
    far_spec = pl.BlockSpec((2, step_h, rows, width), lambda s: (1, s, 0, 0))
    gspec = pl.BlockSpec((2, step_h, rows, width), lambda s: (0, s, 0, 0))
    operands = [place, *held(mine), *held(far), *held(gmine), *gfar]
    return pl.pallas_call(
        functools.partial(tri_backward_kernel, len(mine)),
        grid=(chans // step_h,),
        in_specs=[place_spec()] + [spec] * len(mine) + [far_spec] * len(mine) + [gspec] * (2 * len(mine)),
        out_specs=pl.BlockSpec((4, step_h, total, width), lambda s: (0, s, 0, 0)),
        out_shape=in_hbm((4, chans, total, width), bf16),
        compiler_params=params(40),
        cost_estimate=quick,
        name="tri_backward",
    )(*operands)


def finish_kernel(
    i_steps, fresh, place_ref, sum_ref, pair_ref, norm_ref, mid_ref, gate_ref, score_ref, mask_ref, gain_ref, wall_ref, prev_ref, extra_ref,
    p0, p1, p2, p3, gw_out_ref,
    gw_ref, s0, s1, s2_, s3, wall_t, w_s, gall, nb, po, sc_s, gg_s,
):
    z = place_ref[0]
    step = pl.program_id(0)
    rows, chans, width = pair_ref.shape
    quarter = chans // 4
    sums, outs = (s0, s1, s2_, s3), (p0, p1, p2, p3)
    block_rows = wall_ref.shape[1]
    packed = 4 * block_rows
    heads = score_ref.shape[1]
    here = heads // 4

    @pl.when(step == 0)
    def _():
        for g in range(4):
            gall[g * block_rows : (g + 1) * block_rows, :chans] = wall_ref[lax.bitwise_xor(z, g)]
            w_s[g * 8 * quarter : (g + 1) * 8 * quarter] = wall_ref[lax.bitwise_xor(z, g), : 8 * quarter]
        for f in range(0, packed, 128):
            end = min(f + 128, packed)
            wall_t[:, f:end] = gall[f:end, :chans].astype(f32).T.astype(bf16)
        gw_ref[...] = jnp.zeros_like(gw_ref) if fresh else prev_ref[...]
        gg_s[...] = jnp.zeros_like(gg_s)
        sc_s[...] = jnp.zeros_like(sc_s)

    @pl.when(step < i_steps)
    def _():
        @pl.loop(0, chans, unroll=32)
        def _(h):
            for k in range(4):
                sums[k][pl.ds(h * (rows + 1), rows), :] = sum_ref[k, h].astype(f32)

        gain = jnp.concatenate([gain_ref[...]] * group, axis=1)

        @pl.loop(0, rows // group)
        def _(s2):
            first = s2 * group
            lanes = pl.ds(pl.multiple_of(first * width, group * width), group * width)

            def wide(get):
                return jnp.concatenate([get(first + n) for n in range(group)], axis=1)

            def cut(value, n):
                return value[:, n * width : (n + 1) * width]

            inner = wide(lambda r: norm_ref[r])
            nb[:, lanes] = inner
            mask = wide(lambda r: mask_ref[pl.ds(r, 1), :])
            parts = []
            for g in range(4):
                proj = dot(w_s[g * 8 * quarter : (g + 1) * 8 * quarter], inner)
                for k in range(4):
                    gate = proj[(2 * k) * quarter : (2 * k + 1) * quarter]
                    value = proj[(2 * k + 1) * quarter : (2 * k + 2) * quarter]
                    grad = wide(lambda r: sums[k][pl.ds(g * quarter * (rows + 1) + r, quarter, stride=rows + 1), :])
                    sig = sigmoid(gate)
                    back = grad * mask * sig
                    parts.append((back * value * (1.0 - sig)).astype(bf16))
                    parts.append(back.astype(bf16))
                for d in range(2):
                    at = d * chans + g * quarter
                    parts.append(wide(lambda r: gate_ref[r, at : at + quarter]))
                for n in range(group):
                    sc_s[g * 16 : g * 16 + here, n * width : (n + 1) * width] = score_ref[
                        first + n, g * here : (g + 1) * here
                    ]
                parts.append(sc_s[g * 16 : (g + 1) * 16].astype(bf16))
                parts.append(jnp.zeros((block_rows - 10 * quarter - 16, group * width), bf16))
            every = jnp.concatenate(parts, axis=0)
            gall[:, lanes] = every
            back = dot(wall_t[...], every)
            scaled, inverse = sub_norm(wide(lambda r: pair_ref[r]).astype(f32))
            gg_s[...] += back * scaled
            out = wide(lambda r: mid_ref[r]).astype(f32) + sub_norm_back(gain, scaled, inverse, back)
            out = out.astype(bf16)
            for n in range(group):
                for q in range(4):
                    po[q, first + n] = cut(out[q * quarter : (q + 1) * quarter], n)

        for m in range(4):
            outs[m][...] = po[lax.bitwise_xor(z, m)]
        gw_ref[...] += dot(gall[...], nb[...], 1, 1)

    @pl.when(step == i_steps - 1)
    def _():
        row = lane_sums(gg_s[...])
        for g in range(4):
            at = (g + 1) * block_rows - 1
            gw_ref[at : at + 1] += row
        gw_out_ref[...] = gw_ref[...].astype(gw_out_ref.dtype)

    @pl.when(step == i_steps)
    def _():
        for m in range(4):
            outs[m][: extra_ref.shape[1]] = extra_ref[m]


def finish(place, sums, first_row, pair, norm, mid, gate, scores, mask_rows, gain, wall, prev, extra, step_rows=16):
    rows, chans, width = pair.shape
    quarter = chans // 4
    heads = scores.shape[1]
    packed = 4 * wall.shape[1]
    i_steps = rows // step_rows
    fresh = prev is None
    start = first_row // step_rows
    last = first_row + rows == mask_rows.shape[0]
    total = in_hbm((packed, chans), bf16 if last else f32)

    def at(s):
        return jnp.minimum(s, i_steps - 1)

    if fresh:
        prev = gain
    row_spec = pl.BlockSpec((step_rows, chans, width), lambda s: (at(s), 0, 0))
    piece_spec = pl.BlockSpec((step_rows, quarter, width), lambda s: (s, 0, 0))
    piece = in_hbm((rows + (extra.shape[1] if last else 0), quarter, width), bf16)
    lanes = step_rows * width
    return pl.pallas_call(
        functools.partial(finish_kernel, i_steps, fresh),
        grid=(i_steps + (1 if last else 0),),
        in_specs=[place_spec(), pl.BlockSpec((4, chans, step_rows, width), lambda s: (0, 0, at(s) + start, 0))]
        + [row_spec] * 3
        + [
            pl.BlockSpec((step_rows, 2 * chans, width), lambda s: (at(s), 0, 0)),
            pl.BlockSpec((step_rows, heads, width), lambda s: (at(s) + start, 0, 0)),
            pl.BlockSpec((step_rows, width), lambda s: (at(s) + start, 0)),
        ]
        + [whole_spec(a) for a in (gain, wall, prev, extra)],
        out_specs=[piece_spec] * 4 + [whole_spec(total)],
        out_shape=[piece] * 4 + [total],
        scratch_shapes=[pltpu.VMEM((packed, chans), f32)]
        + [pltpu.VMEM((chans * (step_rows + 1), width), f32)] * 4
        + [
            pltpu.VMEM((chans, packed), bf16),
            pltpu.VMEM((8 * chans, chans), bf16),
            pltpu.VMEM((packed, lanes), bf16),
            pltpu.VMEM((chans, lanes), bf16),
            pltpu.VMEM((4, step_rows, quarter, width), bf16),
            pltpu.VMEM((64, group * width), f32),
            pltpu.VMEM((chans, group * width), f32),
        ],
        compiler_params=params(56),
        cost_estimate=quick,
        name="finish",
    )(place, *held([sums, pair, norm, mid, gate]), scores, mask_rows, gain, wall, prev, extra)


def assemble_kernel(rows, count, nodes, place_ref, *refs):
    pieces, (out_ref, *node_refs) = refs[: 4 * count], refs[4 * count : 4 * count + (3 if nodes else 1)]
    sems, z = refs[-1], place_ref[0]
    copies = []
    for m in range(4):
        crop = lax.bitwise_xor(z, m)
        for n in range(count):
            source, target = pieces[4 * n + m], out_ref.at[crop, pl.ds(n * rows, rows)]
            copies.append(pltpu.make_async_copy(source.at[pl.ds(0, rows)], target, sems.at[m, n]))
        if nodes:
            source = pieces[4 * (count - 1) + m].at[pl.ds(rows, 2)]
            copies.append(pltpu.make_async_copy(source, refs[-2].at[crop], sems.at[m, count]))
    for copy in copies:
        copy.start()
    for copy in copies:
        copy.wait()
    for n, ref in enumerate(node_refs):
        for crop in range(4):
            value = refs[-2][crop, n]
            half, width = value.shape[0], value.shape[1] // 2
            ref[crop, :half] = value[:, :width]
            ref[crop, half:] = value[:, width:]


def assemble(place, chunks, rows, nodes):
    _, quarter, width = chunks[0][0].shape
    count = len(chunks)
    vmem = pl.BlockSpec(memory_space=pltpu.VMEM)
    shapes = [jax.ShapeDtypeStruct((4, rows * count, quarter, width), bf16)]
    scratch = [pltpu.SemaphoreType.DMA((4, count + 1))]
    if nodes:
        shapes += [jax.ShapeDtypeStruct((4, 2 * quarter, width // 2), bf16)] * 2
        scratch = [pltpu.VMEM((4, 2, quarter, width), bf16)] + scratch
    return pl.pallas_call(
        functools.partial(assemble_kernel, rows, count, nodes),
        in_specs=[place_spec()] + [any_spec()] * (4 * count),
        out_specs=[any_spec()] + [vmem] * (len(shapes) - 1),
        out_shape=shapes,
        scratch_shapes=scratch,
        compiler_params=params(16),
        cost_estimate=quick,
        name="assemble",
    )(place, *[piece for chunk in chunks for piece in chunk])


def unpack_kernel(early, node_rows, place_ref, own, far, tri_in, gate, bias, tri_out, trans_in, trans_out, qkv, attn, node_in, node_out, gain_pair, gain_trans, gain_tri, gain_node, gain_node_trans):
    first = place_ref[1] == 0
    own, far = own[...].astype(f32), far[...].astype(f32)
    a, b = jnp.where(first, own[:node_rows], far[:node_rows]), jnp.where(first, far[:node_rows], own[:node_rows])
    last = own[early:] + far[early:]
    quarter = tri_out.shape[1]
    chans = trans_in.shape[0]
    wide = jnp.concatenate([a, b], axis=1)
    rest = own[node_rows:early] + far[node_rows:early]
    for d in range(2):
        for n in range(4):
            at = (4 * d + n) * quarter
            tri_in[d, n] = last[at : at + quarter]
        gate[d] = last[(8 + d) * quarter : (9 + d) * quarter]
        tri_out[d] = rest[d * quarter : (d + 1) * quarter]
    bias[...] = last[10 * quarter : 10 * quarter + bias.shape[0]]
    at = 2 * quarter
    trans_in[...] = rest[at : at + chans].T
    trans_out[...] = rest[at + chans : at + 2 * chans]
    at = at + 2 * chans
    z = place_ref[0]

    def own_block(rows, size):
        blocks = [rows[:, g * size : (g + 1) * size] for g in range(4)]
        low, high = jnp.where(z == 0, blocks[0], blocks[1]), jnp.where(z == 2, blocks[2], blocks[3])
        return jnp.where(z < 2, low, high)

    gain_pair[...] = own_block(last[last.shape[0] - 8 :], quarter)[7:]
    gains = own_block(rest[at : at + 8], quarter)
    gain_trans[...], gain_tri[...] = gains[:1], gains[1:3]
    size = qkv.shape[1]
    for n in range(3):
        qkv[n] = wide[n * size : (n + 1) * size]
    at = 3 * size
    attn[...] = wide[at : at + size]
    at = at + size
    size = node_in.shape[0]
    node_in[...] = wide[at : at + size].T
    node_out[...] = wide[at + size : at + 2 * size]
    at = at + 2 * size
    gains = own_block(wide[at : at + 8], 2 * quarter)
    gain_node[...], gain_node_trans[...] = gains[:1], gains[1:2]


def unpack(place, own, far, early, node_rows, heads):
    chans = own.shape[1]
    quarter, nodes = chans // 4, 2 * chans
    shapes = [
        (2, 4, quarter, chans), (2, quarter, chans), (heads, chans), (2, quarter, chans), (chans, chans), (chans, chans),
        (3, nodes // 4, nodes), (nodes // 4, nodes), (nodes, nodes), (nodes, nodes),
        (1, quarter), (1, quarter), (2, quarter), (1, nodes // 4), (1, nodes // 4),
    ]
    vmem = pl.BlockSpec(memory_space=pltpu.VMEM)
    return pl.pallas_call(
        functools.partial(unpack_kernel, early, node_rows),
        in_specs=[place_spec()] + [vmem] * 2,
        out_specs=[vmem] * len(shapes),
        out_shape=[jax.ShapeDtypeStruct(shape, f32) for shape in shapes],
        compiler_params=params(32),
        cost_estimate=quick,
        name="unpack",
    )(place, own, far)


def node_kernel(place_ref, bias_ref, bias_far, live_ref, gain_ref, gain_mid_ref, near_w, far_w,
                sent_ref, score_ref, gw_ref, w_all, att, gqkv):
    z, core, x = place_ref[0], place_ref[1], place_ref[2]
    first = core == 0
    groups, packed, _ = gw_ref.shape
    half_rows = bias_ref.shape[1]
    length, nodes = 2 * half_rows, gain_ref.shape[1]
    quarter = nodes // groups
    fold = quarter // 2
    count = near_w.shape[1] // 2 - fold
    for m in range(groups):
        for ref, side in ((near_w, core), (far_w, 1 - core)):
            for at, other in ((0, x), (count, 1 - x)):
                here = pl.ds(pl.multiple_of((2 * side + other) * count, count), count)
                w_all[lax.bitwise_xor(z, m), here] = ref[m, at:at + count]
    heads = bias_ref.shape[0]
    head_dim = nodes // heads
    hidden = nodes
    scale = 1.0 / math.sqrt(head_dim)

    def weight(at, size):
        return jnp.concatenate(
            [jnp.concatenate([w_all[g, half * packed + at:half * packed + at + size] for half in range(2)], axis=1) for g in range(groups)], axis=0)

    def ordered(mine, far):
        return jnp.concatenate([jnp.where(first, mine, far), jnp.where(first, far, mine)], axis=0)

    def rows(value):
        return jnp.where(first, value[:half_rows], value[half_rows:])

    def parts(value):
        centered = value - jnp.mean(value, axis=1, keepdims=True)
        inverse = lax.rsqrt(jnp.mean(centered * centered, axis=1, keepdims=True) + epsilon)
        return centered * inverse, inverse

    def back(gain, scaled, inverse, grad):
        weighted = gain * grad
        first_mean = jnp.mean(weighted, axis=1, keepdims=True)
        second_mean = jnp.mean(weighted * scaled, axis=1, keepdims=True)
        return inverse * (weighted - first_mean - scaled * second_mean)

    def own_half(value):
        return jnp.where(first, value[:, :128], value[:, 128:]).astype(bf16)

    def keep(at, value):
        size = value.shape[0] // groups
        for g in range(groups):
            gw_ref[g, at:at + size] = own_half(value[g * size:(g + 1) * size])

    def gain_row(grad, scaled):
        return jnp.sum(grad * scaled, axis=0, keepdims=True)


    def unfolded(ref, n):
        rows_of = slice(2 * count + n * fold, 2 * count + (n + 1) * fold)
        parts = [ref[lax.bitwise_xor(z, g), rows_of].astype(f32) for g in range(groups)]
        half = parts[0].shape[1] // 2
        return jnp.concatenate([jnp.concatenate([v[:, :half], v[:, half:]], axis=0) for v in parts], axis=1)

    def sent(n, value):
        for g in range(groups):
            part = value[:, g * quarter:(g + 1) * quarter]
            half = part.shape[0] // 2
            sent_ref[lax.bitwise_xor(z, g), n] = jnp.concatenate([part[:half], part[half:]], axis=1).astype(bf16)

    node_in = ordered(unfolded(near_w, 0), unfolded(far_w, 0))
    cot = ordered(unfolded(near_w, 1), unfolded(far_w, 1)).astype(bf16)
    scaled_in, inverse_in = parts(node_in)
    low_in = (scaled_in * gain_ref[...]).astype(bf16)
    q, k, v = (dot(low_in, weight(g * quarter, quarter), 1, 1).astype(bf16) for g in range(3))
    lane = lax.broadcasted_iota(jnp.int32, (1, nodes), 1)
    key_live = live_ref[...] > 0.5

    def of_head(value, h):
        here = (lane >= h * head_dim) & (lane < (h + 1) * head_dim)
        return jnp.where(here, value, jnp.zeros_like(value))

    def probs_of(h):
        raw = dot(of_head(q, h), k, 1, 1) * scale + ordered(bias_ref[h], bias_far[h])
        scores = jnp.where(key_live, raw, -1e9)
        exps = jnp.exp(scores - jnp.max(scores, axis=1, keepdims=True))
        return exps / jnp.sum(exps, axis=1, keepdims=True)

    total = jnp.zeros((length, nodes), f32)
    for h in range(heads):
        probs = probs_of(h)
        att[h] = probs
        total = total + dot(probs.astype(bf16), of_head(v, h))
    attn = total.astype(bf16)
    at_a, at_i, at_o = 3 * quarter, 4 * quarter, 4 * quarter + hidden
    mid = node_in + dot(attn, weight(at_a, quarter), 1, 1)
    scaled_mid, inverse_mid = parts(mid)
    low_mid = (scaled_mid * gain_mid_ref[...]).astype(bf16)
    out = mid
    grad = jnp.zeros((length, nodes), f32)
    for g in range(groups):
        w_in = jnp.concatenate([w_all[g, half * packed + at_i:half * packed + at_i + hidden] for half in range(2)], axis=1)
        w_out = jnp.concatenate([w_all[g, half * packed + at_o:half * packed + at_o + hidden] for half in range(2)], axis=1)
        act, slope = gelu_both(dot(low_mid, w_in, 1, 1))
        act = act.astype(bf16)
        out = out + dot(act, w_out)
        grad_pre = (dot(cot, w_out, 1, 1) * slope).astype(bf16)
        grad = grad + dot(grad_pre, w_in)
        gi, go = dot(grad_pre, low_mid, 0, 0), dot(act, cot, 0, 0)
        gw_ref[g, at_i:at_i + hidden] = own_half(gi)
        gw_ref[g, at_o:at_o + hidden] = own_half(go)
    sent(0, rows(out))
    mid_row = gain_row(grad, scaled_mid)
    grad_mid = cot.astype(f32) + back(gain_mid_ref[...], scaled_mid, inverse_mid, grad)
    grad_low = grad_mid.astype(bf16)
    keep(at_a, dot(grad_low, attn, 0, 0))
    grad_attn = dot(grad_low, weight(at_a, quarter)).astype(bf16)
    for g in range(3):
        gqkv[g] = jnp.zeros((length, nodes), f32)
    for h in range(heads):
        probs = att[h]
        grad_probs = dot(of_head(grad_attn, h), v, 1, 1)
        delta = jnp.sum(probs * grad_probs, axis=1, keepdims=True)
        scores = probs * (grad_probs - delta)
        score_ref[:, h, :] = rows(scores)
        scores = scores.astype(bf16)
        gqkv[0] += dot(scores, of_head(k, h))
        gqkv[1] += dot(scores, of_head(q, h), 0, 0)
        gqkv[2] += dot(probs.astype(bf16), of_head(grad_attn, h), 0, 0)
    grad = jnp.zeros((length, nodes), f32)
    for g, factor in enumerate((scale, scale, 1.0)):
        low = (gqkv[g] * factor).astype(bf16)
        keep(g * quarter, dot(low, low_in, 0, 0))
        grad = grad + dot(low, weight(g * quarter, quarter))
    tail = jnp.concatenate([gain_row(grad, scaled_in), mid_row, jnp.zeros((14, nodes), f32)], axis=0)
    for g in range(groups):
        gw_ref[g, packed - 16:] = own_half(tail)
    sent(1, rows(grad_mid + back(gain_ref[...], scaled_in, inverse_in, grad)))

def node_track(place, bias, bias_far, live, gain, gain_mid, near_w, far_w, rows):
    half_rows, length = bias.shape[1], live.shape[1]
    nodes = gain.shape[1]
    heads = bias.shape[0]
    arrays = (bias, bias_far, live, gain, gain_mid, near_w, far_w)
    shapes = [
        jax.ShapeDtypeStruct((near_w.shape[0], 2, half_rows // 2, 128), bf16),
        jax.ShapeDtypeStruct((half_rows, heads, length), f32),
        jax.ShapeDtypeStruct((near_w.shape[0], rows, 128), bf16),
    ]
    vmem = pl.BlockSpec(memory_space=pltpu.VMEM)
    return pl.pallas_call(
        node_kernel,
        in_specs=[pl.BlockSpec(memory_space=pltpu.SMEM)] + [vmem] * len(arrays),
        out_specs=[vmem] * len(shapes),
        out_shape=shapes,
        scratch_shapes=[pltpu.VMEM((near_w.shape[0], 2 * near_w.shape[1], 128), bf16), pltpu.VMEM((heads, length, length), f32), pltpu.VMEM((3, length, nodes), f32)],
        compiler_params=params(40),
        cost_estimate=quick,
        name="node_track",
    )(place, *arrays[:-2], *held(arrays[-2:]))


def shards_by_crop(
    pair,
    node,
    pair_cot,
    node_cot,
    lengths,
    present,
    gain_pair,
    w_tri_in,
    w_out_gate,
    gain_tri,
    w_tri_out,
    gain_trans,
    w_trans_in,
    w_trans_out,
    w_bias,
    gain_node,
    w_qkv,
    w_attn_out,
    gain_node_trans,
    w_node_in,
    w_node_out,
):
    groups = lax.axis_size(CHAN)
    rows_here = pair.shape[1]
    chans = groups * pair.shape[2]
    crop_len = pair.shape[3]
    nodes = groups * node.shape[2]
    heads = groups * w_bias.shape[1]
    quarter, node_quarter = chans // groups, nodes // groups
    z = lax.axis_index(CHAN)
    core = lax.axis_index(DP) % 2
    x = lax.axis_index(ROWS)
    y = lax.axis_index(DP) // 2
    place = jnp.stack([z, core, x, y]).astype(jnp.int32)
    mesh_shape = (lax.axis_size(DP), lax.axis_size(ROWS), groups)

    def device(d, r, c):
        return (d * mesh_shape[1] + r) * groups + c

    def home_perm(m):
        return [
            (device(d, r, c), device(d - d % 2 + r, d % 2, c ^ m))
            for d in range(mesh_shape[0])
            for r in range(mesh_shape[1])
            for c in range(groups)
        ]

    core_pairs = [(d, d ^ 1) for d in range(mesh_shape[0])]
    row_pairs = [(0, 1), (1, 0)]

    def send_home(pieces):
        return [
            lax.ppermute(piece, (DP, ROWS, CHAN), home_perm(m))
            for m, piece in enumerate(pieces)
        ]

    def to_chan(value, m):
        return lax.ppermute(value, CHAN, [(c, c ^ m) for c in range(groups)])

    def swap_core(value):
        return lax.ppermute(value, DP, core_pairs)

    def pick(value, index):
        return lax.dynamic_index_in_dim(value, index, 0, keepdims=False)

    def own_rows(value, axis):
        return lax.dynamic_slice_in_dim(value, core * rows_here, rows_here, axis)

    def packed(parts):
        return jnp.concatenate([part.reshape(-1, chans) for part in parts])

    def split(value):
        return jnp.concatenate([value[:, :chans], value[:, chans:]])

    chunk = min(32, rows_here)
    tied = lax.optimization_barrier

    def blocks(rows):
        rows = jnp.pad(rows, ((0, -rows.shape[0] % (4 * quarter)), (0, 0)))
        return rows.reshape(-1, quarter, chans)

    def with_far(own, far, side):
        return jnp.concatenate([jnp.where(side == 0, own, far), jnp.where(side == 0, far, own)], axis=1)

    def swap_rows(value):
        return lax.ppermute(value, ROWS, row_pairs)

    node_rest = jnp.concatenate(
        [w_qkv.transpose(0, 2, 1).reshape(-1, nodes), w_attn_out.T, w_node_in.T, w_node_out]
    )
    node_rest = jnp.pad(node_rest, ((0, 16), (0, 0)))
    first_rows, pair_rows, node_rows = 10 * quarter + 32, 2 * quarter + 2 * chans, node_rest.shape[0]

    def tiles(values):
        return jnp.broadcast_to(values[..., None], values.shape + (chans,))

    gains = [tiles(values) for values in (gain_pair, gain_tri, gain_trans)]
    sent = pack(
        place,
        pair,
        0,
        chunk,
        first=[
            lengths,
            present,
            node,
            node_cot,
            w_tri_in.transpose(0, 1, 3, 2).reshape(-1, chans),
            w_out_gate.transpose(0, 2, 1).reshape(-1, chans),
            w_bias.T,
            w_tri_out.transpose(0, 2, 1).reshape(-1, chans),
            w_trans_in,
            w_trans_out,
        ],
    )
    sent, pair, pair_cot = tied((sent, pair, pair_cot))
    pieces0 = send_home(sent)
    sent = pack(place, pair, chunk, chunk)
    sent_cots = pack(place, pair_cot, 0, chunk)
    sent_later = pack(place, pair_cot, chunk, chunk, blocks(split(node_rest)))
    sent_cots, sent_later, gains = tied((sent_cots, sent_later, gains))
    sent, sent_cots, sent_later, gains, pieces0 = tied((sent, sent_cots, sent_later, gains, pieces0))
    pieces1 = send_home(sent)
    node_own = jnp.stack([piece[chunk + 1 : chunk + 3] for piece in pieces0])
    weights = jnp.stack([piece[chunk + 3 :] for piece in pieces0]).reshape(groups, -1, chans)
    weights = with_far(weights, swap_core(weights), core)
    wall, rest = weights[:, :first_rows], weights[:, first_rows : first_rows + pair_rows]
    gain, gains_mid = gains[0], gains[1:]
    live = pieces0[0][chunk, 0].astype(jnp.float32)
    mask_rows = own_rows(live, 0)[:, None] * live[None, :]
    tri0, norm0, pair0, bias0 = project(place, pieces0, wall, mask_rows, gain, heads, chunk, 0)
    tri0, pieces1, rest = tied((tri0, pieces1, rest))
    far0 = swap_core(tri0)
    tri1, norm1, pair1, bias1 = project(place, pieces1, wall, mask_rows, gain, heads, chunk, chunk)
    tri1, far0, sent = tied((tri1, far0, sent_cots))
    far1 = swap_core(tri1)
    cots0 = send_home(sent)
    bias = jnp.concatenate([bias0, bias1], axis=1)
    bias, far1 = tied((bias, far1))
    bias_far = swap_core(bias)
    tri = tri_forward(place, (tri0, tri1), (far0, far1))
    sent, bias_far, cots0, tri = tied((sent_later, bias_far, cots0, tri))
    cots1 = send_home(sent)
    norms, pairs = (norm0, norm1), (pair0, pair1)

    core_round, row_round = (core, DP, core_pairs), (x, ROWS, row_pairs)
    y_round = (y, DP, [(d, d ^ 2) for d in range(mesh_shape[0])])

    def halve(value, side, axis, pairs, at=1):
        low, high = jnp.split(value, 2, at)
        far = lax.ppermute(jnp.where(side == 0, high, low).astype(jnp.bfloat16), axis, pairs)
        return jnp.where(side == 0, low, high).astype(jnp.float32), far

    def added(kept, far):
        return (kept + far).astype(jnp.bfloat16)

    def both(value, far, side):
        return jnp.concatenate([jnp.where(side == 0, value, far), jnp.where(side == 0, far, value)])

    def run_middle(n, cots, prev):
        return middle(
            place, tri, n * chunk, pairs[n], norms[n], cots, *gains_mid, wall, rest, prev
        )

    *out0, mid0, gate0, gtri0, gw_rest = run_middle(0, cots0, None)
    out0, gtri0, cots1 = tied((out0, gtri0, cots1))
    out0 = send_home(out0)
    node_rest = jnp.stack([cot[chunk:] for cot in cots1]).reshape(groups, -1, chans)
    node_rest = jnp.concatenate(
        [node_rest, swap_rows(node_rest), node_own.reshape(groups, -1, chans)], axis=1
    )
    *out1, mid1, gate1, gtri1, gw_rest = run_middle(1, cots1, gw_rest)
    gtri0, gtri1, out0, node_rest = tied((gtri0, gtri1, out0, node_rest))
    node_rest_far = swap_core(node_rest)
    gtri0, gtri1, node_rest_far = tied((gtri0, gtri1, node_rest_far))
    gtris = (gtri0, gtri1)
    gtris_far = [swap_core(gtri) for gtri in gtris]
    mids, gates = (mid0, mid1), (gate0, gate1)

    node_sent, scores, gw_node = node_track(
        place,
        bias,
        bias_far,
        live[None, :],
        gain_node[None, :],
        gain_node_trans[None, :],
        node_rest,
        node_rest_far,
        node_rows,
    )
    early = [gw_node, gw_rest]
    early_rows = sum(part.shape[1] for part in early)
    early.append(jnp.zeros((groups, -early_rows % 64, chans), jnp.bfloat16))
    early = jnp.concatenate(early, axis=1)
    out1, gtris_far = tied((out1, gtris_far))
    out1 = send_home(out1)
    kept, far = halve(early, *row_round)
    sums = tri_backward(place, (tri0, tri1), (far0, far1), gtris, gtris_far)

    def run_finish(n, prev):
        return finish(
            place, sums, n * chunk, pairs[n], norms[n], mids[n], gates[n], scores, mask_rows, gain, wall, prev, node_sent
        )

    *grad0, gw_first = run_finish(0, None)
    grad0, out1, kept, far = tied((grad0, out1, kept, far))
    kept, far = halve(added(kept, far), *y_round)
    grad0 = send_home(grad0)
    *grad1, gw_first = run_finish(1, gw_first)
    grad1, gw_first, grad0 = tied((grad1, gw_first, grad0))
    grad1 = send_home(grad1)
    early = added(kept, far)
    shard = early.shape[1]
    low = jnp.concatenate([early, gw_first.reshape(groups, -1, chans)], axis=1)
    total = pick(low, z).astype(jnp.float32)
    for m in range(1, groups):
        total = total + to_chan(pick(low, z ^ m), m)
    total = total.astype(jnp.bfloat16)
    total, out0, out1 = tied((total, out0, out1))
    def joined(chunks):
        rows = [jnp.concatenate([c[m][:chunk] for c in chunks]) for m in range(groups)]
        stacked = jnp.stack(rows)
        return jnp.stack([pick(stacked, z ^ k) for k in range(groups)])

    pair_out = joined((out0, out1))
    early, late = total[:shard], total[shard:]
    for side, axis, pairs in (y_round, row_round):
        far = lax.ppermute(jnp.concatenate([early, late]), axis, pairs)
        if axis != ROWS:
            grad1, far, pair_out = tied((grad1, far, pair_out))
        late = added(late.astype(jnp.float32), far[early.shape[0] :])
        early = both(early, far[: early.shape[0]], side)
    own = jnp.concatenate([early, late])
    far = swap_core(own)
    tri_in, out_gate, bias_w, tri_out, trans_in, trans_out, qkv, attn, node_in, node_out, *gains = unpack(
        place, own, far, early.shape[0], node_rows, w_bias.shape[1]
    )
    pair_grad, node_result, node_grad = assemble(place, (grad0, grad1), chunk, True)

    return (
        pair_out,
        node_result,
        pair_grad,
        node_grad,
        gains[0].reshape(-1),
        tri_in.transpose(0, 1, 3, 2),
        out_gate.transpose(0, 2, 1),
        gains[2],
        tri_out.transpose(0, 2, 1),
        gains[1].reshape(-1),
        trans_in,
        trans_out,
        bias_w.T,
        gains[3].reshape(-1),
        qkv.transpose(0, 2, 1),
        attn.T,
        gains[4].reshape(-1),
        node_in,
        node_out,
    )


def solution(mesh):
    in_specs = (
        P(DP, ROWS, CHAN, None),
        P(DP, ROWS, CHAN),
        P(DP, ROWS, CHAN, None),
        P(DP, ROWS, CHAN),
        P(DP),
        P(DP, None),
        P(),
        P(None, None, None, CHAN),
        P(None, None, CHAN),
        P(),
        P(None, None, CHAN),
        P(),
        P(None, CHAN),
        P(CHAN, None),
        P(None, CHAN),
        P(),
        P(None, None, CHAN),
        P(None, CHAN),
        P(),
        P(None, CHAN),
        P(CHAN, None),
    )
    out_specs = (
        P(DP, ROWS, CHAN, None),
        P(DP, ROWS, CHAN),
        P(DP, ROWS, CHAN, None),
        P(DP, ROWS, CHAN),
        P(CHAN),
        P(None, None, None, CHAN),
        P(None, None, CHAN),
        P(None, CHAN),
        P(None, None, CHAN),
        P(CHAN),
        P(None, CHAN),
        P(CHAN, None),
        P(None, CHAN),
        P(CHAN),
        P(None, None, CHAN),
        P(None, CHAN),
        P(CHAN),
        P(None, CHAN),
        P(CHAN, None),
    )
    sizes = dict(mesh.shape)
    by_crop = sizes[ROWS] == 2 and sizes[DP] == 4 and sizes[CHAN] == 4
    body = shards_by_crop if by_crop else shards
    return jax.shard_map(body, mesh=mesh, in_specs=in_specs, out_specs=out_specs, check_vma=False)
```

```python
import functools
import math

import jax
import jax.numpy as jnp
from jax import lax
from jax.experimental import pallas as pl
from jax.experimental.pallas import tpu as pltpu
from jax.sharding import PartitionSpec as P

f32, bf16 = jnp.float32, jnp.bfloat16
epsilon = 1e-05
DP, ROWS, CHAN = "dp", "rows", "chan"
masked_score = -1000000000.0


def norm_parts(full):
    mean = jnp.mean(full, axis=2, keepdims=True)
    centered = full - mean
    variance = jnp.mean(centered * centered, axis=2, keepdims=True)
    inverse = lax.rsqrt(variance + epsilon)
    return (centered * inverse, inverse)


def shaped(gain, full):
    return gain.reshape(gain.shape + (1,) * (full.ndim - 3))


def normed(full, gain):
    scaled, inverse = norm_parts(full)
    return scaled * shaped(gain, full)


def stat_terms(full, gain, partial_value, groups):
    scaled, inverse = norm_parts(full)
    weighted = shaped(gain, full) * partial_value
    first_sum = jnp.sum(weighted, axis=2)
    second_sum = jnp.sum(weighted * scaled, axis=2)
    stacked = jnp.stack([first_sum, second_sum], axis=2)
    repeats = (1, 1, groups) + (1,) * (full.ndim - 3)
    return jnp.tile(stacked, repeats)


def norm_finish(full, gain, grad_here, totals, chan_index):
    width = full.shape[2]
    here = grad_here.shape[2]
    scaled, inverse = norm_parts(full)
    scaled_here = lax.dynamic_slice_in_dim(scaled, chan_index * here, here, 2)
    gain_here = lax.dynamic_slice_in_dim(gain, chan_index * here, here, 0)
    first_mean = totals[:, :, 0:1] / width
    second_mean = totals[:, :, 1:2] / width
    grad_input = inverse * (
        shaped(gain_here, full) * grad_here - first_mean - scaled_here * second_mean
    )
    summed_axes = (0, 1) + tuple(range(3, full.ndim))
    grad_gain = jnp.sum(grad_here * scaled_here, axis=summed_axes)
    return (grad_input, grad_gain)


def gelu_exact(value):
    return jax.nn.gelu(value, approximate=False)


def softmax_rows(scores):
    top = jnp.max(scores, axis=-1, keepdims=True)
    exps = jnp.exp(scores - top)
    return exps / jnp.sum(exps, axis=-1, keepdims=True)


def shards(
    pair,
    node,
    pair_cot,
    node_cot,
    lengths,
    present,
    gain_pair,
    w_tri_in,
    w_out_gate,
    gain_tri,
    w_tri_out,
    gain_trans,
    w_trans_in,
    w_trans_out,
    w_bias,
    gain_node,
    w_qkv,
    w_attn_out,
    gain_node_trans,
    w_node_in,
    w_node_out,
):
    batch = pair.shape[0]
    rows_here = pair.shape[1]
    crop_len = pair.shape[3]
    groups = lax.axis_size(CHAN)
    chan_index = lax.axis_index(CHAN)
    row_start = lax.axis_index(ROWS) * rows_here
    heads_here = w_bias.shape[1]
    head_dim = w_qkv.shape[2] // heads_here
    scale = 1.0 / math.sqrt(head_dim)
    positions = jnp.arange(crop_len, dtype=jnp.int32)
    mask_all = present.astype(jnp.float32) * (positions[None, :] < lengths[:, None]).astype(
        jnp.float32
    )
    mask_rows = lax.dynamic_slice_in_dim(mask_all, row_start, rows_here, 1)
    pair_mask = mask_rows[:, :, None, None] * mask_all[:, None, None, :]
    key_live = mask_all[:, None, None, :] > 0.5

    def gating(gate, value):
        return jax.nn.sigmoid(gate) * value * pair_mask

    pair_whole, node_whole = (
        lax.all_gather(pair, CHAN, axis=2, tiled=True),
        lax.all_gather(node, CHAN, axis=2, tiled=True),
    )
    full_in = pair_whole.astype(jnp.float32)
    node_full = node_whole.astype(jnp.float32)
    stream_in = pair.astype(jnp.float32)
    node_in = node.astype(jnp.float32)
    normed_in = normed(full_in, gain_pair).astype(jnp.bfloat16)
    projected = jnp.einsum(
        "bicj,dgch->dgbihj", normed_in, w_tri_in, preferred_element_type=jnp.float32
    )
    gate_pre = jnp.einsum(
        "bicj,dcx->dbixj", normed_in, w_out_gate, preferred_element_type=jnp.float32
    )
    bias = jnp.einsum("bicj,ch->bhij", normed_in, w_bias, preferred_element_type=jnp.float32)
    left_out = gating(projected[0, 0], projected[0, 1]).astype(jnp.bfloat16)
    right_out = gating(projected[0, 2], projected[0, 3]).astype(jnp.bfloat16)
    left_in = gating(projected[1, 0], projected[1, 1]).astype(jnp.bfloat16)
    right_in = gating(projected[1, 2], projected[1, 3]).astype(jnp.bfloat16)
    normed_node = normed(node_full, gain_node).astype(jnp.bfloat16)
    qkv = jnp.einsum(
        "bin,gna->gbia", normed_node, w_qkv, preferred_element_type=jnp.float32
    ).astype(jnp.bfloat16)
    whole_right_out, whole_right_in, whole_keys, whole_values = (
        lax.all_gather(right_out, ROWS, axis=1, tiled=True),
        lax.all_gather(right_in, ROWS, axis=1, tiled=True),
        lax.all_gather(qkv[1], ROWS, axis=1, tiled=True),
        lax.all_gather(qkv[2], ROWS, axis=1, tiled=True),
    )
    left_cols = lax.all_to_all(left_in, ROWS, split_axis=3, concat_axis=1, tiled=True)
    queries = qkv[0].reshape(batch, rows_here, heads_here, head_dim)
    keys = whole_keys.reshape(batch, crop_len, heads_here, head_dim)
    values = whole_values.reshape(batch, crop_len, heads_here, head_dim)
    raw = (
        jnp.einsum("bihd,bjhd->bhij", queries, keys, preferred_element_type=jnp.float32) * scale
        + bias
    )
    probs = softmax_rows(jnp.where(key_live, raw, masked_score))
    probs_low = probs.astype(jnp.bfloat16)
    attn = jnp.einsum(
        "bhij,bjhd->bihd", probs_low, values, preferred_element_type=jnp.float32
    ).astype(jnp.bfloat16)
    attn = attn.reshape(batch, rows_here, heads_here * head_dim)
    tri_out = jnp.einsum(
        "bihk,bjhk->bihj", left_out, whole_right_out, preferred_element_type=jnp.float32
    )
    tri_in = jnp.einsum(
        "bkhi,bkhj->bihj", left_cols, whole_right_in, preferred_element_type=jnp.float32
    )
    tri_full_out, tri_full_in, attn_whole = (
        lax.all_gather(tri_out.astype(jnp.bfloat16), CHAN, axis=2, tiled=True).astype(
            tri_out.dtype
        ),
        lax.all_gather(tri_in.astype(jnp.bfloat16), CHAN, axis=2, tiled=True).astype(
            tri_in.dtype
        ),
        lax.all_gather(
            attn.astype(jnp.float32).astype(jnp.bfloat16), CHAN, axis=2, tiled=True
        ).astype(jnp.float32),
    )
    normed_out = normed(tri_full_out, gain_tri[0]).astype(jnp.bfloat16)
    normed_inc = normed(tri_full_in, gain_tri[1]).astype(jnp.bfloat16)
    branch_out = jnp.einsum(
        "bihj,hc->bicj", normed_out, w_tri_out[0], preferred_element_type=jnp.float32
    )
    branch_inc = jnp.einsum(
        "bihj,hc->bicj", normed_inc, w_tri_out[1], preferred_element_type=jnp.float32
    )
    gate_sig = jax.nn.sigmoid(gate_pre)
    stream_mid = stream_in + gate_sig[0] * branch_out + gate_sig[1] * branch_inc
    attn_low = attn_whole.astype(jnp.bfloat16)
    node_mid = node_in + jnp.einsum(
        "bia,an->bin", attn_low, w_attn_out, preferred_element_type=jnp.float32
    )
    full_mid, node_full_mid = (
        lax.all_gather(stream_mid.astype(jnp.bfloat16), CHAN, axis=2, tiled=True).astype(
            stream_mid.dtype
        ),
        lax.all_gather(node_mid.astype(jnp.bfloat16), CHAN, axis=2, tiled=True).astype(
            node_mid.dtype
        ),
    )
    normed_mid = normed(full_mid, gain_trans).astype(jnp.bfloat16)
    pre_hidden = jnp.einsum(
        "bicj,cf->bifj", normed_mid, w_trans_in, preferred_element_type=jnp.float32
    )
    hidden, gelu_pull = jax.vjp(gelu_exact, pre_hidden)
    hidden_low = hidden.astype(jnp.bfloat16)
    out_terms = jnp.einsum(
        "bifj,fc->bicj", hidden_low, w_trans_out, preferred_element_type=jnp.float32
    )
    normed_node_mid = normed(node_full_mid, gain_node_trans).astype(jnp.bfloat16)
    node_pre = jnp.einsum(
        "bin,nf->bif", normed_node_mid, w_node_in, preferred_element_type=jnp.float32
    )
    node_hidden, node_gelu_pull = jax.vjp(gelu_exact, node_pre)
    node_hidden_low = node_hidden.astype(jnp.bfloat16)
    node_terms = jnp.einsum(
        "bif,fn->bin", node_hidden_low, w_node_out, preferred_element_type=jnp.float32
    )
    pair_sum, node_sum = (
        lax.psum_scatter(
            out_terms.astype(jnp.bfloat16), CHAN, scatter_dimension=2, tiled=True
        ).astype(jnp.float32),
        lax.psum_scatter(
            node_terms.astype(jnp.bfloat16), CHAN, scatter_dimension=2, tiled=True
        ).astype(jnp.float32),
    )
    stream_out = stream_mid + pair_sum
    node_out = node_mid + node_sum
    cot_full, node_cot_full = (
        lax.all_gather(pair_cot, CHAN, axis=2, tiled=True),
        lax.all_gather(node_cot, CHAN, axis=2, tiled=True),
    )
    grad_trans_out = jnp.einsum(
        "bifj,bicj->fc", hidden_low, cot_full, preferred_element_type=jnp.float32
    )
    grad_hidden = jnp.einsum(
        "bicj,fc->bifj", cot_full, w_trans_out, preferred_element_type=jnp.float32
    )
    grad_pre = gelu_pull(grad_hidden)[0].astype(jnp.bfloat16)
    grad_trans_in = jnp.einsum(
        "bicj,bifj->cf", normed_mid, grad_pre, preferred_element_type=jnp.float32
    )
    grad_normed_mid = jnp.einsum(
        "bifj,cf->bicj", grad_pre, w_trans_in, preferred_element_type=jnp.float32
    )
    mid_terms = stat_terms(full_mid, gain_trans, grad_normed_mid, groups)
    grad_node_out_w = jnp.einsum(
        "bif,bin->fn", node_hidden_low, node_cot_full, preferred_element_type=jnp.float32
    )
    grad_node_hidden = jnp.einsum(
        "bin,fn->bif", node_cot_full, w_node_out, preferred_element_type=jnp.float32
    )
    grad_node_pre = node_gelu_pull(grad_node_hidden)[0].astype(jnp.bfloat16)
    grad_node_in_w = jnp.einsum(
        "bin,bif->nf", normed_node_mid, grad_node_pre, preferred_element_type=jnp.float32
    )
    grad_normed_node_mid = jnp.einsum(
        "bif,nf->bin", grad_node_pre, w_node_in, preferred_element_type=jnp.float32
    )
    node_mid_terms = stat_terms(node_full_mid, gain_node_trans, grad_normed_node_mid, groups)
    mid_here, mid_totals, node_mid_here, node_mid_totals = (
        lax.psum_scatter(
            grad_normed_mid.astype(jnp.bfloat16), CHAN, scatter_dimension=2, tiled=True
        ).astype(jnp.float32),
        lax.psum_scatter(
            mid_terms.astype(jnp.bfloat16), CHAN, scatter_dimension=2, tiled=True
        ).astype(jnp.float32),
        lax.psum_scatter(
            grad_normed_node_mid.astype(jnp.bfloat16), CHAN, scatter_dimension=2, tiled=True
        ).astype(jnp.float32),
        lax.psum_scatter(
            node_mid_terms.astype(jnp.bfloat16), CHAN, scatter_dimension=2, tiled=True
        ).astype(jnp.float32),
    )
    mid_extra, grad_gain_trans = norm_finish(full_mid, gain_trans, mid_here, mid_totals, chan_index)
    node_mid_extra, grad_gain_node_trans = norm_finish(
        node_full_mid, gain_node_trans, node_mid_here, node_mid_totals, chan_index
    )
    grad_mid = pair_cot.astype(jnp.float32) + mid_extra
    grad_node_mid = node_cot.astype(jnp.float32) + node_mid_extra
    branches = jnp.stack([branch_out, branch_inc])
    grad_branch = (gate_sig * grad_mid[None]).astype(jnp.bfloat16)
    grad_gate = (grad_mid[None] * branches * gate_sig * (1.0 - gate_sig)).astype(jnp.bfloat16)
    tri_normed_both = jnp.stack([normed_out, normed_inc])
    grad_w_tri_out = jnp.einsum(
        "dbihj,dbicj->dhc", tri_normed_both, grad_branch, preferred_element_type=jnp.float32
    )
    grad_out_gate = jnp.einsum(
        "bicj,dbixj->dcx", normed_in, grad_gate, preferred_element_type=jnp.float32
    )
    grad_tri_normed = jnp.einsum(
        "dbicj,dhc->dbihj", grad_branch, w_tri_out, preferred_element_type=jnp.float32
    )
    out_stats = stat_terms(tri_full_out, gain_tri[0], grad_tri_normed[0], groups)
    inc_stats = stat_terms(tri_full_in, gain_tri[1], grad_tri_normed[1], groups)
    grad_attn_branch = grad_node_mid.astype(jnp.bfloat16)
    grad_w_attn_out = jnp.einsum(
        "bia,bin->an", attn_low, grad_attn_branch, preferred_element_type=jnp.float32
    )
    attn_terms = jnp.einsum(
        "bin,an->bia", grad_attn_branch, w_attn_out, preferred_element_type=jnp.float32
    )
    out_here, out_totals, inc_here, inc_totals, attn_here = (
        lax.psum_scatter(
            grad_tri_normed[0].astype(jnp.bfloat16), CHAN, scatter_dimension=2, tiled=True
        ).astype(jnp.float32),
        lax.psum_scatter(
            out_stats.astype(jnp.bfloat16), CHAN, scatter_dimension=2, tiled=True
        ).astype(jnp.float32),
        lax.psum_scatter(
            grad_tri_normed[1].astype(jnp.bfloat16), CHAN, scatter_dimension=2, tiled=True
        ).astype(jnp.float32),
        lax.psum_scatter(
            inc_stats.astype(jnp.bfloat16), CHAN, scatter_dimension=2, tiled=True
        ).astype(jnp.float32),
        lax.psum_scatter(
            attn_terms.astype(jnp.bfloat16), CHAN, scatter_dimension=2, tiled=True
        ).astype(jnp.float32),
    )
    grad_tri_a, gain_grad_out = norm_finish(
        tri_full_out, gain_tri[0], out_here, out_totals, chan_index
    )
    grad_tri_b, gain_grad_inc = norm_finish(
        tri_full_in, gain_tri[1], inc_here, inc_totals, chan_index
    )
    grad_gain_tri = jnp.stack([gain_grad_out, gain_grad_inc])
    grad_out_low = grad_tri_a.astype(jnp.bfloat16)
    grad_inc_low = grad_tri_b.astype(jnp.bfloat16)
    grad_attn = attn_here.astype(jnp.bfloat16).reshape(batch, rows_here, heads_here, head_dim)
    grad_probs = jnp.einsum(
        "bihd,bjhd->bhij", grad_attn, values, preferred_element_type=jnp.float32
    )
    delta = jnp.sum(probs * grad_probs, axis=3, keepdims=True)
    grad_scores = (probs * (grad_probs - delta)).astype(jnp.bfloat16)
    grad_queries = (
        jnp.einsum("bhij,bjhd->bihd", grad_scores, keys, preferred_element_type=jnp.float32) * scale
    )
    key_terms = (
        jnp.einsum("bhij,bihd->bjhd", grad_scores, queries, preferred_element_type=jnp.float32)
        * scale
    )
    value_terms = jnp.einsum(
        "bhij,bihd->bjhd", probs_low, grad_attn, preferred_element_type=jnp.float32
    )
    grad_w_bias = jnp.einsum(
        "bicj,bhij->ch", normed_in, grad_scores, preferred_element_type=jnp.float32
    )
    bias_back = jnp.einsum("bhij,ch->bicj", grad_scores, w_bias, preferred_element_type=jnp.float32)
    grad_left_out = jnp.einsum(
        "bihj,bjhk->bihk", grad_out_low, whole_right_out, preferred_element_type=jnp.float32
    )
    right_terms = jnp.einsum(
        "bihj,bihk->bjhk", grad_out_low, left_out, preferred_element_type=jnp.float32
    )
    grad_right_out, key_grads, value_grads = (
        lax.psum_scatter(
            right_terms.astype(jnp.bfloat16), ROWS, scatter_dimension=1, tiled=True
        ).astype(jnp.float32),
        lax.psum_scatter(
            key_terms.astype(jnp.bfloat16), ROWS, scatter_dimension=1, tiled=True
        ).astype(jnp.float32),
        lax.psum_scatter(
            value_terms.astype(jnp.bfloat16), ROWS, scatter_dimension=1, tiled=True
        ).astype(jnp.float32),
    )
    whole_grad_in = lax.all_gather(grad_inc_low, ROWS, axis=1, tiled=True)
    grad_left_in = jnp.einsum(
        "bihj,bkhj->bkhi", whole_grad_in, right_in, preferred_element_type=jnp.float32
    )
    grad_right_in = jnp.einsum(
        "bkhi,bihj->bkhj", left_in, whole_grad_in, preferred_element_type=jnp.float32
    )

    def gate_back(first, second, grad):
        kept_value, pull = jax.vjp(gating, first, second)
        return pull(grad)

    left_gate_out, left_value_out = gate_back(projected[0, 0], projected[0, 1], grad_left_out)
    right_gate_out, right_value_out = gate_back(projected[0, 2], projected[0, 3], grad_right_out)
    left_gate_in, left_value_in = gate_back(projected[1, 0], projected[1, 1], grad_left_in)
    right_gate_in, right_value_in = gate_back(projected[1, 2], projected[1, 3], grad_right_in)
    grad_proj = jnp.stack(
        [
            jnp.stack([left_gate_out, left_value_out, right_gate_out, right_value_out]),
            jnp.stack([left_gate_in, left_value_in, right_gate_in, right_value_in]),
        ]
    ).astype(jnp.bfloat16)
    grad_tri_in_w = jnp.einsum(
        "bicj,dgbihj->dgch", normed_in, grad_proj, preferred_element_type=jnp.float32
    )
    grad_normed_in = jnp.einsum(
        "dgbihj,dgch->bicj", grad_proj, w_tri_in, preferred_element_type=jnp.float32
    )
    grad_normed_in = grad_normed_in + jnp.einsum(
        "dbixj,dcx->bicj", grad_gate, w_out_gate, preferred_element_type=jnp.float32
    )
    grad_normed_in = grad_normed_in + bias_back
    grad_qkv = jnp.stack(
        [
            grad_queries.reshape(batch, rows_here, heads_here * head_dim),
            key_grads.reshape(batch, rows_here, heads_here * head_dim),
            value_grads.reshape(batch, rows_here, heads_here * head_dim),
        ]
    ).astype(jnp.bfloat16)
    grad_w_qkv = jnp.einsum(
        "bin,gbia->gna", normed_node, grad_qkv, preferred_element_type=jnp.float32
    )
    grad_normed_node = jnp.einsum(
        "gbia,gna->bin", grad_qkv, w_qkv, preferred_element_type=jnp.float32
    )
    in_terms = stat_terms(full_in, gain_pair, grad_normed_in, groups)
    node_in_terms = stat_terms(node_full, gain_node, grad_normed_node, groups)
    in_here, in_totals, node_in_here, node_in_totals = (
        lax.psum_scatter(
            grad_normed_in.astype(jnp.bfloat16), CHAN, scatter_dimension=2, tiled=True
        ).astype(jnp.float32),
        lax.psum_scatter(
            in_terms.astype(jnp.bfloat16), CHAN, scatter_dimension=2, tiled=True
        ).astype(jnp.float32),
        lax.psum_scatter(
            grad_normed_node.astype(jnp.bfloat16), CHAN, scatter_dimension=2, tiled=True
        ).astype(jnp.float32),
        lax.psum_scatter(
            node_in_terms.astype(jnp.bfloat16), CHAN, scatter_dimension=2, tiled=True
        ).astype(jnp.float32),
    )
    in_extra, grad_gain_pair = norm_finish(full_in, gain_pair, in_here, in_totals, chan_index)
    node_in_extra, grad_gain_node = norm_finish(
        node_full, gain_node, node_in_here, node_in_totals, chan_index
    )
    grad_stream = grad_mid + in_extra
    node_grad = grad_node_mid + node_in_extra
    summed = lax.psum(
        (
            grad_gain_pair,
            grad_tri_in_w,
            grad_out_gate,
            grad_gain_tri,
            grad_w_tri_out,
            grad_gain_trans,
            grad_trans_in,
            grad_trans_out,
            grad_w_bias,
            grad_gain_node,
            grad_w_qkv,
            grad_w_attn_out,
            grad_gain_node_trans,
            grad_node_in_w,
            grad_node_out_w,
        ),
        (DP, ROWS),
    )
    return (
        stream_out.astype(jnp.bfloat16),
        node_out.astype(jnp.bfloat16),
        grad_stream.astype(jnp.bfloat16),
        node_grad.astype(jnp.bfloat16),
        summed[0],
        summed[1],
        summed[2],
        summed[3],
        summed[4],
        summed[5],
        summed[6],
        summed[7],
        summed[8],
        summed[9],
        summed[10],
        summed[11],
        summed[12],
        summed[13],
        summed[14],
    )


ORDER = (3, 2, 0, 1)
IN_LEFT, IN_RIGHT, OUT_RIGHT, OUT_LEFT = range(4)

group = 16


def dot(a, b, ca=1, cb=0):
    return lax.dot_general(a, b, (((ca,), (cb,)), ((), ())), preferred_element_type=f32)


def sigmoid(v):
    return 0.5 * jnp.tanh(0.5 * v) + 0.5


def sub_norm(full):
    mean = jnp.mean(full, axis=0, keepdims=True)
    centered = full - mean
    inverse = lax.rsqrt(jnp.mean(centered * centered, axis=0, keepdims=True) + epsilon)
    return centered * inverse, inverse


def sub_norm_back(gain, scaled, inverse, grad):
    weighted = gain * grad
    first = jnp.mean(weighted, axis=0, keepdims=True)
    second = jnp.mean(weighted * scaled, axis=0, keepdims=True)
    return inverse * (weighted - first - scaled * second)


def gelu_both(value):
    cdf = 0.5 * (1.0 + lax.erf(value * (0.5**0.5)))
    density = jnp.exp(-0.5 * value * value) * (1.0 / math.sqrt(2.0 * math.pi))
    return value * cdf, cdf + value * density


def lane_sums(value):
    value = sum(value[:, at : at + 128] for at in range(0, value.shape[1], 128))
    ones = jnp.ones((8, value.shape[1]), f32)
    sums = lax.dot_general(
        ones,
        value,
        (((1,), (1,)), ((), ())),
        precision=lax.Precision.HIGHEST,
        preferred_element_type=f32,
    )
    return sums[:1]


def place_spec():
    return pl.BlockSpec(memory_space=pltpu.SMEM)


def whole_spec(a):
    zeros = (0,) * len(a.shape)
    return pl.BlockSpec(a.shape, lambda s: zeros)


def in_hbm(shape, dtype):
    return pltpu.HBM(shape, dtype)


def held(arrays):
    return [pltpu.with_memory_space_constraint(a, pltpu.HBM) for a in arrays]


def params(mib):
    return pltpu.CompilerParams(vmem_limit_bytes=mib * 2**20)


quick = pl.CostEstimate(flops=1, bytes_accessed=1, transcendentals=0)


def pack_kernel(first_row, rows, live_rows, place_ref, *refs):
    z, part = place_ref[0], 2 * place_ref[2] + place_ref[1]
    sems = refs[-1]
    outs = refs[-7:-3] if live_rows else refs[-5:-1]
    more = outs[0].shape[0] - rows
    copies = []
    for m in range(4):
        rows_of = refs[0].at[lax.bitwise_xor(z, m), pl.ds(first_row, rows)]
        copies.append(pltpu.make_async_copy(rows_of, outs[m].at[pl.ds(0, rows)], sems.at[m]))
    if more and not live_rows:
        for m in range(4):
            rows_of = refs[1].at[pl.ds(part * more, more)]
            copies.append(pltpu.make_async_copy(rows_of, outs[m].at[pl.ds(rows, more)], sems.at[4 + m]))
    for copy in copies:
        copy.start()
    if live_rows:
        lengths, present, node, node_cot, tri_in, gate, bias, tri_out, trans_in, trans_out = refs[1:11]
        extra, weights = refs[-3:-1]
        quarter, width = extra.shape[2:]
        position = lax.broadcasted_iota(jnp.int32, (1, width), 1)
        for crop in range(4):
            for n, ref in enumerate((node, node_cot)):
                value = ref[crop].astype(f32)
                extra[crop, 1 + n] = jnp.concatenate([value[:quarter], value[quarter:]], axis=1).astype(bf16)
            there = jnp.where(position < lengths[crop], present[crop : crop + 1], 0).astype(f32)
            extra[crop, 0] = jnp.broadcast_to(there, (quarter, width)).astype(bf16)
        parts = [tri_in[...], gate[...]]
        low = bias[...].astype(f32)
        parts.append(jnp.concatenate([low, jnp.zeros((32 - low.shape[0], width), f32)], axis=0).astype(bf16))
        parts += [tri_out[...], trans_in[...].astype(f32).T.astype(bf16), trans_out[...]]
        count = sum(part.shape[0] for part in parts)
        parts.append(jnp.zeros((quarter * weights.shape[0] - count, width), bf16))
        weights[...] = jnp.concatenate(parts, axis=0).reshape(weights.shape)
        for m in range(4):
            outs[m][rows : rows + 3] = extra[lax.bitwise_xor(z, m)]
            outs[m][rows + 3 :] = weights[pl.ds(place_ref[2] * (more - 3), more - 3)]
    for copy in copies:
        copy.wait()


def pack(place, source, first_row, rows, weights=None, first=None):
    _, _, quarter, width = source.shape
    vmem = pl.BlockSpec(memory_space=pltpu.VMEM)
    operands, specs, scratch, more = [place, *held([source])], [place_spec(), any_spec()], [], 0
    if first is not None:
        count = sum(a.shape[0] for a in first[4:]) + 32 - first[6].shape[0]
        count = -(-count // (2 * quarter)) * 2
        operands += first[:1] + held(first[1:])
        specs += [place_spec()] + [vmem] * (len(first) - 1)
        scratch = [pltpu.VMEM((4, 3, quarter, width), bf16), pltpu.VMEM((count, quarter, width), bf16)]
        more = 3 + count // 2
    elif weights is not None:
        operands += held([weights])
        specs.append(any_spec())
        more = weights.shape[0] // 4
    return pl.pallas_call(
        functools.partial(pack_kernel, first_row, rows, first is not None),
        in_specs=specs,
        out_specs=[vmem] * 4,
        out_shape=[in_hbm((rows + more, quarter, width), bf16)] * 4,
        scratch_shapes=scratch + [pltpu.SemaphoreType.DMA((8,))],
        compiler_params=params(24),
        cost_estimate=quick,
        name="pack",
    )(*operands)


def project_kernel(
    place_ref, p0, p1, p2, p3, wall_ref, mask_ref, gain_ref, tri_ref, norm_ref, pair_ref, bias_ref, pc, w_s, wb_s, bs, *kept_s
):
    pieces = (p0, p1, p2, p3)
    rows, quarter, width = p0.shape
    chans = 4 * quarter
    z = place_ref[0]
    gain = jnp.concatenate([gain_ref[...]] * group, axis=1)
    heads = bias_ref.shape[0]
    tri_rows = 8 * quarter

    @pl.when(pl.program_id(0) == 0)
    def _():
        for g in range(4):
            w_s[g * tri_rows : (g + 1) * tri_rows] = wall_ref[lax.bitwise_xor(z, g), :tri_rows]
            wb_s[g * 16 : (g + 1) * 16] = wall_ref[lax.bitwise_xor(z, g), 10 * quarter : 10 * quarter + 16]

    for m in range(4):
        pc[lax.bitwise_xor(z, m)] = pieces[m][...]

    @pl.loop(0, rows // group)
    def _(step):
        first = step * group

        def wide(get):
            return jnp.concatenate([get(first + n) for n in range(group)], axis=1)

        rows_in = [jnp.concatenate([pc[q, first + n] for q in range(4)], axis=0) for n in range(group)]
        for n in range(group):
            pair_ref[first + n] = rows_in[n]
        scaled, _ = sub_norm(jnp.concatenate(rows_in, axis=1).astype(f32))
        low = (scaled * gain).astype(bf16)
        for n in range(group):
            norm_ref[first + n] = low[:, n * width : (n + 1) * width]
        mask = wide(lambda r: mask_ref[pl.ds(r, 1), :])
        bias = dot(wb_s[...], low)
        for n in range(group):
            for g in range(4):
                at = (first + n) * heads + g * (heads // 4)
                bs[pl.ds(at, heads // 4), :] = bias[g * 16 : g * 16 + heads // 4, n * width : (n + 1) * width]
        for g in range(4):
            proj = dot(w_s[g * tri_rows : (g + 1) * tri_rows], low)
            for k in range(4):
                gate = proj[(2 * k) * quarter : (2 * k + 1) * quarter]
                value = proj[(2 * k + 1) * quarter : (2 * k + 2) * quarter]
                kept = sigmoid(gate) * value * mask
                for n in range(group):
                    at = (first + n) * (chans + 1) + g * quarter
                    kept_s[ORDER[k]][pl.ds(at, quarter), :] = kept[:, n * width : (n + 1) * width]

    @pl.loop(0, chans, unroll=32)
    def _(h):
        for k in range(4):
            tri_ref[k, h] = kept_s[k][pl.ds(h, rows, stride=chans + 1), :].astype(bf16)

    for h in range(heads):
        bias_ref[h] = bs[pl.ds(h, rows, stride=heads), :]


def any_spec():
    return pl.BlockSpec(memory_space=pl.ANY)


def project(place, pieces, wall, mask_rows, gain, heads, rows, first_row, step_rows=16):
    _, quarter, width = pieces[0].shape
    chans = 4 * quarter
    start = first_row // step_rows
    row_spec = pl.BlockSpec((step_rows, chans, width), lambda i: (i, 0, 0))
    pair = in_hbm((rows, chans, width), bf16)
    return pl.pallas_call(
        project_kernel,
        grid=(rows // step_rows,),
        in_specs=[place_spec()]
        + [pl.BlockSpec((step_rows, quarter, width), lambda i: (i, 0, 0))] * 4
        + [whole_spec(wall), pl.BlockSpec((step_rows, width), lambda i: (i + start, 0)), whole_spec(gain)],
        out_specs=[
            pl.BlockSpec((4, chans, step_rows, width), lambda i: (0, 0, i, 0)),
            row_spec,
            row_spec,
            pl.BlockSpec((heads, step_rows, width), lambda i: (0, i, 0)),
        ],
        out_shape=[
            in_hbm((4, chans, rows, width), bf16),
            pair,
            pair,
            jax.ShapeDtypeStruct((heads, rows, width), f32),
        ],
        scratch_shapes=[
            pltpu.VMEM((4, step_rows, quarter, width), bf16),
            pltpu.VMEM((8 * chans, chans), bf16),
            pltpu.VMEM((64, chans), bf16),
            pltpu.VMEM((step_rows * heads, width), f32),
        ]
        + [pltpu.VMEM((step_rows * (chans + 8), width), f32)] * 4,
        compiler_params=params(40),
        cost_estimate=quick,
        name="project",
    )(place, *pieces, wall, mask_rows, gain)


def in_core_order(core, mine, far):
    first = core == 0
    blocks = [jnp.where(first, a, b) for a, b in zip(mine, far)]
    return jnp.concatenate(blocks + [jnp.where(first, b, a) for a, b in zip(mine, far)], axis=0)


def tri_forward_kernel(count, place_ref, *refs):
    core = place_ref[1]
    mine, far, out_ref = refs[:count], refs[count : 2 * count], refs[-1]
    rows = out_ref.shape[2]

    @pl.loop(0, out_ref.shape[1], unroll=32)
    def _(h):
        left = jnp.concatenate([t[OUT_LEFT, h] for t in mine], axis=0)
        right = in_core_order(core, [t[OUT_RIGHT, h] for t in mine], [t[OUT_RIGHT, h] for t in far])
        out_ref[0, h] = dot(left, right, 1, 1).astype(bf16)
        left = jnp.concatenate([t[IN_LEFT, h] for t in mine + far], axis=0)
        right = jnp.concatenate([t[IN_RIGHT, h] for t in mine + far], axis=0)
        both = dot(left, right, 0, 0)
        out_ref[1, h] = jnp.where(core == 0, both[:rows], both[rows:]).astype(bf16)


def tri_forward(place, mine, far, step_h=32):
    _, chans, rows, width = mine[0].shape
    rows = rows * len(mine)
    spec = pl.BlockSpec((4, step_h) + mine[0].shape[2:], lambda s: (0, s, 0, 0))
    far_spec = pl.BlockSpec((3, step_h) + mine[0].shape[2:], lambda s: (0, s, 0, 0))
    return pl.pallas_call(
        functools.partial(tri_forward_kernel, len(mine)),
        grid=(chans // step_h,),
        in_specs=[place_spec()] + [spec] * len(mine) + [far_spec] * len(mine),
        out_specs=pl.BlockSpec((2, step_h, rows, width), lambda s: (0, s, 0, 0)),
        out_shape=in_hbm((2, chans, rows, width), bf16),
        compiler_params=params(40),
        cost_estimate=quick,
        name="tri_forward",
    )(place, *held(mine), *far)


def middle_kernel(
    fresh, place_ref, tri_ref, pair_ref, norm_ref, c0, c1, c2, c3, gain_tri_ref, gain_trans_ref, wall_ref, rest_ref, prev_ref,
    p0, p1, p2, p3, mid_ref, gate_ref, gtri_ref, gw_out_ref,
    gw_ref, tri_s0, tri_s1, wg_s, wto_s, wti_s, wout_s, wout_t, wti_t, wto_t, gg_trans_s, gg_tri_s,
    cot_s, pc, po, tn0, tn1, nm, hid, gp, gb0, gb1, gs0, gs1,
):
    z = place_ref[0]
    step = pl.program_id(0)
    rows, chans, width = pair_ref.shape
    quarter = chans // 4
    cots, outs = (c0, c1, c2, c3), (p0, p1, p2, p3)
    tris, tns, gbs, gss = (tri_s0, tri_s1), (tn0, tn1), (gb0, gb1), (gs0, gs1)
    gains_at = 2 * quarter + 2 * chans

    @pl.when(step == 0)
    def _():
        for g in range(4):
            for d in range(2):
                wg_s[d * chans + g * quarter : d * chans + (g + 1) * quarter] = wall_ref[
                    lax.bitwise_xor(z, g), (8 + d) * quarter : (9 + d) * quarter
                ]
                wto_s[d, g * quarter : (g + 1) * quarter] = rest_ref[lax.bitwise_xor(z, g), d * quarter : (d + 1) * quarter]
            wti_s[g * chans : (g + 1) * chans] = rest_ref[lax.bitwise_xor(z, g), 2 * quarter : 2 * quarter + chans]
            wout_s[g * chans : (g + 1) * chans] = rest_ref[lax.bitwise_xor(z, g), 2 * quarter + chans : gains_at]
        for f in range(4):
            block = slice(f * chans, (f + 1) * chans)
            wout_t[:, block] = wout_s[block].astype(f32).T.astype(bf16)
            wti_t[:, block] = wti_s[block].astype(f32).T.astype(bf16)
        for d in range(2):
            wto_t[d] = wto_s[d].astype(f32).T.astype(bf16)
        gw_ref[...] = jnp.zeros_like(gw_ref) if fresh else prev_ref[...]
        gg_trans_s[...] = jnp.zeros_like(gg_trans_s)
        gg_tri_s[...] = jnp.zeros_like(gg_tri_s)

    @pl.loop(0, chans, unroll=32)
    def _(h):
        for d in range(2):
            tris[d][pl.ds(h * (rows + 1), rows), :] = tri_ref[d, h].astype(f32)

    gain_trans = jnp.concatenate([gain_trans_ref[...]] * group, axis=1)
    gain_tri = [jnp.concatenate([gain_tri_ref[d]] * group, axis=1) for d in range(2)]

    for m in range(4):
        pc[lax.bitwise_xor(z, m)] = cots[m][...]

    @pl.loop(0, rows // group)
    def _(s2):
        first = s2 * group
        lanes = pl.ds(pl.multiple_of(first * width, group * width), group * width)

        def wide(get):
            return jnp.concatenate([get(first + n) for n in range(group)], axis=1)

        def cut(value, n):
            return value[:, n * width : (n + 1) * width]

        inner = wide(lambda r: norm_ref[r])
        gate = sigmoid(dot(wg_s[...], inner))
        total = wide(lambda r: pair_ref[r]).astype(f32)
        kept = []
        for d in range(2):
            tri = wide(lambda r: tris[d][pl.ds(r, chans, stride=rows + 1), :])
            scaled, inverse = sub_norm(tri)
            low = (scaled * gain_tri[d]).astype(bf16)
            tns[d][:, lanes] = low
            branch = dot(wto_s[d], low)
            total = total + gate[d * chans : (d + 1) * chans] * branch
            kept.append((scaled, inverse, branch))
        scaled, inverse = sub_norm(total)
        low = (scaled * gain_trans).astype(bf16)
        nm[:, lanes] = low
        cot = wide(lambda r: jnp.concatenate([pc[q, r] for q in range(4)], axis=0))
        cot_s[:, lanes] = cot
        acts, backs = [], []
        for f in range(4):
            block = slice(f * chans, (f + 1) * chans)
            act, slope = gelu_both(dot(wti_s[block], low))
            acts.append(act.astype(bf16))
            backs.append((dot(wout_s[block], cot) * slope).astype(bf16))
            hid[block, lanes] = acts[-1]
            gp[block, lanes] = backs[-1]
        out = (total + dot(wout_t[...], jnp.concatenate(acts, axis=0))).astype(bf16)
        for n in range(group):
            for q in range(4):
                po[q, first + n] = cut(out[q * quarter : (q + 1) * quarter], n)
        back = dot(wti_t[...], jnp.concatenate(backs, axis=0))
        gg_trans_s[...] += back * scaled
        grad = cot.astype(f32) + sub_norm_back(gain_trans, scaled, inverse, back)
        for n in range(group):
            mid_ref[first + n] = cut(grad, n).astype(bf16)
        for d in range(2):
            scaled, inverse, branch = kept[d]
            sig = gate[d * chans : (d + 1) * chans]
            grad_branch = sig * grad
            grad_gate = (grad_branch * branch * (1.0 - sig)).astype(bf16)
            grad_branch = grad_branch.astype(bf16)
            for n in range(group):
                gate_ref[first + n, d * chans : (d + 1) * chans] = cut(grad_gate, n)
            gbs[d][:, lanes] = grad_branch
            back = dot(wto_t[d], grad_branch)
            gg_tri_s[d] += back * scaled
            out = sub_norm_back(gain_tri[d], scaled, inverse, back)
            for n in range(group):
                gss[d][pl.ds(first + n, chans, stride=rows + 1), :] = cut(out, n)

    for m in range(4):
        outs[m][...] = po[lax.bitwise_xor(z, m)]
    gw_out = dot(hid[...], cot_s[...], 1, 1)
    gw_in = dot(gp[...], nm[...], 1, 1)
    for g in range(4):
        at = 2 * quarter
        gw_ref[g, at : at + chans] += gw_in[g * chans : (g + 1) * chans]
        gw_ref[g, at + chans : at + 2 * chans] += gw_out[g * chans : (g + 1) * chans]
    for d in range(2):
        gw_tri = dot(gbs[d][...], tns[d][...], 1, 1)
        for g in range(4):
            gw_ref[g, d * quarter : (d + 1) * quarter] += gw_tri[g * quarter : (g + 1) * quarter]

        @pl.loop(0, chans, unroll=32)
        def _(h):
            gtri_ref[d, h] = gss[d][pl.ds(h * (rows + 1), rows), :].astype(bf16)

    @pl.when(step == pl.num_programs(0) - 1)
    def _():
        for n, total in enumerate((gg_trans_s[...], gg_tri_s[0], gg_tri_s[1])):
            row = lane_sums(total)
            for g in range(4):
                gw_ref[g, gains_at + n : gains_at + n + 1] += row
        gw_out_ref[...] = gw_ref[...].astype(gw_out_ref.dtype)


def middle(place, tri, first_row, pair, norm, cots, gain_tri, gain_trans, wall, rest, prev, step_rows=16):
    rows, chans, width = pair.shape
    hidden, quarter = 4 * chans, chans // 4
    fresh = prev is None
    sums = in_hbm((4, 2 * quarter + 2 * chans + 16, chans), f32 if fresh else bf16)
    start = first_row // step_rows
    row_spec = pl.BlockSpec((step_rows, chans, width), lambda s: (s, 0, 0))
    piece_spec = pl.BlockSpec((step_rows, quarter, width), lambda s: (s, 0, 0))
    piece = in_hbm((rows, quarter, width), bf16)
    gate = in_hbm((rows, 2 * chans, width), bf16)
    lanes = step_rows * width
    operands = [place, *held([tri, pair, norm]), *cots, gain_tri, gain_trans, wall, rest]
    operands.append(gain_tri if fresh else prev)
    return pl.pallas_call(
        functools.partial(middle_kernel, fresh),
        grid=(rows // step_rows,),
        in_specs=[place_spec(), pl.BlockSpec((2, chans, step_rows, width), lambda s: (0, 0, s + start, 0)), row_spec, row_spec]
        + [piece_spec] * 4
        + [whole_spec(a) for a in operands[8:]],
        out_specs=[piece_spec] * 4
        + [
            row_spec,
            pl.BlockSpec((step_rows, 2 * chans, width), lambda s: (s, 0, 0)),
            pl.BlockSpec((2, chans, step_rows, width), lambda s: (0, 0, s, 0)),
            whole_spec(sums),
        ],
        out_shape=[piece] * 4
        + [
            in_hbm((rows, chans, width), bf16),
            gate,
            jax.ShapeDtypeStruct((2, chans, rows, width), bf16),
            sums,
        ],
        scratch_shapes=[pltpu.VMEM(sums.shape, f32)]
        + [pltpu.VMEM((chans * (step_rows + 1), width), f32)] * 2
        + [pltpu.VMEM((2 * chans, chans), bf16), pltpu.VMEM((2, chans, chans), bf16)]
        + [pltpu.VMEM((hidden, chans), bf16)] * 2
        + [pltpu.VMEM((chans, hidden), bf16)] * 2
        + [
            pltpu.VMEM((2, chans, chans), bf16),
            pltpu.VMEM((chans, group * width), f32),
            pltpu.VMEM((2, chans, group * width), f32),
            pltpu.VMEM((chans, lanes), bf16),
            pltpu.VMEM((4, step_rows, quarter, width), bf16),
            pltpu.VMEM((4, step_rows, quarter, width), bf16),
        ]
        + [pltpu.VMEM((chans, lanes), bf16)] * 3
        + [pltpu.VMEM((hidden, lanes), bf16)] * 2
        + [pltpu.VMEM((chans, lanes), bf16)] * 2
        + [pltpu.VMEM((chans * (step_rows + 1), width), f32)] * 2,
        compiler_params=params(56),
        cost_estimate=quick,
        name="middle",
    )(*operands)


def tri_backward_kernel(count, place_ref, *refs):
    core = place_ref[1]
    mine, far, gmine, gfar = (refs[n * count : (n + 1) * count] for n in range(4))
    out_ref = refs[-1]
    rows = out_ref.shape[2]

    def joined(a, k, h):
        return jnp.concatenate([t[k, h] for t in a], axis=0)

    @pl.loop(0, out_ref.shape[1], unroll=32)
    def _(h):
        right = in_core_order(core, [t[OUT_RIGHT, h] for t in mine], [t[0, h] for t in far])
        out_ref[0, h] = dot(joined(gmine, 0, h), right).astype(bf16)
        left = jnp.concatenate([t[OUT_LEFT, h] for t in mine] + [t[1, h] for t in far], axis=0)
        both = dot(joined(gmine + gfar, 0, h), left, 0, 0)
        out_ref[1, h] = jnp.where(core == 0, both[:rows], both[rows:]).astype(bf16)
        grad = in_core_order(core, [t[1, h] for t in gmine], [t[1, h] for t in gfar])
        out_ref[2, h] = dot(joined(mine, IN_RIGHT, h), grad, 1, 1).astype(bf16)
        out_ref[3, h] = dot(joined(mine, IN_LEFT, h), grad).astype(bf16)


def tri_backward(place, mine, far, gmine, gfar, step_h=32):
    _, chans, rows, width = mine[0].shape
    total = rows * len(mine)
    spec = pl.BlockSpec((4, step_h, rows, width), lambda s: (0, s, 0, 0))
    far_spec = pl.BlockSpec((2, step_h, rows, width), lambda s: (1, s, 0, 0))
    gspec = pl.BlockSpec((2, step_h, rows, width), lambda s: (0, s, 0, 0))
    operands = [place, *held(mine), *held(far), *held(gmine), *gfar]
    return pl.pallas_call(
        functools.partial(tri_backward_kernel, len(mine)),
        grid=(chans // step_h,),
        in_specs=[place_spec()] + [spec] * len(mine) + [far_spec] * len(mine) + [gspec] * (2 * len(mine)),
        out_specs=pl.BlockSpec((4, step_h, total, width), lambda s: (0, s, 0, 0)),
        out_shape=in_hbm((4, chans, total, width), bf16),
        compiler_params=params(40),
        cost_estimate=quick,
        name="tri_backward",
    )(*operands)


def finish_kernel(
    i_steps, fresh, place_ref, sum_ref, pair_ref, norm_ref, mid_ref, gate_ref, score_ref, mask_ref, gain_ref, wall_ref, prev_ref, extra_ref,
    p0, p1, p2, p3, gw_out_ref,
    gw_ref, s0, s1, s2_, s3, wall_t, w_s, gall, nb, po, sc_s, gg_s,
):
    z = place_ref[0]
    step = pl.program_id(0)
    rows, chans, width = pair_ref.shape
    quarter = chans // 4
    sums, outs = (s0, s1, s2_, s3), (p0, p1, p2, p3)
    block_rows = wall_ref.shape[1]
    packed = 4 * block_rows
    heads = score_ref.shape[1]
    here = heads // 4

    @pl.when(step == 0)
    def _():
        for g in range(4):
            gall[g * block_rows : (g + 1) * block_rows, :chans] = wall_ref[lax.bitwise_xor(z, g)]
            w_s[g * 8 * quarter : (g + 1) * 8 * quarter] = wall_ref[lax.bitwise_xor(z, g), : 8 * quarter]
        for f in range(0, packed, 128):
            end = min(f + 128, packed)
            wall_t[:, f:end] = gall[f:end, :chans].astype(f32).T.astype(bf16)
        gw_ref[...] = jnp.zeros_like(gw_ref) if fresh else prev_ref[...]
        gg_s[...] = jnp.zeros_like(gg_s)
        sc_s[...] = jnp.zeros_like(sc_s)

    @pl.when(step < i_steps)
    def _():
        @pl.loop(0, chans, unroll=32)
        def _(h):
            for k in range(4):
                sums[k][pl.ds(h * (rows + 1), rows), :] = sum_ref[k, h].astype(f32)

        gain = jnp.concatenate([gain_ref[...]] * group, axis=1)

        @pl.loop(0, rows // group)
        def _(s2):
            first = s2 * group
            lanes = pl.ds(pl.multiple_of(first * width, group * width), group * width)

            def wide(get):
                return jnp.concatenate([get(first + n) for n in range(group)], axis=1)

            def cut(value, n):
                return value[:, n * width : (n + 1) * width]

            inner = wide(lambda r: norm_ref[r])
            nb[:, lanes] = inner
            mask = wide(lambda r: mask_ref[pl.ds(r, 1), :])
            parts = []
            for g in range(4):
                proj = dot(w_s[g * 8 * quarter : (g + 1) * 8 * quarter], inner)
                for k in range(4):
                    gate = proj[(2 * k) * quarter : (2 * k + 1) * quarter]
                    value = proj[(2 * k + 1) * quarter : (2 * k + 2) * quarter]
                    grad = wide(lambda r: sums[k][pl.ds(g * quarter * (rows + 1) + r, quarter, stride=rows + 1), :])
                    sig = sigmoid(gate)
                    back = grad * mask * sig
                    parts.append((back * value * (1.0 - sig)).astype(bf16))
                    parts.append(back.astype(bf16))
                for d in range(2):
                    at = d * chans + g * quarter
                    parts.append(wide(lambda r: gate_ref[r, at : at + quarter]))
                for n in range(group):
                    sc_s[g * 16 : g * 16 + here, n * width : (n + 1) * width] = score_ref[
                        first + n, g * here : (g + 1) * here
                    ]
                parts.append(sc_s[g * 16 : (g + 1) * 16].astype(bf16))
                parts.append(jnp.zeros((block_rows - 10 * quarter - 16, group * width), bf16))
            every = jnp.concatenate(parts, axis=0)
            gall[:, lanes] = every
            back = dot(wall_t[...], every)
            scaled, inverse = sub_norm(wide(lambda r: pair_ref[r]).astype(f32))
            gg_s[...] += back * scaled
            out = wide(lambda r: mid_ref[r]).astype(f32) + sub_norm_back(gain, scaled, inverse, back)
            out = out.astype(bf16)
            for n in range(group):
                for q in range(4):
                    po[q, first + n] = cut(out[q * quarter : (q + 1) * quarter], n)

        for m in range(4):
            outs[m][...] = po[lax.bitwise_xor(z, m)]
        gw_ref[...] += dot(gall[...], nb[...], 1, 1)

    @pl.when(step == i_steps - 1)
    def _():
        row = lane_sums(gg_s[...])
        for g in range(4):
            at = (g + 1) * block_rows - 1
            gw_ref[at : at + 1] += row
        gw_out_ref[...] = gw_ref[...].astype(gw_out_ref.dtype)

    @pl.when(step == i_steps)
    def _():
        for m in range(4):
            outs[m][: extra_ref.shape[1]] = extra_ref[m]


def finish(place, sums, first_row, pair, norm, mid, gate, scores, mask_rows, gain, wall, prev, extra, step_rows=16):
    rows, chans, width = pair.shape
    quarter = chans // 4
    heads = scores.shape[1]
    packed = 4 * wall.shape[1]
    i_steps = rows // step_rows
    fresh = prev is None
    start = first_row // step_rows
    last = first_row + rows == mask_rows.shape[0]
    total = in_hbm((packed, chans), bf16 if last else f32)

    def at(s):
        return jnp.minimum(s, i_steps - 1)

    if fresh:
        prev = gain
    row_spec = pl.BlockSpec((step_rows, chans, width), lambda s: (at(s), 0, 0))
    piece_spec = pl.BlockSpec((step_rows, quarter, width), lambda s: (s, 0, 0))
    piece = in_hbm((rows + (extra.shape[1] if last else 0), quarter, width), bf16)
    lanes = step_rows * width
    return pl.pallas_call(
        functools.partial(finish_kernel, i_steps, fresh),
        grid=(i_steps + (1 if last else 0),),
        in_specs=[place_spec(), pl.BlockSpec((4, chans, step_rows, width), lambda s: (0, 0, at(s) + start, 0))]
        + [row_spec] * 3
        + [
            pl.BlockSpec((step_rows, 2 * chans, width), lambda s: (at(s), 0, 0)),
            pl.BlockSpec((step_rows, heads, width), lambda s: (at(s) + start, 0, 0)),
            pl.BlockSpec((step_rows, width), lambda s: (at(s) + start, 0)),
        ]
        + [whole_spec(a) for a in (gain, wall, prev, extra)],
        out_specs=[piece_spec] * 4 + [whole_spec(total)],
        out_shape=[piece] * 4 + [total],
        scratch_shapes=[pltpu.VMEM((packed, chans), f32)]
        + [pltpu.VMEM((chans * (step_rows + 1), width), f32)] * 4
        + [
            pltpu.VMEM((chans, packed), bf16),
            pltpu.VMEM((8 * chans, chans), bf16),
            pltpu.VMEM((packed, lanes), bf16),
            pltpu.VMEM((chans, lanes), bf16),
            pltpu.VMEM((4, step_rows, quarter, width), bf16),
            pltpu.VMEM((64, group * width), f32),
            pltpu.VMEM((chans, group * width), f32),
        ],
        compiler_params=params(56),
        cost_estimate=quick,
        name="finish",
    )(place, *held([sums, pair, norm, mid, gate]), scores, mask_rows, gain, wall, prev, extra)


def assemble_kernel(rows, count, nodes, place_ref, *refs):
    pieces, (out_ref, *node_refs) = refs[: 4 * count], refs[4 * count : 4 * count + (3 if nodes else 1)]
    sems, z = refs[-1], place_ref[0]
    copies = []
    for m in range(4):
        crop = lax.bitwise_xor(z, m)
        for n in range(count):
            source, target = pieces[4 * n + m], out_ref.at[crop, pl.ds(n * rows, rows)]
            copies.append(pltpu.make_async_copy(source.at[pl.ds(0, rows)], target, sems.at[m, n]))
        if nodes:
            source = pieces[4 * (count - 1) + m].at[pl.ds(rows, 2)]
            copies.append(pltpu.make_async_copy(source, refs[-2].at[crop], sems.at[m, count]))
    for copy in copies:
        copy.start()
    for copy in copies:
        copy.wait()
    for n, ref in enumerate(node_refs):
        for crop in range(4):
            value = refs[-2][crop, n]
            half, width = value.shape[0], value.shape[1] // 2
            ref[crop, :half] = value[:, :width]
            ref[crop, half:] = value[:, width:]


def assemble(place, chunks, rows, nodes):
    _, quarter, width = chunks[0][0].shape
    count = len(chunks)
    vmem = pl.BlockSpec(memory_space=pltpu.VMEM)
    shapes = [jax.ShapeDtypeStruct((4, rows * count, quarter, width), bf16)]
    scratch = [pltpu.SemaphoreType.DMA((4, count + 1))]
    if nodes:
        shapes += [jax.ShapeDtypeStruct((4, 2 * quarter, width // 2), bf16)] * 2
        scratch = [pltpu.VMEM((4, 2, quarter, width), bf16)] + scratch
    return pl.pallas_call(
        functools.partial(assemble_kernel, rows, count, nodes),
        in_specs=[place_spec()] + [any_spec()] * (4 * count),
        out_specs=[any_spec()] + [vmem] * (len(shapes) - 1),
        out_shape=shapes,
        scratch_shapes=scratch,
        compiler_params=params(16),
        cost_estimate=quick,
        name="assemble",
    )(place, *[piece for chunk in chunks for piece in chunk])


def unpack_kernel(early, node_rows, place_ref, own, far, tri_in, gate, bias, tri_out, trans_in, trans_out, qkv, attn, node_in, node_out, gain_pair, gain_trans, gain_tri, gain_node, gain_node_trans):
    first = place_ref[1] == 0
    own, far = own[...].astype(f32), far[...].astype(f32)
    a, b = jnp.where(first, own[:node_rows], far[:node_rows]), jnp.where(first, far[:node_rows], own[:node_rows])
    last = own[early:] + far[early:]
    quarter = tri_out.shape[1]
    chans = trans_in.shape[0]
    wide = jnp.concatenate([a, b], axis=1)
    rest = own[node_rows:early] + far[node_rows:early]
    for d in range(2):
        for n in range(4):
            at = (4 * d + n) * quarter
            tri_in[d, n] = last[at : at + quarter]
        gate[d] = last[(8 + d) * quarter : (9 + d) * quarter]
        tri_out[d] = rest[d * quarter : (d + 1) * quarter]
    bias[...] = last[10 * quarter : 10 * quarter + bias.shape[0]]
    at = 2 * quarter
    trans_in[...] = rest[at : at + chans].T
    trans_out[...] = rest[at + chans : at + 2 * chans]
    at = at + 2 * chans
    z = lax.bitwise_xor(place_ref[0], 3)

    def own_block(rows, size):
        blocks = [rows[:, g * size : (g + 1) * size] for g in range(4)]
        low, high = jnp.where(z == 0, blocks[0], blocks[1]), jnp.where(z == 2, blocks[2], blocks[3])
        return jnp.where(z < 2, low, high)

    gain_pair[...] = own_block(last[last.shape[0] - 8 :], quarter)[7:]
    gains = own_block(rest[at : at + 8], quarter)
    gain_trans[...], gain_tri[...] = gains[:1], gains[1:3]
    size = qkv.shape[1]
    for n in range(3):
        qkv[n] = wide[n * size : (n + 1) * size]
    at = 3 * size
    attn[...] = wide[at : at + size]
    at = at + size
    size = node_in.shape[0]
    node_in[...] = wide[at : at + size].T
    node_out[...] = wide[at + size : at + 2 * size]
    at = at + 2 * size
    gains = own_block(wide[at : at + 8], 2 * quarter)
    gain_node[...], gain_node_trans[...] = gains[:1], gains[1:2]


def unpack(place, own, far, early, node_rows, heads):
    chans = own.shape[1]
    quarter, nodes = chans // 4, 2 * chans
    shapes = [
        (2, 4, quarter, chans), (2, quarter, chans), (heads, chans), (2, quarter, chans), (chans, chans), (chans, chans),
        (3, nodes // 4, nodes), (nodes // 4, nodes), (nodes, nodes), (nodes, nodes),
        (1, quarter), (1, quarter), (2, quarter), (1, nodes // 4), (1, nodes // 4),
    ]
    vmem = pl.BlockSpec(memory_space=pltpu.VMEM)
    return pl.pallas_call(
        functools.partial(unpack_kernel, early, node_rows),
        in_specs=[place_spec()] + [vmem] * 2,
        out_specs=[vmem] * len(shapes),
        out_shape=[jax.ShapeDtypeStruct(shape, f32) for shape in shapes],
        compiler_params=params(32),
        cost_estimate=quick,
        name="unpack",
    )(place, own, far)


def node_kernel(place_ref, bias_ref, bias_far, live_ref, gain_ref, gain_mid_ref, near_w, far_w,
                sent_ref, score_ref, gw_ref, w_all, att, gqkv):
    z, core, x = place_ref[0], place_ref[1], place_ref[2]
    first = core == 0
    groups, packed, _ = gw_ref.shape
    half_rows = bias_ref.shape[1]
    length, nodes = 2 * half_rows, gain_ref.shape[1]
    quarter = nodes // groups
    fold = quarter // 2
    count = near_w.shape[1] // 2 - fold
    for m in range(groups):
        for ref, side in ((near_w, core), (far_w, 1 - core)):
            for at, other in ((0, x), (count, 1 - x)):
                here = pl.ds(pl.multiple_of((2 * side + other) * count, count), count)
                w_all[lax.bitwise_xor(z, m), here] = ref[m, at:at + count]
    heads = bias_ref.shape[0]
    head_dim = nodes // heads
    hidden = nodes
    scale = 1.0 / math.sqrt(head_dim)

    def weight(at, size):
        return jnp.concatenate(
            [jnp.concatenate([w_all[g, half * packed + at:half * packed + at + size] for half in range(2)], axis=1) for g in range(groups)], axis=0)

    def ordered(mine, far):
        return jnp.concatenate([jnp.where(first, mine, far), jnp.where(first, far, mine)], axis=0)

    def rows(value):
        return jnp.where(first, value[:half_rows], value[half_rows:])

    def parts(value):
        centered = value - jnp.mean(value, axis=1, keepdims=True)
        inverse = lax.rsqrt(jnp.mean(centered * centered, axis=1, keepdims=True) + epsilon)
        return centered * inverse, inverse

    def back(gain, scaled, inverse, grad):
        weighted = gain * grad
        first_mean = jnp.mean(weighted, axis=1, keepdims=True)
        second_mean = jnp.mean(weighted * scaled, axis=1, keepdims=True)
        return inverse * (weighted - first_mean - scaled * second_mean)

    def own_half(value):
        return jnp.where(first, value[:, :128], value[:, 128:]).astype(bf16)

    def keep(at, value):
        size = value.shape[0] // groups
        for g in range(groups):
            gw_ref[g, at:at + size] = own_half(value[g * size:(g + 1) * size])

    def gain_row(grad, scaled):
        return jnp.sum(grad * scaled, axis=0, keepdims=True)


    def unfolded(ref, n):
        rows_of = slice(2 * count + n * fold, 2 * count + (n + 1) * fold)
        parts = [ref[lax.bitwise_xor(z, g), rows_of].astype(f32) for g in range(groups)]
        half = parts[0].shape[1] // 2
        return jnp.concatenate([jnp.concatenate([v[:, :half], v[:, half:]], axis=0) for v in parts], axis=1)

    def sent(n, value):
        for g in range(groups):
            part = value[:, g * quarter:(g + 1) * quarter]
            half = part.shape[0] // 2
            sent_ref[lax.bitwise_xor(z, g), n] = jnp.concatenate([part[:half], part[half:]], axis=1).astype(bf16)

    node_in = ordered(unfolded(near_w, 0), unfolded(far_w, 0))
    cot = ordered(unfolded(near_w, 1), unfolded(far_w, 1)).astype(bf16)
    scaled_in, inverse_in = parts(node_in)
    low_in = (scaled_in * gain_ref[...]).astype(bf16)
    q, k, v = (dot(low_in, weight(g * quarter, quarter), 1, 1).astype(bf16) for g in range(3))
    lane = lax.broadcasted_iota(jnp.int32, (1, nodes), 1)
    key_live = live_ref[...] > 0.5

    def of_head(value, h):
        here = (lane >= h * head_dim) & (lane < (h + 1) * head_dim)
        return jnp.where(here, value, jnp.zeros_like(value))

    def probs_of(h):
        raw = dot(of_head(q, h), k, 1, 1) * scale + ordered(bias_ref[h], bias_far[h])
        scores = jnp.where(key_live, raw, -1e9)
        exps = jnp.exp(scores - jnp.max(scores, axis=1, keepdims=True))
        return exps / jnp.sum(exps, axis=1, keepdims=True)

    total = jnp.zeros((length, nodes), f32)
    for h in range(heads):
        probs = probs_of(h)
        att[h] = probs
        total = total + dot(probs.astype(bf16), of_head(v, h))
    attn = total.astype(bf16)
    at_a, at_i, at_o = 3 * quarter, 4 * quarter, 4 * quarter + hidden
    mid = node_in + dot(attn, weight(at_a, quarter), 1, 1)
    scaled_mid, inverse_mid = parts(mid)
    low_mid = (scaled_mid * gain_mid_ref[...]).astype(bf16)
    out = mid
    grad = jnp.zeros((length, nodes), f32)
    for g in range(groups):
        w_in = jnp.concatenate([w_all[g, half * packed + at_i:half * packed + at_i + hidden] for half in range(2)], axis=1)
        w_out = jnp.concatenate([w_all[g, half * packed + at_o:half * packed + at_o + hidden] for half in range(2)], axis=1)
        act, slope = gelu_both(dot(low_mid, w_in, 1, 1))
        act = act.astype(bf16)
        out = out + dot(act, w_out)
        grad_pre = (dot(cot, w_out, 1, 1) * slope).astype(bf16)
        grad = grad + dot(grad_pre, w_in)
        gi, go = dot(grad_pre, low_mid, 0, 0), dot(act, cot, 0, 0)
        gw_ref[g, at_i:at_i + hidden] = own_half(gi)
        gw_ref[g, at_o:at_o + hidden] = own_half(go)
    sent(0, rows(out))
    mid_row = gain_row(grad, scaled_mid)
    grad_mid = cot.astype(f32) + back(gain_mid_ref[...], scaled_mid, inverse_mid, grad)
    grad_low = grad_mid.astype(bf16)
    keep(at_a, dot(grad_low, attn, 0, 0))
    grad_attn = dot(grad_low, weight(at_a, quarter)).astype(bf16)
    for g in range(3):
        gqkv[g] = jnp.zeros((length, nodes), f32)
    for h in range(heads):
        probs = att[h]
        grad_probs = dot(of_head(grad_attn, h), v, 1, 1)
        delta = jnp.sum(probs * grad_probs, axis=1, keepdims=True)
        scores = probs * (grad_probs - delta)
        score_ref[:, h, :] = rows(scores)
        scores = scores.astype(bf16)
        gqkv[0] += dot(scores, of_head(k, h))
        gqkv[1] += dot(scores, of_head(q, h), 0, 0)
        gqkv[2] += dot(probs.astype(bf16), of_head(grad_attn, h), 0, 0)
    grad = jnp.zeros((length, nodes), f32)
    for g, factor in enumerate((scale, scale, 1.0)):
        low = (gqkv[g] * factor).astype(bf16)
        keep(g * quarter, dot(low, low_in, 0, 0))
        grad = grad + dot(low, weight(g * quarter, quarter))
    tail = jnp.concatenate([gain_row(grad, scaled_in), mid_row, jnp.zeros((14, nodes), f32)], axis=0)
    for g in range(groups):
        gw_ref[g, packed - 16:] = own_half(tail)
    sent(1, rows(grad_mid + back(gain_ref[...], scaled_in, inverse_in, grad)))

def node_track(place, bias, bias_far, live, gain, gain_mid, near_w, far_w, rows):
    half_rows, length = bias.shape[1], live.shape[1]
    nodes = gain.shape[1]
    heads = bias.shape[0]
    arrays = (bias, bias_far, live, gain, gain_mid, near_w, far_w)
    shapes = [
        jax.ShapeDtypeStruct((near_w.shape[0], 2, half_rows // 2, 128), bf16),
        jax.ShapeDtypeStruct((half_rows, heads, length), f32),
        jax.ShapeDtypeStruct((near_w.shape[0], rows, 128), bf16),
    ]
    vmem = pl.BlockSpec(memory_space=pltpu.VMEM)
    return pl.pallas_call(
        node_kernel,
        in_specs=[pl.BlockSpec(memory_space=pltpu.SMEM)] + [vmem] * len(arrays),
        out_specs=[vmem] * len(shapes),
        out_shape=shapes,
        scratch_shapes=[pltpu.VMEM((near_w.shape[0], 2 * near_w.shape[1], 128), bf16), pltpu.VMEM((heads, length, length), f32), pltpu.VMEM((3, length, nodes), f32)],
        compiler_params=params(40),
        cost_estimate=quick,
        name="node_track",
    )(place, *arrays[:-2], *held(arrays[-2:]))


def shards_by_crop(
    pair,
    node,
    pair_cot,
    node_cot,
    lengths,
    present,
    gain_pair,
    w_tri_in,
    w_out_gate,
    gain_tri,
    w_tri_out,
    gain_trans,
    w_trans_in,
    w_trans_out,
    w_bias,
    gain_node,
    w_qkv,
    w_attn_out,
    gain_node_trans,
    w_node_in,
    w_node_out,
):
    groups = lax.axis_size(CHAN)
    rows_here = pair.shape[1]
    chans = groups * pair.shape[2]
    crop_len = pair.shape[3]
    nodes = groups * node.shape[2]
    heads = groups * w_bias.shape[1]
    quarter, node_quarter = chans // groups, nodes // groups
    z = lax.axis_index(CHAN)
    core = lax.axis_index(DP) % 2
    x = lax.axis_index(ROWS)
    y = lax.axis_index(DP) // 2
    far_z = z ^ (groups - 1)
    place = jnp.stack([far_z, core, x, y]).astype(jnp.int32)
    mesh_shape = (lax.axis_size(DP), lax.axis_size(ROWS), groups)

    def device(d, r, c):
        return (d * mesh_shape[1] + r) * groups + c

    def home_perm(m):
        return [
            (device(d, r, c), device(d - d % 2 + r, d % 2, c ^ m))
            for d in range(mesh_shape[0])
            for r in range(mesh_shape[1])
            for c in range(groups)
        ]

    core_pairs = [(d, d ^ 1) for d in range(mesh_shape[0])]
    row_pairs = [(0, 1), (1, 0)]

    def send_home(pieces):
        return [
            lax.ppermute(piece, (DP, ROWS, CHAN), home_perm(n ^ (groups - 1)))
            for n, piece in enumerate(pieces)
        ]

    def to_chan(value, m):
        return lax.ppermute(value, CHAN, [(c, c ^ m) for c in range(groups)])

    def swap_core(value):
        return lax.ppermute(value, DP, core_pairs)

    def pick(value, index):
        return lax.dynamic_index_in_dim(value, index, 0, keepdims=False)

    def own_rows(value, axis):
        return lax.dynamic_slice_in_dim(value, core * rows_here, rows_here, axis)

    def packed(parts):
        return jnp.concatenate([part.reshape(-1, chans) for part in parts])

    def split(value):
        return jnp.concatenate([value[:, :chans], value[:, chans:]])

    chunk = min(32, rows_here)
    tied = lax.optimization_barrier

    def blocks(rows):
        rows = jnp.pad(rows, ((0, -rows.shape[0] % (4 * quarter)), (0, 0)))
        return rows.reshape(-1, quarter, chans)

    def with_far(own, far, side):
        return jnp.concatenate([jnp.where(side == 0, own, far), jnp.where(side == 0, far, own)], axis=1)

    def swap_rows(value):
        return lax.ppermute(value, ROWS, row_pairs)

    node_rest = jnp.concatenate(
        [w_qkv.transpose(0, 2, 1).reshape(-1, nodes), w_attn_out.T, w_node_in.T, w_node_out]
    )
    node_rest = jnp.pad(node_rest, ((0, 16), (0, 0)))
    first_rows, pair_rows, node_rows = 10 * quarter + 32, 2 * quarter + 2 * chans, node_rest.shape[0]

    def tiles(values):
        return jnp.broadcast_to(values[..., None], values.shape + (chans,))

    gains = [tiles(values) for values in (gain_pair, gain_tri, gain_trans)]
    sent = pack(
        place,
        pair,
        0,
        chunk,
        first=[
            lengths,
            present,
            node,
            node_cot,
            w_tri_in.transpose(0, 1, 3, 2).reshape(-1, chans),
            w_out_gate.transpose(0, 2, 1).reshape(-1, chans),
            w_bias.T,
            w_tri_out.transpose(0, 2, 1).reshape(-1, chans),
            w_trans_in,
            w_trans_out,
        ],
    )
    sent, pair, pair_cot = tied((sent, pair, pair_cot))
    pieces0 = send_home(sent)
    sent = pack(place, pair, chunk, chunk)
    sent_cots = pack(place, pair_cot, 0, chunk)
    sent_later = pack(place, pair_cot, chunk, chunk, blocks(split(node_rest)))
    sent_cots, sent_later, gains = tied((sent_cots, sent_later, gains))
    sent, sent_cots, sent_later, gains, pieces0 = tied((sent, sent_cots, sent_later, gains, pieces0))
    pieces1 = send_home(sent)
    node_own = jnp.stack([piece[chunk + 1 : chunk + 3] for piece in pieces0])
    weights = jnp.stack([piece[chunk + 3 :] for piece in pieces0]).reshape(groups, -1, chans)
    weights = with_far(weights, swap_core(weights), core)
    wall, rest = weights[:, :first_rows], weights[:, first_rows : first_rows + pair_rows]
    gain, gains_mid = gains[0], gains[1:]
    live = pieces0[0][chunk, 0].astype(jnp.float32)
    mask_rows = own_rows(live, 0)[:, None] * live[None, :]
    tri0, norm0, pair0, bias0 = project(place, pieces0, wall, mask_rows, gain, heads, chunk, 0)
    tri0, pieces1, rest, sent_cots = tied((tri0, pieces1, rest, sent_cots))
    cots0 = send_home(sent_cots)
    far0 = swap_core(tri0)
    tri1, norm1, pair1, bias1 = project(place, pieces1, wall, mask_rows, gain, heads, chunk, chunk)
    bias = jnp.concatenate([bias0, bias1], axis=1)
    c0, c1, c2, c3 = cots0
    tri1, far0, c1 = tied((tri1, far0, c1))
    cots0 = [c0, c1, c2, c3]
    far1 = swap_core(tri1)
    far1, bias = tied((far1, bias))
    bias_far = swap_core(bias)
    tri = tri_forward(place, (tri0, tri1), (far0, far1))
    sent, bias_far, cots0, tri = tied((sent_later, bias_far, cots0, tri))
    cots1 = send_home(sent)
    norms, pairs = (norm0, norm1), (pair0, pair1)

    core_round, row_round = (core, DP, core_pairs), (x, ROWS, row_pairs)
    y_round = (y, DP, [(d, d ^ 2) for d in range(mesh_shape[0])])

    def halve(value, side, axis, pairs, at=1):
        low, high = jnp.split(value, 2, at)
        far = lax.ppermute(jnp.where(side == 0, high, low).astype(jnp.bfloat16), axis, pairs)
        return jnp.where(side == 0, low, high).astype(jnp.float32), far

    def added(kept, far):
        return (kept + far).astype(jnp.bfloat16)

    def both(value, far, side):
        return jnp.concatenate([jnp.where(side == 0, value, far), jnp.where(side == 0, far, value)])

    def run_middle(n, cots, prev):
        return middle(
            place, tri, n * chunk, pairs[n], norms[n], cots, *gains_mid, wall, rest, prev
        )

    *out0, mid0, gate0, gtri0, gw_rest = run_middle(0, cots0, None)
    out0, gtri0, cots1 = tied((out0, gtri0, cots1))
    out0 = send_home(out0)
    node_rest = jnp.stack([cot[chunk:] for cot in cots1]).reshape(groups, -1, chans)
    node_rest = jnp.concatenate(
        [node_rest, swap_rows(node_rest), node_own.reshape(groups, -1, chans)], axis=1
    )
    *out1, mid1, gate1, gtri1, gw_rest = run_middle(1, cots1, gw_rest)
    gtri0, gtri1, out0, node_rest = tied((gtri0, gtri1, out0, node_rest))
    node_rest_far = swap_core(node_rest)
    gtri0, gtri1, node_rest_far = tied((gtri0, gtri1, node_rest_far))
    gtris = (gtri0, gtri1)
    gtris_far = [swap_core(gtri) for gtri in gtris]
    mids, gates = (mid0, mid1), (gate0, gate1)

    node_sent, scores, gw_node = node_track(
        place,
        bias,
        bias_far,
        live[None, :],
        gain_node[None, :],
        gain_node_trans[None, :],
        node_rest,
        node_rest_far,
        node_rows,
    )
    early = [gw_node, gw_rest]
    early_rows = sum(part.shape[1] for part in early)
    early.append(jnp.zeros((groups, -early_rows % 64, chans), jnp.bfloat16))
    early = jnp.concatenate(early, axis=1)
    out1, gtris_far = tied((out1, gtris_far))
    out1 = send_home(out1)
    kept, far = halve(early, *row_round)
    sums = tri_backward(place, (tri0, tri1), (far0, far1), gtris, gtris_far)

    def run_finish(n, prev):
        return finish(
            place, sums, n * chunk, pairs[n], norms[n], mids[n], gates[n], scores, mask_rows, gain, wall, prev, node_sent
        )

    *grad0, gw_first = run_finish(0, None)
    grad0, out1, kept, far = tied((grad0, out1, kept, far))
    kept, far = halve(added(kept, far), *y_round)
    grad0 = send_home(grad0)
    *grad1, gw_first = run_finish(1, gw_first)
    grad1, gw_first, grad0 = tied((grad1, gw_first, grad0))
    grad1 = send_home(grad1)
    early = added(kept, far)
    shard = early.shape[1]
    low = jnp.concatenate([early, gw_first.reshape(groups, -1, chans)], axis=1)
    total = pick(low, z).astype(jnp.float32)
    for m in range(1, groups):
        total = total + to_chan(pick(low, z ^ m), m)
    total = total.astype(jnp.bfloat16)
    total, out0, out1 = tied((total, out0, out1))
    def joined(chunks):
        rows = [jnp.concatenate([c[m][:chunk] for c in chunks]) for m in range(groups)]
        stacked = jnp.stack(rows)
        return jnp.stack([pick(stacked, far_z ^ k) for k in range(groups)])

    pair_out = joined((out0, out1))
    early, late = total[:shard], total[shard:]
    for side, axis, pairs in (y_round, row_round):
        far = lax.ppermute(jnp.concatenate([early, late]), axis, pairs)
        if axis == ROWS:
            grad1, far, pair_out = tied((grad1, far, pair_out))
        late = added(late.astype(jnp.float32), far[early.shape[0] :])
        early = both(early, far[: early.shape[0]], side)
    own = jnp.concatenate([early, late])
    far = swap_core(own)
    tri_in, out_gate, bias_w, tri_out, trans_in, trans_out, qkv, attn, node_in, node_out, *gains = unpack(
        place, own, far, early.shape[0], node_rows, w_bias.shape[1]
    )
    pair_grad, node_result, node_grad = assemble(place, (grad0, grad1), chunk, True)

    return (
        pair_out,
        node_result,
        pair_grad,
        node_grad,
        gains[0].reshape(-1),
        tri_in.transpose(0, 1, 3, 2),
        out_gate.transpose(0, 2, 1),
        gains[2],
        tri_out.transpose(0, 2, 1),
        gains[1].reshape(-1),
        trans_in,
        trans_out,
        bias_w.T,
        gains[3].reshape(-1),
        qkv.transpose(0, 2, 1),
        attn.T,
        gains[4].reshape(-1),
        node_in,
        node_out,
    )


def solution(mesh):
    in_specs = (
        P(DP, ROWS, CHAN, None),
        P(DP, ROWS, CHAN),
        P(DP, ROWS, CHAN, None),
        P(DP, ROWS, CHAN),
        P(DP),
        P(DP, None),
        P(),
        P(None, None, None, CHAN),
        P(None, None, CHAN),
        P(),
        P(None, None, CHAN),
        P(),
        P(None, CHAN),
        P(CHAN, None),
        P(None, CHAN),
        P(),
        P(None, None, CHAN),
        P(None, CHAN),
        P(),
        P(None, CHAN),
        P(CHAN, None),
    )
    out_specs = (
        P(DP, ROWS, CHAN, None),
        P(DP, ROWS, CHAN),
        P(DP, ROWS, CHAN, None),
        P(DP, ROWS, CHAN),
        P(CHAN),
        P(None, None, None, CHAN),
        P(None, None, CHAN),
        P(None, CHAN),
        P(None, None, CHAN),
        P(CHAN),
        P(None, CHAN),
        P(CHAN, None),
        P(None, CHAN),
        P(CHAN),
        P(None, None, CHAN),
        P(None, CHAN),
        P(CHAN),
        P(None, CHAN),
        P(CHAN, None),
    )
    sizes = dict(mesh.shape)
    by_crop = sizes[ROWS] == 2 and sizes[DP] == 4 and sizes[CHAN] == 4
    body = shards_by_crop if by_crop else shards
    return jax.shard_map(body, mesh=mesh, in_specs=in_specs, out_specs=out_specs, check_vma=False)
```

```python
import functools
import math

import jax
import jax.numpy as jnp
from jax import lax
from jax.experimental import pallas as pl
from jax.experimental.pallas import tpu as pltpu
from jax.sharding import PartitionSpec as P

f32, bf16 = jnp.float32, jnp.bfloat16
epsilon = 1e-05
DP, ROWS, CHAN = "dp", "rows", "chan"
masked_score = -1000000000.0


def norm_parts(full):
    mean = jnp.mean(full, axis=2, keepdims=True)
    centered = full - mean
    variance = jnp.mean(centered * centered, axis=2, keepdims=True)
    inverse = lax.rsqrt(variance + epsilon)
    return (centered * inverse, inverse)


def shaped(gain, full):
    return gain.reshape(gain.shape + (1,) * (full.ndim - 3))


def normed(full, gain):
    scaled, inverse = norm_parts(full)
    return scaled * shaped(gain, full)


def stat_terms(full, gain, partial_value, groups):
    scaled, inverse = norm_parts(full)
    weighted = shaped(gain, full) * partial_value
    first_sum = jnp.sum(weighted, axis=2)
    second_sum = jnp.sum(weighted * scaled, axis=2)
    stacked = jnp.stack([first_sum, second_sum], axis=2)
    repeats = (1, 1, groups) + (1,) * (full.ndim - 3)
    return jnp.tile(stacked, repeats)


def norm_finish(full, gain, grad_here, totals, chan_index):
    width = full.shape[2]
    here = grad_here.shape[2]
    scaled, inverse = norm_parts(full)
    scaled_here = lax.dynamic_slice_in_dim(scaled, chan_index * here, here, 2)
    gain_here = lax.dynamic_slice_in_dim(gain, chan_index * here, here, 0)
    first_mean = totals[:, :, 0:1] / width
    second_mean = totals[:, :, 1:2] / width
    grad_input = inverse * (
        shaped(gain_here, full) * grad_here - first_mean - scaled_here * second_mean
    )
    summed_axes = (0, 1) + tuple(range(3, full.ndim))
    grad_gain = jnp.sum(grad_here * scaled_here, axis=summed_axes)
    return (grad_input, grad_gain)


def gelu_exact(value):
    return jax.nn.gelu(value, approximate=False)


def softmax_rows(scores):
    top = jnp.max(scores, axis=-1, keepdims=True)
    exps = jnp.exp(scores - top)
    return exps / jnp.sum(exps, axis=-1, keepdims=True)


def shards(
    pair,
    node,
    pair_cot,
    node_cot,
    lengths,
    present,
    gain_pair,
    w_tri_in,
    w_out_gate,
    gain_tri,
    w_tri_out,
    gain_trans,
    w_trans_in,
    w_trans_out,
    w_bias,
    gain_node,
    w_qkv,
    w_attn_out,
    gain_node_trans,
    w_node_in,
    w_node_out,
):
    batch = pair.shape[0]
    rows_here = pair.shape[1]
    crop_len = pair.shape[3]
    groups = lax.axis_size(CHAN)
    chan_index = lax.axis_index(CHAN)
    row_start = lax.axis_index(ROWS) * rows_here
    heads_here = w_bias.shape[1]
    head_dim = w_qkv.shape[2] // heads_here
    scale = 1.0 / math.sqrt(head_dim)
    positions = jnp.arange(crop_len, dtype=jnp.int32)
    mask_all = present.astype(jnp.float32) * (positions[None, :] < lengths[:, None]).astype(
        jnp.float32
    )
    mask_rows = lax.dynamic_slice_in_dim(mask_all, row_start, rows_here, 1)
    pair_mask = mask_rows[:, :, None, None] * mask_all[:, None, None, :]
    key_live = mask_all[:, None, None, :] > 0.5

    def gating(gate, value):
        return jax.nn.sigmoid(gate) * value * pair_mask

    pair_whole, node_whole = (
        lax.all_gather(pair, CHAN, axis=2, tiled=True),
        lax.all_gather(node, CHAN, axis=2, tiled=True),
    )
    full_in = pair_whole.astype(jnp.float32)
    node_full = node_whole.astype(jnp.float32)
    stream_in = pair.astype(jnp.float32)
    node_in = node.astype(jnp.float32)
    normed_in = normed(full_in, gain_pair).astype(jnp.bfloat16)
    projected = jnp.einsum(
        "bicj,dgch->dgbihj", normed_in, w_tri_in, preferred_element_type=jnp.float32
    )
    gate_pre = jnp.einsum(
        "bicj,dcx->dbixj", normed_in, w_out_gate, preferred_element_type=jnp.float32
    )
    bias = jnp.einsum("bicj,ch->bhij", normed_in, w_bias, preferred_element_type=jnp.float32)
    left_out = gating(projected[0, 0], projected[0, 1]).astype(jnp.bfloat16)
    right_out = gating(projected[0, 2], projected[0, 3]).astype(jnp.bfloat16)
    left_in = gating(projected[1, 0], projected[1, 1]).astype(jnp.bfloat16)
    right_in = gating(projected[1, 2], projected[1, 3]).astype(jnp.bfloat16)
    normed_node = normed(node_full, gain_node).astype(jnp.bfloat16)
    qkv = jnp.einsum(
        "bin,gna->gbia", normed_node, w_qkv, preferred_element_type=jnp.float32
    ).astype(jnp.bfloat16)
    whole_right_out, whole_right_in, whole_keys, whole_values = (
        lax.all_gather(right_out, ROWS, axis=1, tiled=True),
        lax.all_gather(right_in, ROWS, axis=1, tiled=True),
        lax.all_gather(qkv[1], ROWS, axis=1, tiled=True),
        lax.all_gather(qkv[2], ROWS, axis=1, tiled=True),
    )
    left_cols = lax.all_to_all(left_in, ROWS, split_axis=3, concat_axis=1, tiled=True)
    queries = qkv[0].reshape(batch, rows_here, heads_here, head_dim)
    keys = whole_keys.reshape(batch, crop_len, heads_here, head_dim)
    values = whole_values.reshape(batch, crop_len, heads_here, head_dim)
    raw = (
        jnp.einsum("bihd,bjhd->bhij", queries, keys, preferred_element_type=jnp.float32) * scale
        + bias
    )
    probs = softmax_rows(jnp.where(key_live, raw, masked_score))
    probs_low = probs.astype(jnp.bfloat16)
    attn = jnp.einsum(
        "bhij,bjhd->bihd", probs_low, values, preferred_element_type=jnp.float32
    ).astype(jnp.bfloat16)
    attn = attn.reshape(batch, rows_here, heads_here * head_dim)
    tri_out = jnp.einsum(
        "bihk,bjhk->bihj", left_out, whole_right_out, preferred_element_type=jnp.float32
    )
    tri_in = jnp.einsum(
        "bkhi,bkhj->bihj", left_cols, whole_right_in, preferred_element_type=jnp.float32
    )
    tri_full_out, tri_full_in, attn_whole = (
        lax.all_gather(tri_out.astype(jnp.bfloat16), CHAN, axis=2, tiled=True).astype(
            tri_out.dtype
        ),
        lax.all_gather(tri_in.astype(jnp.bfloat16), CHAN, axis=2, tiled=True).astype(
            tri_in.dtype
        ),
        lax.all_gather(
            attn.astype(jnp.float32).astype(jnp.bfloat16), CHAN, axis=2, tiled=True
        ).astype(jnp.float32),
    )
    normed_out = normed(tri_full_out, gain_tri[0]).astype(jnp.bfloat16)
    normed_inc = normed(tri_full_in, gain_tri[1]).astype(jnp.bfloat16)
    branch_out = jnp.einsum(
        "bihj,hc->bicj", normed_out, w_tri_out[0], preferred_element_type=jnp.float32
    )
    branch_inc = jnp.einsum(
        "bihj,hc->bicj", normed_inc, w_tri_out[1], preferred_element_type=jnp.float32
    )
    gate_sig = jax.nn.sigmoid(gate_pre)
    stream_mid = stream_in + gate_sig[0] * branch_out + gate_sig[1] * branch_inc
    attn_low = attn_whole.astype(jnp.bfloat16)
    node_mid = node_in + jnp.einsum(
        "bia,an->bin", attn_low, w_attn_out, preferred_element_type=jnp.float32
    )
    full_mid, node_full_mid = (
        lax.all_gather(stream_mid.astype(jnp.bfloat16), CHAN, axis=2, tiled=True).astype(
            stream_mid.dtype
        ),
        lax.all_gather(node_mid.astype(jnp.bfloat16), CHAN, axis=2, tiled=True).astype(
            node_mid.dtype
        ),
    )
    normed_mid = normed(full_mid, gain_trans).astype(jnp.bfloat16)
    pre_hidden = jnp.einsum(
        "bicj,cf->bifj", normed_mid, w_trans_in, preferred_element_type=jnp.float32
    )
    hidden, gelu_pull = jax.vjp(gelu_exact, pre_hidden)
    hidden_low = hidden.astype(jnp.bfloat16)
    out_terms = jnp.einsum(
        "bifj,fc->bicj", hidden_low, w_trans_out, preferred_element_type=jnp.float32
    )
    normed_node_mid = normed(node_full_mid, gain_node_trans).astype(jnp.bfloat16)
    node_pre = jnp.einsum(
        "bin,nf->bif", normed_node_mid, w_node_in, preferred_element_type=jnp.float32
    )
    node_hidden, node_gelu_pull = jax.vjp(gelu_exact, node_pre)
    node_hidden_low = node_hidden.astype(jnp.bfloat16)
    node_terms = jnp.einsum(
        "bif,fn->bin", node_hidden_low, w_node_out, preferred_element_type=jnp.float32
    )
    pair_sum, node_sum = (
        lax.psum_scatter(
            out_terms.astype(jnp.bfloat16), CHAN, scatter_dimension=2, tiled=True
        ).astype(jnp.float32),
        lax.psum_scatter(
            node_terms.astype(jnp.bfloat16), CHAN, scatter_dimension=2, tiled=True
        ).astype(jnp.float32),
    )
    stream_out = stream_mid + pair_sum
    node_out = node_mid + node_sum
    cot_full, node_cot_full = (
        lax.all_gather(pair_cot, CHAN, axis=2, tiled=True),
        lax.all_gather(node_cot, CHAN, axis=2, tiled=True),
    )
    grad_trans_out = jnp.einsum(
        "bifj,bicj->fc", hidden_low, cot_full, preferred_element_type=jnp.float32
    )
    grad_hidden = jnp.einsum(
        "bicj,fc->bifj", cot_full, w_trans_out, preferred_element_type=jnp.float32
    )
    grad_pre = gelu_pull(grad_hidden)[0].astype(jnp.bfloat16)
    grad_trans_in = jnp.einsum(
        "bicj,bifj->cf", normed_mid, grad_pre, preferred_element_type=jnp.float32
    )
    grad_normed_mid = jnp.einsum(
        "bifj,cf->bicj", grad_pre, w_trans_in, preferred_element_type=jnp.float32
    )
    mid_terms = stat_terms(full_mid, gain_trans, grad_normed_mid, groups)
    grad_node_out_w = jnp.einsum(
        "bif,bin->fn", node_hidden_low, node_cot_full, preferred_element_type=jnp.float32
    )
    grad_node_hidden = jnp.einsum(
        "bin,fn->bif", node_cot_full, w_node_out, preferred_element_type=jnp.float32
    )
    grad_node_pre = node_gelu_pull(grad_node_hidden)[0].astype(jnp.bfloat16)
    grad_node_in_w = jnp.einsum(
        "bin,bif->nf", normed_node_mid, grad_node_pre, preferred_element_type=jnp.float32
    )
    grad_normed_node_mid = jnp.einsum(
        "bif,nf->bin", grad_node_pre, w_node_in, preferred_element_type=jnp.float32
    )
    node_mid_terms = stat_terms(node_full_mid, gain_node_trans, grad_normed_node_mid, groups)
    mid_here, mid_totals, node_mid_here, node_mid_totals = (
        lax.psum_scatter(
            grad_normed_mid.astype(jnp.bfloat16), CHAN, scatter_dimension=2, tiled=True
        ).astype(jnp.float32),
        lax.psum_scatter(
            mid_terms.astype(jnp.bfloat16), CHAN, scatter_dimension=2, tiled=True
        ).astype(jnp.float32),
        lax.psum_scatter(
            grad_normed_node_mid.astype(jnp.bfloat16), CHAN, scatter_dimension=2, tiled=True
        ).astype(jnp.float32),
        lax.psum_scatter(
            node_mid_terms.astype(jnp.bfloat16), CHAN, scatter_dimension=2, tiled=True
        ).astype(jnp.float32),
    )
    mid_extra, grad_gain_trans = norm_finish(full_mid, gain_trans, mid_here, mid_totals, chan_index)
    node_mid_extra, grad_gain_node_trans = norm_finish(
        node_full_mid, gain_node_trans, node_mid_here, node_mid_totals, chan_index
    )
    grad_mid = pair_cot.astype(jnp.float32) + mid_extra
    grad_node_mid = node_cot.astype(jnp.float32) + node_mid_extra
    branches = jnp.stack([branch_out, branch_inc])
    grad_branch = (gate_sig * grad_mid[None]).astype(jnp.bfloat16)
    grad_gate = (grad_mid[None] * branches * gate_sig * (1.0 - gate_sig)).astype(jnp.bfloat16)
    tri_normed_both = jnp.stack([normed_out, normed_inc])
    grad_w_tri_out = jnp.einsum(
        "dbihj,dbicj->dhc", tri_normed_both, grad_branch, preferred_element_type=jnp.float32
    )
    grad_out_gate = jnp.einsum(
        "bicj,dbixj->dcx", normed_in, grad_gate, preferred_element_type=jnp.float32
    )
    grad_tri_normed = jnp.einsum(
        "dbicj,dhc->dbihj", grad_branch, w_tri_out, preferred_element_type=jnp.float32
    )
    out_stats = stat_terms(tri_full_out, gain_tri[0], grad_tri_normed[0], groups)
    inc_stats = stat_terms(tri_full_in, gain_tri[1], grad_tri_normed[1], groups)
    grad_attn_branch = grad_node_mid.astype(jnp.bfloat16)
    grad_w_attn_out = jnp.einsum(
        "bia,bin->an", attn_low, grad_attn_branch, preferred_element_type=jnp.float32
    )
    attn_terms = jnp.einsum(
        "bin,an->bia", grad_attn_branch, w_attn_out, preferred_element_type=jnp.float32
    )
    out_here, out_totals, inc_here, inc_totals, attn_here = (
        lax.psum_scatter(
            grad_tri_normed[0].astype(jnp.bfloat16), CHAN, scatter_dimension=2, tiled=True
        ).astype(jnp.float32),
        lax.psum_scatter(
            out_stats.astype(jnp.bfloat16), CHAN, scatter_dimension=2, tiled=True
        ).astype(jnp.float32),
        lax.psum_scatter(
            grad_tri_normed[1].astype(jnp.bfloat16), CHAN, scatter_dimension=2, tiled=True
        ).astype(jnp.float32),
        lax.psum_scatter(
            inc_stats.astype(jnp.bfloat16), CHAN, scatter_dimension=2, tiled=True
        ).astype(jnp.float32),
        lax.psum_scatter(
            attn_terms.astype(jnp.bfloat16), CHAN, scatter_dimension=2, tiled=True
        ).astype(jnp.float32),
    )
    grad_tri_a, gain_grad_out = norm_finish(
        tri_full_out, gain_tri[0], out_here, out_totals, chan_index
    )
    grad_tri_b, gain_grad_inc = norm_finish(
        tri_full_in, gain_tri[1], inc_here, inc_totals, chan_index
    )
    grad_gain_tri = jnp.stack([gain_grad_out, gain_grad_inc])
    grad_out_low = grad_tri_a.astype(jnp.bfloat16)
    grad_inc_low = grad_tri_b.astype(jnp.bfloat16)
    grad_attn = attn_here.astype(jnp.bfloat16).reshape(batch, rows_here, heads_here, head_dim)
    grad_probs = jnp.einsum(
        "bihd,bjhd->bhij", grad_attn, values, preferred_element_type=jnp.float32
    )
    delta = jnp.sum(probs * grad_probs, axis=3, keepdims=True)
    grad_scores = (probs * (grad_probs - delta)).astype(jnp.bfloat16)
    grad_queries = (
        jnp.einsum("bhij,bjhd->bihd", grad_scores, keys, preferred_element_type=jnp.float32) * scale
    )
    key_terms = (
        jnp.einsum("bhij,bihd->bjhd", grad_scores, queries, preferred_element_type=jnp.float32)
        * scale
    )
    value_terms = jnp.einsum(
        "bhij,bihd->bjhd", probs_low, grad_attn, preferred_element_type=jnp.float32
    )
    grad_w_bias = jnp.einsum(
        "bicj,bhij->ch", normed_in, grad_scores, preferred_element_type=jnp.float32
    )
    bias_back = jnp.einsum("bhij,ch->bicj", grad_scores, w_bias, preferred_element_type=jnp.float32)
    grad_left_out = jnp.einsum(
        "bihj,bjhk->bihk", grad_out_low, whole_right_out, preferred_element_type=jnp.float32
    )
    right_terms = jnp.einsum(
        "bihj,bihk->bjhk", grad_out_low, left_out, preferred_element_type=jnp.float32
    )
    grad_right_out, key_grads, value_grads = (
        lax.psum_scatter(
            right_terms.astype(jnp.bfloat16), ROWS, scatter_dimension=1, tiled=True
        ).astype(jnp.float32),
        lax.psum_scatter(
            key_terms.astype(jnp.bfloat16), ROWS, scatter_dimension=1, tiled=True
        ).astype(jnp.float32),
        lax.psum_scatter(
            value_terms.astype(jnp.bfloat16), ROWS, scatter_dimension=1, tiled=True
        ).astype(jnp.float32),
    )
    whole_grad_in = lax.all_gather(grad_inc_low, ROWS, axis=1, tiled=True)
    grad_left_in = jnp.einsum(
        "bihj,bkhj->bkhi", whole_grad_in, right_in, preferred_element_type=jnp.float32
    )
    grad_right_in = jnp.einsum(
        "bkhi,bihj->bkhj", left_in, whole_grad_in, preferred_element_type=jnp.float32
    )

    def gate_back(first, second, grad):
        kept_value, pull = jax.vjp(gating, first, second)
        return pull(grad)

    left_gate_out, left_value_out = gate_back(projected[0, 0], projected[0, 1], grad_left_out)
    right_gate_out, right_value_out = gate_back(projected[0, 2], projected[0, 3], grad_right_out)
    left_gate_in, left_value_in = gate_back(projected[1, 0], projected[1, 1], grad_left_in)
    right_gate_in, right_value_in = gate_back(projected[1, 2], projected[1, 3], grad_right_in)
    grad_proj = jnp.stack(
        [
            jnp.stack([left_gate_out, left_value_out, right_gate_out, right_value_out]),
            jnp.stack([left_gate_in, left_value_in, right_gate_in, right_value_in]),
        ]
    ).astype(jnp.bfloat16)
    grad_tri_in_w = jnp.einsum(
        "bicj,dgbihj->dgch", normed_in, grad_proj, preferred_element_type=jnp.float32
    )
    grad_normed_in = jnp.einsum(
        "dgbihj,dgch->bicj", grad_proj, w_tri_in, preferred_element_type=jnp.float32
    )
    grad_normed_in = grad_normed_in + jnp.einsum(
        "dbixj,dcx->bicj", grad_gate, w_out_gate, preferred_element_type=jnp.float32
    )
    grad_normed_in = grad_normed_in + bias_back
    grad_qkv = jnp.stack(
        [
            grad_queries.reshape(batch, rows_here, heads_here * head_dim),
            key_grads.reshape(batch, rows_here, heads_here * head_dim),
            value_grads.reshape(batch, rows_here, heads_here * head_dim),
        ]
    ).astype(jnp.bfloat16)
    grad_w_qkv = jnp.einsum(
        "bin,gbia->gna", normed_node, grad_qkv, preferred_element_type=jnp.float32
    )
    grad_normed_node = jnp.einsum(
        "gbia,gna->bin", grad_qkv, w_qkv, preferred_element_type=jnp.float32
    )
    in_terms = stat_terms(full_in, gain_pair, grad_normed_in, groups)
    node_in_terms = stat_terms(node_full, gain_node, grad_normed_node, groups)
    in_here, in_totals, node_in_here, node_in_totals = (
        lax.psum_scatter(
            grad_normed_in.astype(jnp.bfloat16), CHAN, scatter_dimension=2, tiled=True
        ).astype(jnp.float32),
        lax.psum_scatter(
            in_terms.astype(jnp.bfloat16), CHAN, scatter_dimension=2, tiled=True
        ).astype(jnp.float32),
        lax.psum_scatter(
            grad_normed_node.astype(jnp.bfloat16), CHAN, scatter_dimension=2, tiled=True
        ).astype(jnp.float32),
        lax.psum_scatter(
            node_in_terms.astype(jnp.bfloat16), CHAN, scatter_dimension=2, tiled=True
        ).astype(jnp.float32),
    )
    in_extra, grad_gain_pair = norm_finish(full_in, gain_pair, in_here, in_totals, chan_index)
    node_in_extra, grad_gain_node = norm_finish(
        node_full, gain_node, node_in_here, node_in_totals, chan_index
    )
    grad_stream = grad_mid + in_extra
    node_grad = grad_node_mid + node_in_extra
    summed = lax.psum(
        (
            grad_gain_pair,
            grad_tri_in_w,
            grad_out_gate,
            grad_gain_tri,
            grad_w_tri_out,
            grad_gain_trans,
            grad_trans_in,
            grad_trans_out,
            grad_w_bias,
            grad_gain_node,
            grad_w_qkv,
            grad_w_attn_out,
            grad_gain_node_trans,
            grad_node_in_w,
            grad_node_out_w,
        ),
        (DP, ROWS),
    )
    return (
        stream_out.astype(jnp.bfloat16),
        node_out.astype(jnp.bfloat16),
        grad_stream.astype(jnp.bfloat16),
        node_grad.astype(jnp.bfloat16),
        summed[0],
        summed[1],
        summed[2],
        summed[3],
        summed[4],
        summed[5],
        summed[6],
        summed[7],
        summed[8],
        summed[9],
        summed[10],
        summed[11],
        summed[12],
        summed[13],
        summed[14],
    )


ORDER = (3, 2, 0, 1)
IN_LEFT, IN_RIGHT, OUT_RIGHT, OUT_LEFT = range(4)

group = 16


def dot(a, b, ca=1, cb=0):
    return lax.dot_general(a, b, (((ca,), (cb,)), ((), ())), preferred_element_type=f32)


def sigmoid(v):
    return 0.5 * jnp.tanh(0.5 * v) + 0.5


def sub_norm(full):
    mean = jnp.mean(full, axis=0, keepdims=True)
    centered = full - mean
    inverse = lax.rsqrt(jnp.mean(centered * centered, axis=0, keepdims=True) + epsilon)
    return centered * inverse, inverse


def sub_norm_back(gain, scaled, inverse, grad):
    weighted = gain * grad
    first = jnp.mean(weighted, axis=0, keepdims=True)
    second = jnp.mean(weighted * scaled, axis=0, keepdims=True)
    return inverse * (weighted - first - scaled * second)


def gelu_both(value):
    cdf = 0.5 * (1.0 + lax.erf(value * (0.5**0.5)))
    density = jnp.exp(-0.5 * value * value) * (1.0 / math.sqrt(2.0 * math.pi))
    return value * cdf, cdf + value * density


def lane_sums(value):
    value = sum(value[:, at : at + 128] for at in range(0, value.shape[1], 128))
    ones = jnp.ones((8, value.shape[1]), f32)
    sums = lax.dot_general(
        ones,
        value,
        (((1,), (1,)), ((), ())),
        precision=lax.Precision.HIGHEST,
        preferred_element_type=f32,
    )
    return sums[:1]


def place_spec():
    return pl.BlockSpec(memory_space=pltpu.SMEM)


def whole_spec(a):
    zeros = (0,) * len(a.shape)
    return pl.BlockSpec(a.shape, lambda s: zeros)


def in_hbm(shape, dtype):
    return pltpu.HBM(shape, dtype)


def held(arrays):
    return [pltpu.with_memory_space_constraint(a, pltpu.HBM) for a in arrays]


def params(mib):
    return pltpu.CompilerParams(vmem_limit_bytes=mib * 2**20)


quick = pl.CostEstimate(flops=1, bytes_accessed=1, transcendentals=0)


def pack_kernel(first_row, rows, live_rows, place_ref, *refs):
    z, part = place_ref[0], 2 * place_ref[2] + place_ref[1]
    sems = refs[-1]
    outs = refs[-7:-3] if live_rows else refs[-5:-1]
    more = outs[0].shape[0] - rows
    copies = []
    for m in range(4):
        rows_of = refs[0].at[lax.bitwise_xor(z, m), pl.ds(first_row, rows)]
        copies.append(pltpu.make_async_copy(rows_of, outs[m].at[pl.ds(0, rows)], sems.at[m]))
    if more and not live_rows:
        for m in range(4):
            rows_of = refs[1].at[pl.ds(part * more, more)]
            copies.append(pltpu.make_async_copy(rows_of, outs[m].at[pl.ds(rows, more)], sems.at[4 + m]))
    for copy in copies:
        copy.start()
    if live_rows:
        lengths, present, node, node_cot, tri_in, gate, bias, tri_out, trans_in, trans_out = refs[1:11]
        extra, weights = refs[-3:-1]
        quarter, width = extra.shape[2:]
        position = lax.broadcasted_iota(jnp.int32, (1, width), 1)
        for crop in range(4):
            for n, ref in enumerate((node, node_cot)):
                value = ref[crop].astype(f32)
                extra[crop, 1 + n] = jnp.concatenate([value[:quarter], value[quarter:]], axis=1).astype(bf16)
            there = jnp.where(position < lengths[crop], present[crop : crop + 1], 0).astype(f32)
            extra[crop, 0] = jnp.broadcast_to(there, (quarter, width)).astype(bf16)
        parts = [tri_in[...], gate[...]]
        low = bias[...].astype(f32)
        parts.append(jnp.concatenate([low, jnp.zeros((32 - low.shape[0], width), f32)], axis=0).astype(bf16))
        parts += [tri_out[...], trans_in[...].astype(f32).T.astype(bf16), trans_out[...]]
        count = sum(part.shape[0] for part in parts)
        parts.append(jnp.zeros((quarter * weights.shape[0] - count, width), bf16))
        weights[...] = jnp.concatenate(parts, axis=0).reshape(weights.shape)
        for m in range(4):
            outs[m][rows : rows + 3] = extra[lax.bitwise_xor(z, m)]
            outs[m][rows + 3 :] = weights[pl.ds(place_ref[2] * (more - 3), more - 3)]
    for copy in copies:
        copy.wait()


def pack(place, source, first_row, rows, weights=None, first=None):
    _, _, quarter, width = source.shape
    vmem = pl.BlockSpec(memory_space=pltpu.VMEM)
    operands, specs, scratch, more = [place, *held([source])], [place_spec(), any_spec()], [], 0
    if first is not None:
        count = sum(a.shape[0] for a in first[4:]) + 32 - first[6].shape[0]
        count = -(-count // (2 * quarter)) * 2
        operands += first[:1] + held(first[1:])
        specs += [place_spec()] + [vmem] * (len(first) - 1)
        scratch = [pltpu.VMEM((4, 3, quarter, width), bf16), pltpu.VMEM((count, quarter, width), bf16)]
        more = 3 + count // 2
    elif weights is not None:
        operands += held([weights])
        specs.append(any_spec())
        more = weights.shape[0] // 4
    return pl.pallas_call(
        functools.partial(pack_kernel, first_row, rows, first is not None),
        in_specs=specs,
        out_specs=[vmem] * 4,
        out_shape=[in_hbm((rows + more, quarter, width), bf16)] * 4,
        scratch_shapes=scratch + [pltpu.SemaphoreType.DMA((8,))],
        compiler_params=params(24),
        cost_estimate=quick,
        name="pack",
    )(*operands)


def project_kernel(
    place_ref, p0, p1, p2, p3, wall_ref, mask_ref, gain_ref, tri_ref, norm_ref, pair_ref, bias_ref, pc, w_s, wb_s, bs, *kept_s
):
    pieces = (p0, p1, p2, p3)
    rows, quarter, width = p0.shape
    chans = 4 * quarter
    z = place_ref[0]
    gain = jnp.concatenate([gain_ref[...]] * group, axis=1)
    heads = bias_ref.shape[0]
    tri_rows = 8 * quarter

    @pl.when(pl.program_id(0) == 0)
    def _():
        for g in range(4):
            w_s[g * tri_rows : (g + 1) * tri_rows] = wall_ref[lax.bitwise_xor(z, g), :tri_rows]
            wb_s[g * 16 : (g + 1) * 16] = wall_ref[lax.bitwise_xor(z, g), 10 * quarter : 10 * quarter + 16]

    for m in range(4):
        pc[lax.bitwise_xor(z, m)] = pieces[m][...]

    @pl.loop(0, rows // group)
    def _(step):
        first = step * group

        def wide(get):
            return jnp.concatenate([get(first + n) for n in range(group)], axis=1)

        rows_in = [jnp.concatenate([pc[q, first + n] for q in range(4)], axis=0) for n in range(group)]
        for n in range(group):
            pair_ref[first + n] = rows_in[n]
        scaled, _ = sub_norm(jnp.concatenate(rows_in, axis=1).astype(f32))
        low = (scaled * gain).astype(bf16)
        for n in range(group):
            norm_ref[first + n] = low[:, n * width : (n + 1) * width]
        mask = wide(lambda r: mask_ref[pl.ds(r, 1), :])
        bias = dot(wb_s[...], low)
        for n in range(group):
            for g in range(4):
                at = (first + n) * heads + g * (heads // 4)
                bs[pl.ds(at, heads // 4), :] = bias[g * 16 : g * 16 + heads // 4, n * width : (n + 1) * width]
        for g in range(4):
            proj = dot(w_s[g * tri_rows : (g + 1) * tri_rows], low)
            for k in range(4):
                gate = proj[(2 * k) * quarter : (2 * k + 1) * quarter]
                value = proj[(2 * k + 1) * quarter : (2 * k + 2) * quarter]
                kept = sigmoid(gate) * value * mask
                for n in range(group):
                    at = (first + n) * (chans + 1) + g * quarter
                    kept_s[ORDER[k]][pl.ds(at, quarter), :] = kept[:, n * width : (n + 1) * width]

    @pl.loop(0, chans, unroll=32)
    def _(h):
        for k in range(4):
            tri_ref[k, h] = kept_s[k][pl.ds(h, rows, stride=chans + 1), :].astype(bf16)

    for h in range(heads):
        bias_ref[h] = bs[pl.ds(h, rows, stride=heads), :]


def any_spec():
    return pl.BlockSpec(memory_space=pl.ANY)


def project(place, pieces, wall, mask_rows, gain, heads, rows, first_row, step_rows=16):
    _, quarter, width = pieces[0].shape
    chans = 4 * quarter
    start = first_row // step_rows
    row_spec = pl.BlockSpec((step_rows, chans, width), lambda i: (i, 0, 0))
    pair = in_hbm((rows, chans, width), bf16)
    return pl.pallas_call(
        project_kernel,
        grid=(rows // step_rows,),
        in_specs=[place_spec()]
        + [pl.BlockSpec((step_rows, quarter, width), lambda i: (i, 0, 0))] * 4
        + [whole_spec(wall), pl.BlockSpec((step_rows, width), lambda i: (i + start, 0)), whole_spec(gain)],
        out_specs=[
            pl.BlockSpec((4, chans, step_rows, width), lambda i: (0, 0, i, 0)),
            row_spec,
            row_spec,
            pl.BlockSpec((heads, step_rows, width), lambda i: (0, i, 0)),
        ],
        out_shape=[
            in_hbm((4, chans, rows, width), bf16),
            pair,
            pair,
            jax.ShapeDtypeStruct((heads, rows, width), f32),
        ],
        scratch_shapes=[
            pltpu.VMEM((4, step_rows, quarter, width), bf16),
            pltpu.VMEM((8 * chans, chans), bf16),
            pltpu.VMEM((64, chans), bf16),
            pltpu.VMEM((step_rows * heads, width), f32),
        ]
        + [pltpu.VMEM((step_rows * (chans + 8), width), f32)] * 4,
        compiler_params=params(40),
        cost_estimate=quick,
        name="project",
    )(place, *pieces, wall, mask_rows, gain)


def in_core_order(core, mine, far):
    first = core == 0
    blocks = [jnp.where(first, a, b) for a, b in zip(mine, far)]
    return jnp.concatenate(blocks + [jnp.where(first, b, a) for a, b in zip(mine, far)], axis=0)


def tri_forward_kernel(count, place_ref, *refs):
    core = place_ref[1]
    mine, far, out_ref = refs[:count], refs[count : 2 * count], refs[-1]
    rows = out_ref.shape[2]

    @pl.loop(0, out_ref.shape[1], unroll=32)
    def _(h):
        left = jnp.concatenate([t[OUT_LEFT, h] for t in mine], axis=0)
        right = in_core_order(core, [t[OUT_RIGHT, h] for t in mine], [t[OUT_RIGHT, h] for t in far])
        out_ref[0, h] = dot(left, right, 1, 1).astype(bf16)
        left = jnp.concatenate([t[IN_LEFT, h] for t in mine + far], axis=0)
        right = jnp.concatenate([t[IN_RIGHT, h] for t in mine + far], axis=0)
        both = dot(left, right, 0, 0)
        out_ref[1, h] = jnp.where(core == 0, both[:rows], both[rows:]).astype(bf16)


def tri_forward(place, mine, far, step_h=32):
    _, chans, rows, width = mine[0].shape
    rows = rows * len(mine)
    spec = pl.BlockSpec((4, step_h) + mine[0].shape[2:], lambda s: (0, s, 0, 0))
    far_spec = pl.BlockSpec((3, step_h) + mine[0].shape[2:], lambda s: (0, s, 0, 0))
    return pl.pallas_call(
        functools.partial(tri_forward_kernel, len(mine)),
        grid=(chans // step_h,),
        in_specs=[place_spec()] + [spec] * len(mine) + [far_spec] * len(mine),
        out_specs=pl.BlockSpec((2, step_h, rows, width), lambda s: (0, s, 0, 0)),
        out_shape=in_hbm((2, chans, rows, width), bf16),
        compiler_params=params(40),
        cost_estimate=quick,
        name="tri_forward",
    )(place, *held(mine), *far)


def middle_kernel(
    fresh, place_ref, tri_ref, pair_ref, norm_ref, c0, c1, c2, c3, gain_tri_ref, gain_trans_ref, wall_ref, rest_ref, prev_ref,
    p0, p1, p2, p3, mid_ref, gate_ref, gtri_ref, gw_out_ref,
    gw_ref, tri_s0, tri_s1, wg_s, wto_s, wti_s, wout_s, wout_t, wti_t, wto_t, gg_trans_s, gg_tri_s,
    cot_s, pc, po, tn0, tn1, nm, hid, gp, gb0, gb1, gs0, gs1,
):
    z = place_ref[0]
    step = pl.program_id(0)
    rows, chans, width = pair_ref.shape
    quarter = chans // 4
    cots, outs = (c0, c1, c2, c3), (p0, p1, p2, p3)
    tris, tns, gbs, gss = (tri_s0, tri_s1), (tn0, tn1), (gb0, gb1), (gs0, gs1)
    gains_at = 2 * quarter + 2 * chans

    @pl.when(step == 0)
    def _():
        for g in range(4):
            for d in range(2):
                wg_s[d * chans + g * quarter : d * chans + (g + 1) * quarter] = wall_ref[
                    lax.bitwise_xor(z, g), (8 + d) * quarter : (9 + d) * quarter
                ]
                wto_s[d, g * quarter : (g + 1) * quarter] = rest_ref[lax.bitwise_xor(z, g), d * quarter : (d + 1) * quarter]
            wti_s[g * chans : (g + 1) * chans] = rest_ref[lax.bitwise_xor(z, g), 2 * quarter : 2 * quarter + chans]
            wout_s[g * chans : (g + 1) * chans] = rest_ref[lax.bitwise_xor(z, g), 2 * quarter + chans : gains_at]
        for f in range(4):
            block = slice(f * chans, (f + 1) * chans)
            wout_t[:, block] = wout_s[block].astype(f32).T.astype(bf16)
            wti_t[:, block] = wti_s[block].astype(f32).T.astype(bf16)
        for d in range(2):
            wto_t[d] = wto_s[d].astype(f32).T.astype(bf16)
        gw_ref[...] = jnp.zeros_like(gw_ref) if fresh else prev_ref[...]
        gg_trans_s[...] = jnp.zeros_like(gg_trans_s)
        gg_tri_s[...] = jnp.zeros_like(gg_tri_s)

    @pl.loop(0, chans, unroll=32)
    def _(h):
        for d in range(2):
            tris[d][pl.ds(h * (rows + 1), rows), :] = tri_ref[d, h].astype(f32)

    gain_trans = jnp.concatenate([gain_trans_ref[...]] * group, axis=1)
    gain_tri = [jnp.concatenate([gain_tri_ref[d]] * group, axis=1) for d in range(2)]

    for m in range(4):
        pc[lax.bitwise_xor(z, m)] = cots[m][...]

    @pl.loop(0, rows // group)
    def _(s2):
        first = s2 * group
        lanes = pl.ds(pl.multiple_of(first * width, group * width), group * width)

        def wide(get):
            return jnp.concatenate([get(first + n) for n in range(group)], axis=1)

        def cut(value, n):
            return value[:, n * width : (n + 1) * width]

        inner = wide(lambda r: norm_ref[r])
        gate = sigmoid(dot(wg_s[...], inner))
        total = wide(lambda r: pair_ref[r]).astype(f32)
        kept = []
        for d in range(2):
            tri = wide(lambda r: tris[d][pl.ds(r, chans, stride=rows + 1), :])
            scaled, inverse = sub_norm(tri)
            low = (scaled * gain_tri[d]).astype(bf16)
            tns[d][:, lanes] = low
            branch = dot(wto_s[d], low)
            total = total + gate[d * chans : (d + 1) * chans] * branch
            kept.append((scaled, inverse, branch))
        scaled, inverse = sub_norm(total)
        low = (scaled * gain_trans).astype(bf16)
        nm[:, lanes] = low
        cot = wide(lambda r: jnp.concatenate([pc[q, r] for q in range(4)], axis=0))
        cot_s[:, lanes] = cot
        acts, backs = [], []
        for f in range(4):
            block = slice(f * chans, (f + 1) * chans)
            act, slope = gelu_both(dot(wti_s[block], low))
            acts.append(act.astype(bf16))
            backs.append((dot(wout_s[block], cot) * slope).astype(bf16))
            hid[block, lanes] = acts[-1]
            gp[block, lanes] = backs[-1]
        out = (total + dot(wout_t[...], jnp.concatenate(acts, axis=0))).astype(bf16)
        for n in range(group):
            for q in range(4):
                po[q, first + n] = cut(out[q * quarter : (q + 1) * quarter], n)
        back = dot(wti_t[...], jnp.concatenate(backs, axis=0))
        gg_trans_s[...] += back * scaled
        grad = cot.astype(f32) + sub_norm_back(gain_trans, scaled, inverse, back)
        for n in range(group):
            mid_ref[first + n] = cut(grad, n).astype(bf16)
        for d in range(2):
            scaled, inverse, branch = kept[d]
            sig = gate[d * chans : (d + 1) * chans]
            grad_branch = sig * grad
            grad_gate = (grad_branch * branch * (1.0 - sig)).astype(bf16)
            grad_branch = grad_branch.astype(bf16)
            for n in range(group):
                gate_ref[first + n, d * chans : (d + 1) * chans] = cut(grad_gate, n)
            gbs[d][:, lanes] = grad_branch
            back = dot(wto_t[d], grad_branch)
            gg_tri_s[d] += back * scaled
            out = sub_norm_back(gain_tri[d], scaled, inverse, back)
            for n in range(group):
                gss[d][pl.ds(first + n, chans, stride=rows + 1), :] = cut(out, n)

    for m in range(4):
        outs[m][...] = po[lax.bitwise_xor(z, m)]
    gw_out = dot(hid[...], cot_s[...], 1, 1)
    gw_in = dot(gp[...], nm[...], 1, 1)
    for g in range(4):
        at = 2 * quarter
        gw_ref[g, at : at + chans] += gw_in[g * chans : (g + 1) * chans]
        gw_ref[g, at + chans : at + 2 * chans] += gw_out[g * chans : (g + 1) * chans]
    for d in range(2):
        gw_tri = dot(gbs[d][...], tns[d][...], 1, 1)
        for g in range(4):
            gw_ref[g, d * quarter : (d + 1) * quarter] += gw_tri[g * quarter : (g + 1) * quarter]

        @pl.loop(0, chans, unroll=32)
        def _(h):
            gtri_ref[d, h] = gss[d][pl.ds(h * (rows + 1), rows), :].astype(bf16)

    @pl.when(step == pl.num_programs(0) - 1)
    def _():
        for n, total in enumerate((gg_trans_s[...], gg_tri_s[0], gg_tri_s[1])):
            row = lane_sums(total)
            for g in range(4):
                gw_ref[g, gains_at + n : gains_at + n + 1] += row
        gw_out_ref[...] = gw_ref[...].astype(gw_out_ref.dtype)


def middle(place, tri, first_row, pair, norm, cots, gain_tri, gain_trans, wall, rest, prev, step_rows=16):
    rows, chans, width = pair.shape
    hidden, quarter = 4 * chans, chans // 4
    fresh = prev is None
    sums = in_hbm((4, 2 * quarter + 2 * chans + 16, chans), f32 if fresh else bf16)
    start = first_row // step_rows
    row_spec = pl.BlockSpec((step_rows, chans, width), lambda s: (s, 0, 0))
    piece_spec = pl.BlockSpec((step_rows, quarter, width), lambda s: (s, 0, 0))
    piece = in_hbm((rows, quarter, width), bf16)
    gate = in_hbm((rows, 2 * chans, width), bf16)
    lanes = step_rows * width
    operands = [place, *held([tri, pair, norm]), *cots, gain_tri, gain_trans, wall, rest]
    operands.append(gain_tri if fresh else prev)
    return pl.pallas_call(
        functools.partial(middle_kernel, fresh),
        grid=(rows // step_rows,),
        in_specs=[place_spec(), pl.BlockSpec((2, chans, step_rows, width), lambda s: (0, 0, s + start, 0)), row_spec, row_spec]
        + [piece_spec] * 4
        + [whole_spec(a) for a in operands[8:]],
        out_specs=[piece_spec] * 4
        + [
            row_spec,
            pl.BlockSpec((step_rows, 2 * chans, width), lambda s: (s, 0, 0)),
            pl.BlockSpec((2, chans, step_rows, width), lambda s: (0, 0, s, 0)),
            whole_spec(sums),
        ],
        out_shape=[piece] * 4
        + [
            in_hbm((rows, chans, width), bf16),
            gate,
            jax.ShapeDtypeStruct((2, chans, rows, width), bf16),
            sums,
        ],
        scratch_shapes=[pltpu.VMEM(sums.shape, f32)]
        + [pltpu.VMEM((chans * (step_rows + 1), width), f32)] * 2
        + [pltpu.VMEM((2 * chans, chans), bf16), pltpu.VMEM((2, chans, chans), bf16)]
        + [pltpu.VMEM((hidden, chans), bf16)] * 2
        + [pltpu.VMEM((chans, hidden), bf16)] * 2
        + [
            pltpu.VMEM((2, chans, chans), bf16),
            pltpu.VMEM((chans, group * width), f32),
            pltpu.VMEM((2, chans, group * width), f32),
            pltpu.VMEM((chans, lanes), bf16),
            pltpu.VMEM((4, step_rows, quarter, width), bf16),
            pltpu.VMEM((4, step_rows, quarter, width), bf16),
        ]
        + [pltpu.VMEM((chans, lanes), bf16)] * 3
        + [pltpu.VMEM((hidden, lanes), bf16)] * 2
        + [pltpu.VMEM((chans, lanes), bf16)] * 2
        + [pltpu.VMEM((chans * (step_rows + 1), width), f32)] * 2,
        compiler_params=params(56),
        cost_estimate=quick,
        name="middle",
    )(*operands)


def tri_backward_kernel(count, place_ref, *refs):
    core = place_ref[1]
    mine, far, gmine, gfar = (refs[n * count : (n + 1) * count] for n in range(4))
    out_ref = refs[-1]
    rows = out_ref.shape[2]

    def joined(a, k, h):
        return jnp.concatenate([t[k, h] for t in a], axis=0)

    @pl.loop(0, out_ref.shape[1], unroll=32)
    def _(h):
        right = in_core_order(core, [t[OUT_RIGHT, h] for t in mine], [t[0, h] for t in far])
        out_ref[0, h] = dot(joined(gmine, 0, h), right).astype(bf16)
        left = jnp.concatenate([t[OUT_LEFT, h] for t in mine] + [t[1, h] for t in far], axis=0)
        both = dot(joined(gmine + gfar, 0, h), left, 0, 0)
        out_ref[1, h] = jnp.where(core == 0, both[:rows], both[rows:]).astype(bf16)
        grad = in_core_order(core, [t[1, h] for t in gmine], [t[1, h] for t in gfar])
        out_ref[2, h] = dot(joined(mine, IN_RIGHT, h), grad, 1, 1).astype(bf16)
        out_ref[3, h] = dot(joined(mine, IN_LEFT, h), grad).astype(bf16)


def tri_backward(place, mine, far, gmine, gfar, step_h=32):
    _, chans, rows, width = mine[0].shape
    total = rows * len(mine)
    spec = pl.BlockSpec((4, step_h, rows, width), lambda s: (0, s, 0, 0))
    far_spec = pl.BlockSpec((2, step_h, rows, width), lambda s: (1, s, 0, 0))
    gspec = pl.BlockSpec((2, step_h, rows, width), lambda s: (0, s, 0, 0))
    operands = [place, *held(mine), *held(far), *held(gmine), *gfar]
    return pl.pallas_call(
        functools.partial(tri_backward_kernel, len(mine)),
        grid=(chans // step_h,),
        in_specs=[place_spec()] + [spec] * len(mine) + [far_spec] * len(mine) + [gspec] * (2 * len(mine)),
        out_specs=pl.BlockSpec((4, step_h, total, width), lambda s: (0, s, 0, 0)),
        out_shape=in_hbm((4, chans, total, width), bf16),
        compiler_params=params(40),
        cost_estimate=quick,
        name="tri_backward",
    )(*operands)


def finish_kernel(
    i_steps, fresh, place_ref, sum_ref, pair_ref, norm_ref, mid_ref, gate_ref, score_ref, mask_ref, gain_ref, wall_ref, prev_ref, extra_ref,
    p0, p1, p2, p3, gw_out_ref,
    gw_ref, s0, s1, s2_, s3, wall_t, w_s, gall, nb, po, sc_s, gg_s,
):
    z = place_ref[0]
    step = pl.program_id(0)
    rows, chans, width = pair_ref.shape
    quarter = chans // 4
    sums, outs = (s0, s1, s2_, s3), (p0, p1, p2, p3)
    block_rows = wall_ref.shape[1]
    packed = 4 * block_rows
    heads = score_ref.shape[1]
    here = heads // 4

    @pl.when(step == 0)
    def _():
        for g in range(4):
            gall[g * block_rows : (g + 1) * block_rows, :chans] = wall_ref[lax.bitwise_xor(z, g)]
            w_s[g * 8 * quarter : (g + 1) * 8 * quarter] = wall_ref[lax.bitwise_xor(z, g), : 8 * quarter]
        for f in range(0, packed, 128):
            end = min(f + 128, packed)
            wall_t[:, f:end] = gall[f:end, :chans].astype(f32).T.astype(bf16)
        gw_ref[...] = jnp.zeros_like(gw_ref) if fresh else prev_ref[...]
        gg_s[...] = jnp.zeros_like(gg_s)
        sc_s[...] = jnp.zeros_like(sc_s)

    @pl.when(step < i_steps)
    def _():
        @pl.loop(0, chans, unroll=32)
        def _(h):
            for k in range(4):
                sums[k][pl.ds(h * (rows + 1), rows), :] = sum_ref[k, h].astype(f32)

        gain = jnp.concatenate([gain_ref[...]] * group, axis=1)

        @pl.loop(0, rows // group)
        def _(s2):
            first = s2 * group
            lanes = pl.ds(pl.multiple_of(first * width, group * width), group * width)

            def wide(get):
                return jnp.concatenate([get(first + n) for n in range(group)], axis=1)

            def cut(value, n):
                return value[:, n * width : (n + 1) * width]

            inner = wide(lambda r: norm_ref[r])
            nb[:, lanes] = inner
            mask = wide(lambda r: mask_ref[pl.ds(r, 1), :])
            parts = []
            for g in range(4):
                proj = dot(w_s[g * 8 * quarter : (g + 1) * 8 * quarter], inner)
                for k in range(4):
                    gate = proj[(2 * k) * quarter : (2 * k + 1) * quarter]
                    value = proj[(2 * k + 1) * quarter : (2 * k + 2) * quarter]
                    grad = wide(lambda r: sums[k][pl.ds(g * quarter * (rows + 1) + r, quarter, stride=rows + 1), :])
                    sig = sigmoid(gate)
                    back = grad * mask * sig
                    parts.append((back * value * (1.0 - sig)).astype(bf16))
                    parts.append(back.astype(bf16))
                for d in range(2):
                    at = d * chans + g * quarter
                    parts.append(wide(lambda r: gate_ref[r, at : at + quarter]))
                for n in range(group):
                    sc_s[g * 16 : g * 16 + here, n * width : (n + 1) * width] = score_ref[
                        first + n, g * here : (g + 1) * here
                    ]
                parts.append(sc_s[g * 16 : (g + 1) * 16].astype(bf16))
                parts.append(jnp.zeros((block_rows - 10 * quarter - 16, group * width), bf16))
            every = jnp.concatenate(parts, axis=0)
            gall[:, lanes] = every
            back = dot(wall_t[...], every)
            scaled, inverse = sub_norm(wide(lambda r: pair_ref[r]).astype(f32))
            gg_s[...] += back * scaled
            out = wide(lambda r: mid_ref[r]).astype(f32) + sub_norm_back(gain, scaled, inverse, back)
            out = out.astype(bf16)
            for n in range(group):
                for q in range(4):
                    po[q, first + n] = cut(out[q * quarter : (q + 1) * quarter], n)

        for m in range(4):
            outs[m][...] = po[lax.bitwise_xor(z, m)]
        gw_ref[...] += dot(gall[...], nb[...], 1, 1)

    @pl.when(step == i_steps - 1)
    def _():
        row = lane_sums(gg_s[...])
        for g in range(4):
            at = (g + 1) * block_rows - 1
            gw_ref[at : at + 1] += row
        gw_out_ref[...] = gw_ref[...].astype(gw_out_ref.dtype)

    @pl.when(step == i_steps)
    def _():
        for m in range(4):
            outs[m][: extra_ref.shape[1]] = extra_ref[m]


def finish(place, sums, first_row, pair, norm, mid, gate, scores, mask_rows, gain, wall, prev, extra, step_rows=16):
    rows, chans, width = pair.shape
    quarter = chans // 4
    heads = scores.shape[1]
    packed = 4 * wall.shape[1]
    i_steps = rows // step_rows
    fresh = prev is None
    start = first_row // step_rows
    last = first_row + rows == mask_rows.shape[0]
    total = in_hbm((packed, chans), bf16 if last else f32)

    def at(s):
        return jnp.minimum(s, i_steps - 1)

    if fresh:
        prev = gain
    row_spec = pl.BlockSpec((step_rows, chans, width), lambda s: (at(s), 0, 0))
    piece_spec = pl.BlockSpec((step_rows, quarter, width), lambda s: (s, 0, 0))
    piece = in_hbm((rows + (extra.shape[1] if last else 0), quarter, width), bf16)
    lanes = step_rows * width
    return pl.pallas_call(
        functools.partial(finish_kernel, i_steps, fresh),
        grid=(i_steps + (1 if last else 0),),
        in_specs=[place_spec(), pl.BlockSpec((4, chans, step_rows, width), lambda s: (0, 0, at(s) + start, 0))]
        + [row_spec] * 3
        + [
            pl.BlockSpec((step_rows, 2 * chans, width), lambda s: (at(s), 0, 0)),
            pl.BlockSpec((step_rows, heads, width), lambda s: (at(s) + start, 0, 0)),
            pl.BlockSpec((step_rows, width), lambda s: (at(s) + start, 0)),
        ]
        + [whole_spec(a) for a in (gain, wall, prev, extra)],
        out_specs=[piece_spec] * 4 + [whole_spec(total)],
        out_shape=[piece] * 4 + [total],
        scratch_shapes=[pltpu.VMEM((packed, chans), f32)]
        + [pltpu.VMEM((chans * (step_rows + 1), width), f32)] * 4
        + [
            pltpu.VMEM((chans, packed), bf16),
            pltpu.VMEM((8 * chans, chans), bf16),
            pltpu.VMEM((packed, lanes), bf16),
            pltpu.VMEM((chans, lanes), bf16),
            pltpu.VMEM((4, step_rows, quarter, width), bf16),
            pltpu.VMEM((64, group * width), f32),
            pltpu.VMEM((chans, group * width), f32),
        ],
        compiler_params=params(56),
        cost_estimate=quick,
        name="finish",
    )(place, *held([sums, pair, norm, mid, gate]), scores, mask_rows, gain, wall, prev, extra)


def assemble_kernel(rows, count, nodes, place_ref, *refs):
    pieces, (out_ref, *node_refs) = refs[: 4 * count], refs[4 * count : 4 * count + (3 if nodes else 1)]
    sems, z = refs[-1], place_ref[0]
    copies = []
    for m in range(4):
        crop = lax.bitwise_xor(z, m)
        for n in range(count):
            source, target = pieces[4 * n + m], out_ref.at[crop, pl.ds(n * rows, rows)]
            copies.append(pltpu.make_async_copy(source.at[pl.ds(0, rows)], target, sems.at[m, n]))
        if nodes:
            source = pieces[4 * (count - 1) + m].at[pl.ds(rows, 2)]
            copies.append(pltpu.make_async_copy(source, refs[-2].at[crop], sems.at[m, count]))
    for copy in copies:
        copy.start()
    for copy in copies:
        copy.wait()
    for n, ref in enumerate(node_refs):
        for crop in range(4):
            value = refs[-2][crop, n]
            half, width = value.shape[0], value.shape[1] // 2
            ref[crop, :half] = value[:, :width]
            ref[crop, half:] = value[:, width:]


def assemble(place, chunks, rows, nodes):
    _, quarter, width = chunks[0][0].shape
    count = len(chunks)
    vmem = pl.BlockSpec(memory_space=pltpu.VMEM)
    shapes = [jax.ShapeDtypeStruct((4, rows * count, quarter, width), bf16)]
    scratch = [pltpu.SemaphoreType.DMA((4, count + 1))]
    if nodes:
        shapes += [jax.ShapeDtypeStruct((4, 2 * quarter, width // 2), bf16)] * 2
        scratch = [pltpu.VMEM((4, 2, quarter, width), bf16)] + scratch
    return pl.pallas_call(
        functools.partial(assemble_kernel, rows, count, nodes),
        in_specs=[place_spec()] + [any_spec()] * (4 * count),
        out_specs=[any_spec()] + [vmem] * (len(shapes) - 1),
        out_shape=shapes,
        scratch_shapes=scratch,
        compiler_params=params(16),
        cost_estimate=quick,
        name="assemble",
    )(place, *[piece for chunk in chunks for piece in chunk])


def unpack_kernel(early, node_rows, place_ref, own, far, tri_in, gate, bias, tri_out, trans_in, trans_out, qkv, attn, node_in, node_out, gain_pair, gain_trans, gain_tri, gain_node, gain_node_trans):
    first = place_ref[1] == 0
    own, far = own[...].astype(f32), far[...].astype(f32)
    a, b = jnp.where(first, own[:node_rows], far[:node_rows]), jnp.where(first, far[:node_rows], own[:node_rows])
    last = own[early:] + far[early:]
    quarter = tri_out.shape[1]
    chans = trans_in.shape[0]
    wide = jnp.concatenate([a, b], axis=1)
    rest = own[node_rows:early] + far[node_rows:early]
    for d in range(2):
        for n in range(4):
            at = (4 * d + n) * quarter
            tri_in[d, n] = last[at : at + quarter]
        gate[d] = last[(8 + d) * quarter : (9 + d) * quarter]
        tri_out[d] = rest[d * quarter : (d + 1) * quarter]
    bias[...] = last[10 * quarter : 10 * quarter + bias.shape[0]]
    at = 2 * quarter
    trans_in[...] = rest[at : at + chans].T
    trans_out[...] = rest[at + chans : at + 2 * chans]
    at = at + 2 * chans
    z = lax.bitwise_xor(place_ref[0], 3)

    def own_block(rows, size):
        blocks = [rows[:, g * size : (g + 1) * size] for g in range(4)]
        low, high = jnp.where(z == 0, blocks[0], blocks[1]), jnp.where(z == 2, blocks[2], blocks[3])
        return jnp.where(z < 2, low, high)

    gain_pair[...] = own_block(last[last.shape[0] - 8 :], quarter)[7:]
    gains = own_block(rest[at : at + 8], quarter)
    gain_trans[...], gain_tri[...] = gains[:1], gains[1:3]
    size = qkv.shape[1]
    for n in range(3):
        qkv[n] = wide[n * size : (n + 1) * size]
    at = 3 * size
    attn[...] = wide[at : at + size]
    at = at + size
    size = node_in.shape[0]
    node_in[...] = wide[at : at + size].T
    node_out[...] = wide[at + size : at + 2 * size]
    at = at + 2 * size
    gains = own_block(wide[at : at + 8], 2 * quarter)
    gain_node[...], gain_node_trans[...] = gains[:1], gains[1:2]


def unpack(place, own, far, early, node_rows, heads):
    chans = own.shape[1]
    quarter, nodes = chans // 4, 2 * chans
    shapes = [
        (2, 4, quarter, chans), (2, quarter, chans), (heads, chans), (2, quarter, chans), (chans, chans), (chans, chans),
        (3, nodes // 4, nodes), (nodes // 4, nodes), (nodes, nodes), (nodes, nodes),
        (1, quarter), (1, quarter), (2, quarter), (1, nodes // 4), (1, nodes // 4),
    ]
    vmem = pl.BlockSpec(memory_space=pltpu.VMEM)
    return pl.pallas_call(
        functools.partial(unpack_kernel, early, node_rows),
        in_specs=[place_spec()] + [vmem] * 2,
        out_specs=[vmem] * len(shapes),
        out_shape=[jax.ShapeDtypeStruct(shape, f32) for shape in shapes],
        compiler_params=params(32),
        cost_estimate=quick,
        name="unpack",
    )(place, own, far)


def node_kernel(packed, place_ref, bias_ref, bias_far, live_ref, gain_ref, gain_mid_ref, near_w, far_w, more_ref,
                sent_ref, score_ref, gw_ref, w_all, att, gqkv):
    z, core, x = place_ref[0], place_ref[1], place_ref[2]
    first = core == 0
    groups = gw_ref.shape[0]
    more = more_ref.shape[1]
    gw_ref[:, packed:packed + more] = more_ref[...]
    gw_ref[:, packed + more:] = jnp.zeros((groups, gw_ref.shape[1] - packed - more, 128), bf16)
    half_rows = bias_ref.shape[1]
    length, nodes = 2 * half_rows, gain_ref.shape[1]
    quarter = nodes // groups
    fold = quarter // 2
    count = near_w.shape[1] // 2 - fold
    for m in range(groups):
        for ref, side in ((near_w, core), (far_w, 1 - core)):
            for at, other in ((0, x), (count, 1 - x)):
                here = pl.ds(pl.multiple_of((2 * side + other) * count, count), count)
                w_all[lax.bitwise_xor(z, m), here] = ref[m, at:at + count]
    heads = bias_ref.shape[0]
    head_dim = nodes // heads
    hidden = nodes
    scale = 1.0 / math.sqrt(head_dim)

    def weight(at, size):
        return jnp.concatenate(
            [jnp.concatenate([w_all[g, half * packed + at:half * packed + at + size] for half in range(2)], axis=1) for g in range(groups)], axis=0)

    def ordered(mine, far):
        return jnp.concatenate([jnp.where(first, mine, far), jnp.where(first, far, mine)], axis=0)

    def rows(value):
        return jnp.where(first, value[:half_rows], value[half_rows:])

    def parts(value):
        centered = value - jnp.mean(value, axis=1, keepdims=True)
        inverse = lax.rsqrt(jnp.mean(centered * centered, axis=1, keepdims=True) + epsilon)
        return centered * inverse, inverse

    def back(gain, scaled, inverse, grad):
        weighted = gain * grad
        first_mean = jnp.mean(weighted, axis=1, keepdims=True)
        second_mean = jnp.mean(weighted * scaled, axis=1, keepdims=True)
        return inverse * (weighted - first_mean - scaled * second_mean)

    def own_half(value):
        return jnp.where(first, value[:, :128], value[:, 128:]).astype(bf16)

    def keep(at, value):
        size = value.shape[0] // groups
        for g in range(groups):
            gw_ref[g, at:at + size] = own_half(value[g * size:(g + 1) * size])

    def gain_row(grad, scaled):
        return jnp.sum(grad * scaled, axis=0, keepdims=True)


    def unfolded(ref, n):
        rows_of = slice(2 * count + n * fold, 2 * count + (n + 1) * fold)
        parts = [ref[lax.bitwise_xor(z, g), rows_of].astype(f32) for g in range(groups)]
        half = parts[0].shape[1] // 2
        return jnp.concatenate([jnp.concatenate([v[:, :half], v[:, half:]], axis=0) for v in parts], axis=1)

    def sent(n, value):
        for g in range(groups):
            part = value[:, g * quarter:(g + 1) * quarter]
            half = part.shape[0] // 2
            sent_ref[lax.bitwise_xor(z, g), n] = jnp.concatenate([part[:half], part[half:]], axis=1).astype(bf16)

    node_in = ordered(unfolded(near_w, 0), unfolded(far_w, 0))
    cot = ordered(unfolded(near_w, 1), unfolded(far_w, 1)).astype(bf16)
    scaled_in, inverse_in = parts(node_in)
    low_in = (scaled_in * gain_ref[...]).astype(bf16)
    q, k, v = (dot(low_in, weight(g * quarter, quarter), 1, 1).astype(bf16) for g in range(3))
    lane = lax.broadcasted_iota(jnp.int32, (1, nodes), 1)
    key_live = live_ref[...] > 0.5

    def of_head(value, h):
        here = (lane >= h * head_dim) & (lane < (h + 1) * head_dim)
        return jnp.where(here, value, jnp.zeros_like(value))

    def probs_of(h):
        raw = dot(of_head(q, h), k, 1, 1) * scale + ordered(bias_ref[h], bias_far[h])
        scores = jnp.where(key_live, raw, -1e9)
        exps = jnp.exp(scores - jnp.max(scores, axis=1, keepdims=True))
        return exps / jnp.sum(exps, axis=1, keepdims=True)

    total = jnp.zeros((length, nodes), f32)
    for h in range(heads):
        probs = probs_of(h)
        att[h] = probs
        total = total + dot(probs.astype(bf16), of_head(v, h))
    attn = total.astype(bf16)
    at_a, at_i, at_o = 3 * quarter, 4 * quarter, 4 * quarter + hidden
    mid = node_in + dot(attn, weight(at_a, quarter), 1, 1)
    scaled_mid, inverse_mid = parts(mid)
    low_mid = (scaled_mid * gain_mid_ref[...]).astype(bf16)
    out = mid
    grad = jnp.zeros((length, nodes), f32)
    for g in range(groups):
        w_in = jnp.concatenate([w_all[g, half * packed + at_i:half * packed + at_i + hidden] for half in range(2)], axis=1)
        w_out = jnp.concatenate([w_all[g, half * packed + at_o:half * packed + at_o + hidden] for half in range(2)], axis=1)
        act, slope = gelu_both(dot(low_mid, w_in, 1, 1))
        act = act.astype(bf16)
        out = out + dot(act, w_out)
        grad_pre = (dot(cot, w_out, 1, 1) * slope).astype(bf16)
        grad = grad + dot(grad_pre, w_in)
        gi, go = dot(grad_pre, low_mid, 0, 0), dot(act, cot, 0, 0)
        gw_ref[g, at_i:at_i + hidden] = own_half(gi)
        gw_ref[g, at_o:at_o + hidden] = own_half(go)
    sent(0, rows(out))
    mid_row = gain_row(grad, scaled_mid)
    grad_mid = cot.astype(f32) + back(gain_mid_ref[...], scaled_mid, inverse_mid, grad)
    grad_low = grad_mid.astype(bf16)
    keep(at_a, dot(grad_low, attn, 0, 0))
    grad_attn = dot(grad_low, weight(at_a, quarter)).astype(bf16)
    for g in range(3):
        gqkv[g] = jnp.zeros((length, nodes), f32)
    for h in range(heads):
        probs = att[h]
        grad_probs = dot(of_head(grad_attn, h), v, 1, 1)
        delta = jnp.sum(probs * grad_probs, axis=1, keepdims=True)
        scores = probs * (grad_probs - delta)
        score_ref[:, h, :] = rows(scores)
        scores = scores.astype(bf16)
        gqkv[0] += dot(scores, of_head(k, h))
        gqkv[1] += dot(scores, of_head(q, h), 0, 0)
        gqkv[2] += dot(probs.astype(bf16), of_head(grad_attn, h), 0, 0)
    grad = jnp.zeros((length, nodes), f32)
    for g, factor in enumerate((scale, scale, 1.0)):
        low = (gqkv[g] * factor).astype(bf16)
        keep(g * quarter, dot(low, low_in, 0, 0))
        grad = grad + dot(low, weight(g * quarter, quarter))
    tail = jnp.concatenate([gain_row(grad, scaled_in), mid_row, jnp.zeros((14, nodes), f32)], axis=0)
    for g in range(groups):
        gw_ref[g, packed - 16:packed] = own_half(tail)
    sent(1, rows(grad_mid + back(gain_ref[...], scaled_in, inverse_in, grad)))

def node_track(place, bias, bias_far, live, gain, gain_mid, near_w, far_w, rows, more):
    half_rows, length = bias.shape[1], live.shape[1]
    nodes = gain.shape[1]
    heads = bias.shape[0]
    arrays = (bias, bias_far, live, gain, gain_mid, near_w, far_w, more)
    shapes = [
        jax.ShapeDtypeStruct((near_w.shape[0], 2, half_rows // 2, 128), bf16),
        jax.ShapeDtypeStruct((half_rows, heads, length), f32),
        jax.ShapeDtypeStruct((near_w.shape[0], -(-(rows + more.shape[1]) // 64) * 64, 128), bf16),
    ]
    vmem = pl.BlockSpec(memory_space=pltpu.VMEM)
    return pl.pallas_call(
        functools.partial(node_kernel, rows),
        in_specs=[pl.BlockSpec(memory_space=pltpu.SMEM)] + [vmem] * len(arrays),
        out_specs=[vmem] * len(shapes),
        out_shape=shapes,
        scratch_shapes=[pltpu.VMEM((near_w.shape[0], 2 * near_w.shape[1], 128), bf16), pltpu.VMEM((heads, length, length), f32), pltpu.VMEM((3, length, nodes), f32)],
        compiler_params=params(40),
        cost_estimate=quick,
        name="node_track",
    )(place, *arrays[:-2], *held(arrays[-2:]))


def shards_by_crop(
    pair,
    node,
    pair_cot,
    node_cot,
    lengths,
    present,
    gain_pair,
    w_tri_in,
    w_out_gate,
    gain_tri,
    w_tri_out,
    gain_trans,
    w_trans_in,
    w_trans_out,
    w_bias,
    gain_node,
    w_qkv,
    w_attn_out,
    gain_node_trans,
    w_node_in,
    w_node_out,
):
    groups = lax.axis_size(CHAN)
    rows_here = pair.shape[1]
    chans = groups * pair.shape[2]
    crop_len = pair.shape[3]
    nodes = groups * node.shape[2]
    heads = groups * w_bias.shape[1]
    quarter, node_quarter = chans // groups, nodes // groups
    z = lax.axis_index(CHAN)
    core = lax.axis_index(DP) % 2
    x = lax.axis_index(ROWS)
    y = lax.axis_index(DP) // 2
    far_z = z ^ (groups - 1)
    place = jnp.stack([far_z, core, x, y]).astype(jnp.int32)
    mesh_shape = (lax.axis_size(DP), lax.axis_size(ROWS), groups)

    def device(d, r, c):
        return (d * mesh_shape[1] + r) * groups + c

    def home_perm(m):
        return [
            (device(d, r, c), device(d - d % 2 + r, d % 2, c ^ m))
            for d in range(mesh_shape[0])
            for r in range(mesh_shape[1])
            for c in range(groups)
        ]

    core_pairs = [(d, d ^ 1) for d in range(mesh_shape[0])]
    row_pairs = [(0, 1), (1, 0)]

    def send_home(pieces):
        return [
            lax.ppermute(piece, (DP, ROWS, CHAN), home_perm(n ^ (groups - 1)))
            for n, piece in enumerate(pieces)
        ]

    def to_chan(value, m):
        return lax.ppermute(value, CHAN, [(c, c ^ m) for c in range(groups)])

    def swap_core(value):
        return lax.ppermute(value, DP, core_pairs)

    def pick(value, index):
        return lax.dynamic_index_in_dim(value, index, 0, keepdims=False)

    def own_rows(value, axis):
        return lax.dynamic_slice_in_dim(value, core * rows_here, rows_here, axis)

    def packed(parts):
        return jnp.concatenate([part.reshape(-1, chans) for part in parts])

    def split(value):
        return jnp.concatenate([value[:, :chans], value[:, chans:]])

    chunk = min(32, rows_here)
    tied = lax.optimization_barrier

    def blocks(rows):
        rows = jnp.pad(rows, ((0, -rows.shape[0] % (4 * quarter)), (0, 0)))
        return rows.reshape(-1, quarter, chans)

    def with_far(own, far, side):
        return jnp.concatenate([jnp.where(side == 0, own, far), jnp.where(side == 0, far, own)], axis=1)

    def swap_rows(value):
        return lax.ppermute(value, ROWS, row_pairs)

    node_rest = jnp.concatenate(
        [w_qkv.transpose(0, 2, 1).reshape(-1, nodes), w_attn_out.T, w_node_in.T, w_node_out]
    )
    node_rest = jnp.pad(node_rest, ((0, 16), (0, 0)))
    first_rows, pair_rows, node_rows = 10 * quarter + 32, 2 * quarter + 2 * chans, node_rest.shape[0]

    def tiles(values):
        return jnp.broadcast_to(values[..., None], values.shape + (chans,))

    gains = [tiles(values) for values in (gain_pair, gain_tri, gain_trans)]
    sent = pack(
        place,
        pair,
        0,
        chunk,
        first=[
            lengths,
            present,
            node,
            node_cot,
            w_tri_in.transpose(0, 1, 3, 2).reshape(-1, chans),
            w_out_gate.transpose(0, 2, 1).reshape(-1, chans),
            w_bias.T,
            w_tri_out.transpose(0, 2, 1).reshape(-1, chans),
            w_trans_in,
            w_trans_out,
        ],
    )
    sent, pair, pair_cot = tied((sent, pair, pair_cot))
    pieces0 = send_home(sent)
    sent = pack(place, pair, chunk, chunk)
    sent_cots = pack(place, pair_cot, 0, chunk)
    sent_later = pack(place, pair_cot, chunk, chunk, blocks(split(node_rest)))
    sent_cots, sent_later, gains = tied((sent_cots, sent_later, gains))
    sent, sent_cots, sent_later, gains, pieces0 = tied((sent, sent_cots, sent_later, gains, pieces0))
    pieces1 = send_home(sent)
    node_own = jnp.stack([piece[chunk + 1 : chunk + 3] for piece in pieces0])
    weights = jnp.stack([piece[chunk + 3 :] for piece in pieces0]).reshape(groups, -1, chans)
    weights = with_far(weights, swap_core(weights), core)
    wall, rest = weights[:, :first_rows], weights[:, first_rows : first_rows + pair_rows]
    gain, gains_mid = gains[0], gains[1:]
    live = pieces0[0][chunk, 0].astype(jnp.float32)
    mask_rows = own_rows(live, 0)[:, None] * live[None, :]
    tri0, norm0, pair0, bias0 = project(place, pieces0, wall, mask_rows, gain, heads, chunk, 0)
    tri0, pieces1, rest, sent_cots = tied((tri0, pieces1, rest, sent_cots))
    cots0 = send_home(sent_cots)
    far0 = swap_core(tri0)
    tri1, norm1, pair1, bias1 = project(place, pieces1, wall, mask_rows, gain, heads, chunk, chunk)
    bias = jnp.concatenate([bias0, bias1], axis=1)
    c0, c1, c2, c3 = cots0
    tri1, far0, c1 = tied((tri1, far0, c1))
    cots0 = [c0, c1, c2, c3]
    far1 = swap_core(tri1)
    far1, bias = tied((far1, bias))
    bias_far = swap_core(bias)
    tri = tri_forward(place, (tri0, tri1), (far0, far1))
    sent, bias_far, cots0, tri = tied((sent_later, bias_far, cots0, tri))
    cots1 = send_home(sent)
    norms, pairs = (norm0, norm1), (pair0, pair1)

    core_round, row_round = (core, DP, core_pairs), (x, ROWS, row_pairs)
    y_round = (y, DP, [(d, d ^ 2) for d in range(mesh_shape[0])])

    def halve(value, side, axis, pairs, at=1):
        half = value.shape[at] // 2
        sent, kept = (
            lax.dynamic_slice_in_dim(value, k * half, half, at) for k in (1 - side, side)
        )
        far = lax.ppermute(sent, axis, pairs)
        return kept.astype(jnp.float32), far

    def added(kept, far):
        return (kept + far).astype(jnp.bfloat16)

    def both(value, far, side):
        return jnp.concatenate([jnp.where(side == 0, value, far), jnp.where(side == 0, far, value)])

    def run_middle(n, cots, prev):
        return middle(
            place, tri, n * chunk, pairs[n], norms[n], cots, *gains_mid, wall, rest, prev
        )

    *out0, mid0, gate0, gtri0, gw_rest = run_middle(0, cots0, None)
    out0, gtri0, cots1 = tied((out0, gtri0, cots1))
    out0 = send_home(out0)
    node_rest = jnp.stack([cot[chunk:] for cot in cots1]).reshape(groups, -1, chans)
    node_rest = jnp.concatenate(
        [node_rest, swap_rows(node_rest), node_own.reshape(groups, -1, chans)], axis=1
    )
    *out1, mid1, gate1, gtri1, gw_rest = run_middle(1, cots1, gw_rest)
    gtri0, gtri1, out0, node_rest = tied((gtri0, gtri1, out0, node_rest))
    node_rest_far = swap_core(node_rest)
    gtri0, gtri1, node_rest_far = tied((gtri0, gtri1, node_rest_far))
    gtris = (gtri0, gtri1)
    gtris_far = [swap_core(gtri) for gtri in gtris]
    mids, gates = (mid0, mid1), (gate0, gate1)

    node_sent, scores, early = node_track(
        place,
        bias,
        bias_far,
        live[None, :],
        gain_node[None, :],
        gain_node_trans[None, :],
        node_rest,
        node_rest_far,
        node_rows,
        gw_rest,
    )
    out1, gtris_far = tied((out1, gtris_far))
    out1 = send_home(out1)
    kept, far = halve(early, *row_round)
    sums = tri_backward(place, (tri0, tri1), (far0, far1), gtris, gtris_far)

    def run_finish(n, prev):
        return finish(
            place, sums, n * chunk, pairs[n], norms[n], mids[n], gates[n], scores, mask_rows, gain, wall, prev, node_sent
        )

    *grad0, gw_first = run_finish(0, None)
    grad0, out1, kept, far = tied((grad0, out1, kept, far))
    kept, far = halve(added(kept, far), *y_round)
    grad0 = send_home(grad0)
    *grad1, gw_first = run_finish(1, gw_first)
    grad1, gw_first, grad0 = tied((grad1, gw_first, grad0))
    grad1 = send_home(grad1)
    early = added(kept, far)
    shard = early.shape[1]
    low = jnp.concatenate([early, gw_first.reshape(groups, -1, chans)], axis=1)
    total = pick(low, z).astype(jnp.float32)
    for m in range(1, groups):
        total = total + to_chan(pick(low, z ^ m), m)
    total = total.astype(jnp.bfloat16)
    total, out0, out1 = tied((total, out0, out1))
    def joined(chunks):
        rows = [jnp.concatenate([c[m][:chunk] for c in chunks]) for m in range(groups)]
        stacked = jnp.stack(rows)
        return jnp.stack([pick(stacked, far_z ^ k) for k in range(groups)])

    pair_out = joined((out0, out1))
    early, late = total[:shard], total[shard:]
    for side, axis, pairs in (y_round, row_round):
        far = lax.ppermute(jnp.concatenate([early, late]), axis, pairs)
        if axis == ROWS:
            grad1, far, pair_out = tied((grad1, far, pair_out))
        late = added(late.astype(jnp.float32), far[early.shape[0] :])
        early = both(early, far[: early.shape[0]], side)
    own = jnp.concatenate([early, late])
    far = swap_core(own)
    tri_in, out_gate, bias_w, tri_out, trans_in, trans_out, qkv, attn, node_in, node_out, *gains = unpack(
        place, own, far, early.shape[0], node_rows, w_bias.shape[1]
    )
    pair_grad, node_result, node_grad = assemble(place, (grad0, grad1), chunk, True)

    return (
        pair_out,
        node_result,
        pair_grad,
        node_grad,
        gains[0].reshape(-1),
        tri_in.transpose(0, 1, 3, 2),
        out_gate.transpose(0, 2, 1),
        gains[2],
        tri_out.transpose(0, 2, 1),
        gains[1].reshape(-1),
        trans_in,
        trans_out,
        bias_w.T,
        gains[3].reshape(-1),
        qkv.transpose(0, 2, 1),
        attn.T,
        gains[4].reshape(-1),
        node_in,
        node_out,
    )


def solution(mesh):
    in_specs = (
        P(DP, ROWS, CHAN, None),
        P(DP, ROWS, CHAN),
        P(DP, ROWS, CHAN, None),
        P(DP, ROWS, CHAN),
        P(DP),
        P(DP, None),
        P(),
        P(None, None, None, CHAN),
        P(None, None, CHAN),
        P(),
        P(None, None, CHAN),
        P(),
        P(None, CHAN),
        P(CHAN, None),
        P(None, CHAN),
        P(),
        P(None, None, CHAN),
        P(None, CHAN),
        P(),
        P(None, CHAN),
        P(CHAN, None),
    )
    out_specs = (
        P(DP, ROWS, CHAN, None),
        P(DP, ROWS, CHAN),
        P(DP, ROWS, CHAN, None),
        P(DP, ROWS, CHAN),
        P(CHAN),
        P(None, None, None, CHAN),
        P(None, None, CHAN),
        P(None, CHAN),
        P(None, None, CHAN),
        P(CHAN),
        P(None, CHAN),
        P(CHAN, None),
        P(None, CHAN),
        P(CHAN),
        P(None, None, CHAN),
        P(None, CHAN),
        P(CHAN),
        P(None, CHAN),
        P(CHAN, None),
    )
    sizes = dict(mesh.shape)
    by_crop = sizes[ROWS] == 2 and sizes[DP] == 4 and sizes[CHAN] == 4
    body = shards_by_crop if by_crop else shards
    return jax.shard_map(body, mesh=mesh, in_specs=in_specs, out_specs=out_specs, check_vma=False)
```
